32 devices in a mesh: scen: 2 (over y), blk: 16 (over z, x, core).
Axes of the slice: x: 2, y: 2, z: 4, core: 2. Of those that a mesh axis runs over, the one named last changes fastest.
Arguments:
- returns: bfloat16 [128, 8192], P(('scen', 'blk')), may hold values from -6 to 6
- vol_hist: float32 [128, 8192], P(('scen', 'blk')), may hold values from 0.5 to 5.5, as said below
- vol_now: float32 [8192], replicated, may hold values from 0.5 to 2
- sensitivity: bfloat16 [4096, 128, 128], P('blk'), may hold values from -0.109375 to 0.109375
- block_pairs: int32 [4096, 3], P('blk'), may hold values from 0 to 63, as said below
- book_order: int32 [32], replicated, may hold values from 0 to 31, each once
Outputs:
- profit_loss: float32 [128, 4096], P('scen', 'blk')
- book_rms: float32 [4096], P('blk')
The draws below stay inside these ranges and needn't reach their ends.
Inputs may be any that keep to these rules, and one draw needn't show every extreme that they name: `block_pairs`: each index k of blk holds 256 slots; their factor blocks lie in k * 4 to k * 4 + 3; on each index the live slots come first; some index has all 256 slots live. `vol_hist`: positive volatilities.
All inputs are finite; a program needn't handle non-finite values.
Results may differ from the reference program's by a relative error of at most 0.0029.
Values may be sent and summed in bfloat16 or wider, within the bound.
No kernel may reach another device: no remote copies, remote signals or barrier semaphores. Data moves between devices by JAX's collectives and lax.ppermute only.
A program may use at most 64 MiB of HBM per device.

```python
import math
import jax
import jax.numpy as jnp
from jax import lax

BS = 128
FB_DEV = 4
BLK_DEV = 256
NFB = 64
NBB = 32
F = 8192
SLOTS = 4096
S = 128
N_BLK = 16


def draw_vol_hist(key, part):
    rows = jnp.arange(S, dtype=jnp.float32) / S
    base = jnp.exp(jax.random.uniform(key, (S, F), jnp.float32, jnp.log(0.5), jnp.log(2.0)))
    ramp = 0.7
    return base * jnp.exp(ramp * rows)[:, None]


def draw_block_pairs(key, part):
    devices = NFB // FB_DEV
    key_count = jax.random.fold_in(key, 11)
    key_full = jax.random.fold_in(key, 12)
    key_factor = jax.random.fold_in(key, 13)
    key_book = jax.random.fold_in(key, 14)
    counts = jax.random.randint(key_count, (devices,), BLK_DEV // 4, BLK_DEV // 2 + 1)
    full_device = jax.random.randint(key_full, (), 0, devices)
    counts = jnp.where(jnp.arange(devices) == full_device, BLK_DEV, counts)
    slot_index = jnp.arange(BLK_DEV, dtype=jnp.int32)
    live = (slot_index[None, :] < counts[:, None]).astype(jnp.int32)
    factor = jnp.arange(devices, dtype=jnp.int32)[:, None] * FB_DEV + jax.random.randint(key_factor, (devices, BLK_DEV), 0, FB_DEV)
    book = jax.random.randint(key_book, (devices, BLK_DEV), 0, NBB)
    stacked = jnp.stack([factor.astype(jnp.int32), book.astype(jnp.int32), live], axis=-1)
    return stacked.reshape(devices * BLK_DEV, 3)


def levels(own_key, dims, pieces, low, high):
    def one(axis_at, parts):
        steps = jax.random.uniform(jax.random.fold_in(jax.random.fold_in(own_key, 6), axis_at), (parts,), jnp.float32, low / len(pieces), high / len(pieces))
        return jnp.repeat(jnp.exp(steps), dims[axis_at] // parts).reshape((-1,) + (1,) * (len(dims) - axis_at - 1))

    loudness = one(*pieces[0])
    for cut in pieces[1:]:
        loudness = loudness * one(*cut)
    return loudness


def scatter_about(own_key, extent, deviation, reach, pieces=(), held_as=jnp.bfloat16):
    entries = jax.random.normal(own_key, extent, jnp.float32) * deviation
    if len(pieces) > 0:
        entries = levels(own_key, extent, pieces, -0.22, 0.18) * entries
    return jnp.clip(entries, min=-reach, max=reach).astype(held_as)


def setup_inputs(seed: int = 0) -> dict:
    arg_keys = jax.random.split(jax.random.key(seed), 7)
    returns = scatter_about(arg_keys[0], (S, F), 1.0, 6.0, ((0, 32),))
    vol_hist = draw_vol_hist(jax.random.fold_in(arg_keys[6], 71), 0)
    vol_now = jnp.clip(jnp.exp(jax.random.uniform(arg_keys[2], (F,), jnp.float32, math.log(0.5), math.log(2.0))), 0.5, 2.0)
    sensitivity = scatter_about(arg_keys[3], (SLOTS, BS, BS), (BS * 24) ** -0.5, 0.109375, ((0, 16),))
    block_pairs = draw_block_pairs(jax.random.fold_in(arg_keys[6], 71), 0)
    book_order = jax.random.permutation(arg_keys[5], NBB).astype(jnp.int32)
    return {"returns": returns, "vol_hist": vol_hist, "vol_now": vol_now, "sensitivity": sensitivity, "block_pairs": block_pairs, "book_order": book_order}


def reference(returns, vol_hist, vol_now, sensitivity, block_pairs, book_order):
    rescaled = (returns.astype(jnp.float32) * vol_now[None, :] / vol_hist).astype(jnp.bfloat16)
    shock_blocks = rescaled.reshape(S, NFB, BS)
    order_index = jnp.arange(NBB, dtype=jnp.int32)
    position_of = jnp.zeros((NBB,), jnp.int32).at[book_order].set(order_index)
    sens_groups = sensitivity.reshape(N_BLK, BLK_DEV, BS, BS)
    pair_groups = block_pairs.reshape(N_BLK, BLK_DEV, 3)

    def add_group(total, group):
        sens_group, pair_group = group
        picked = jnp.take(shock_blocks, pair_group[:, 0], axis=1)
        products = jnp.einsum('skc,kcd->ksd', picked.astype(jnp.float32), sens_group.astype(jnp.float32))
        products = products * pair_group[:, 2].astype(jnp.float32)[:, None, None]
        target = position_of[pair_group[:, 1]]
        return (total + jax.ops.segment_sum(products, target, num_segments=NBB), None)
    start_total = jnp.zeros((NBB, S, BS), jnp.float32)
    total, _ = lax.scan(add_group, start_total, (sens_groups, pair_groups))
    profit_loss = total.transpose(1, 0, 2).reshape(S, NBB * BS)
    book_rms = jnp.sqrt(lax.optimization_barrier(jnp.sum(profit_loss * profit_loss, axis=0)) / S + 1e-06)
    return (profit_loss, book_rms)
```

```python
import functools

import jax
import jax.numpy as jnp
from jax import lax
from jax.experimental import pallas as pl
from jax.experimental.pallas import tpu as pltpu
from jax.sharding import PartitionSpec as P


def accumulate(chunk, unroll, factors, pairs, order, shocks, sens, out, acc, position, base):
    step = pl.program_id(0)
    books = order.shape[0]
    slots = pairs.shape[1]

    @pl.when(step == 0)
    def _():
        acc[...] = jnp.zeros_like(acc)

        def place(p, carry):
            position[order[p]] = p
            return carry

        lax.fori_loop(0, books, place, 0)
        base[0] = lax.axis_index("blk") * factors

    first = step * chunk

    def group(g, carry):
        local = g * unroll
        terms = []
        places = []
        for u in range(unroll):
            k = first + local + u
            f = pairs[0, k] - base[0]
            live = pairs[2, k] != 0
            places.append(jnp.where(live, position[pairs[1, k]], books))
            terms.append(jnp.dot(shocks[f], sens[local + u], preferred_element_type=jnp.float32))
        for p, term in zip(places, terms):
            acc[p] += term
        return carry

    @pl.when(pairs[2, first] != 0)
    def _():
        lax.fori_loop(0, chunk // unroll, group, 0)

    @pl.when(step == slots // chunk - 1)
    def _():
        out[...] = acc[:books].astype(out.dtype)


def partials(shocks, sensitivity, block_pairs, book_order):
    slots, block, _ = sensitivity.shape
    factors, rows, _ = shocks.shape
    books = book_order.shape[0]
    chunk, unroll = 32, 4

    def sens_map(i, pairs, order):
        return (jnp.where(pairs[2, i * chunk] != 0, i, 0), 0, 0)

    return pl.pallas_call(
        functools.partial(accumulate, chunk, unroll, factors),
        grid_spec=pltpu.PrefetchScalarGridSpec(
            num_scalar_prefetch=2,
            grid=(slots // chunk,),
            in_specs=[
                pl.BlockSpec((factors, rows, block), lambda i, *_: (0, 0, 0)),
                pl.BlockSpec((chunk, block, block), sens_map),
            ],
            out_specs=pl.BlockSpec((books, rows, block), lambda i, *_: (0, 0, 0)),
            scratch_shapes=[
                pltpu.VMEM((books + 1, rows, block), jnp.float32),
                pltpu.SMEM((books,), jnp.int32),
                pltpu.SMEM((1,), jnp.int32),
            ],
        ),
        out_shape=jax.ShapeDtypeStruct((books, rows, block), jnp.bfloat16),
        compiler_params=pltpu.CompilerParams(vmem_limit_bytes=32 * 1024 * 1024),
        cost_estimate=pl.CostEstimate(
            flops=2 * slots * rows * block * block,
            bytes_accessed=2 * slots * block * block,
            transcendentals=0,
        ),
    )(block_pairs.T, book_order, shocks, sensitivity)


def shards(returns, vol_hist, vol_now, sensitivity, block_pairs, book_order):
    rescaled = (returns.astype(jnp.float32) * vol_now[None, :] / vol_hist).astype(jnp.bfloat16)
    groups = lax.axis_size("blk")
    own_rows, width = rescaled.shape
    block = sensitivity.shape[1]
    own = width // groups
    outgoing = rescaled.reshape(own_rows, groups, own).transpose(1, 0, 2)
    incoming = lax.all_to_all(outgoing, "blk", 0, 0)
    rows = groups * own_rows
    shocks = incoming.reshape(rows, own // block, block).transpose(1, 0, 2)
    partial = partials(shocks, sensitivity, block_pairs, book_order)
    books = book_order.shape[0] // groups
    arrived = lax.all_to_all(partial.reshape(groups, books, rows, block), "blk", 0, 0)
    owned = jnp.sum(arrived.astype(jnp.float32), axis=0)
    profit_loss = owned.transpose(1, 0, 2).reshape(rows, books * block)
    squares = lax.psum(jnp.sum(owned * owned, axis=1).reshape(-1), "scen")
    total_rows = rows * lax.axis_size("scen")
    book_rms = jnp.sqrt(squares / total_rows + 1e-06)
    return (profit_loss, book_rms)


def solution(mesh):
    return jax.shard_map(
        shards,
        mesh=mesh,
        in_specs=(
            P(("scen", "blk"), None),
            P(("scen", "blk"), None),
            P(),
            P("blk", None, None),
            P("blk", None),
            P(),
        ),
        out_specs=(P("scen", "blk"), P("blk")),
        check_vma=False,
    )
```

```python
import functools

import jax
import jax.numpy as jnp
from jax import lax
from jax.experimental import pallas as pl
from jax.experimental.pallas import tpu as pltpu
from jax.sharding import PartitionSpec as P


UNROLL = 4


def accumulate(groups, pairs_hbm, order_hbm, shocks, sens_hbm, kept, sent, sens, pairs, order, position, small, arrived):
    slots = sens.shape[0]
    chunks = arrived.shape[0]
    chunk = slots // chunks
    books = order.shape[0]
    half = books // 2
    per_owner = books // groups
    index = lax.axis_index("blk")
    first_factor = index * shocks.shape[0]

    def fetch(c):
        span = pl.ds(c * chunk, chunk)
        return pltpu.make_async_copy(sens_hbm.at[span], sens.at[span], arrived.at[c])

    get_pairs = pltpu.make_async_copy(pairs_hbm, pairs, small.at[0])
    get_order = pltpu.make_async_copy(order_hbm, order, small.at[1])
    get_pairs.start()
    get_order.start()
    fetch(0).start()
    kept[...] = jnp.zeros_like(kept)
    sent[...] = jnp.zeros_like(sent)
    get_pairs.wait()

    def fetch_next(c, carry):
        @pl.when(pairs[2, c * chunk] != 0)
        def _():
            fetch(c).start()

        return carry

    lax.fori_loop(1, chunks, fetch_next, 0)
    get_order.wait()

    def place(p, carry):
        owner = p // per_owner
        side = (owner + index) % 2
        position[order[p]] = side * half + (owner // 2) * per_owner + p % per_owner
        return carry

    lax.fori_loop(0, books, place, 0)

    def group(k):
        terms = []
        for u in range(UNROLL):
            f = pairs[0, k + u] - first_factor
            terms.append(jnp.dot(shocks[f], sens[k + u], preferred_element_type=jnp.float32))
        for u in range(UNROLL):
            live = pairs[2, k + u] != 0
            p = position[pairs[1, k + u]]

            @pl.when(live & (p < half))
            def _():
                kept[p] += terms[u]

            @pl.when(live & (p >= half))
            def _():
                sent[p - half] += terms[u]

    def work(c, carry):
        @pl.when((c == 0) | (pairs[2, c * chunk] != 0))
        def _():
            fetch(c).wait()

            def step(g, inner):
                group(c * chunk + g * UNROLL)
                return inner

            lax.fori_loop(0, chunk // UNROLL, step, 0)

        return carry

    lax.fori_loop(0, chunks, work, 0)


def partials(groups, shocks, sensitivity, block_pairs, book_order):
    slots, block, _ = sensitivity.shape
    factors, rows, _ = shocks.shape
    books = book_order.shape[0]
    chunks = 16
    hbm = pl.BlockSpec(memory_space=pltpu.HBM)
    vmem = pl.BlockSpec(memory_space=pltpu.VMEM)
    return pl.pallas_call(
        functools.partial(accumulate, groups),
        in_specs=[hbm, hbm, vmem, hbm],
        out_specs=[vmem, vmem],
        out_shape=[jax.ShapeDtypeStruct((books // 2, rows, block), jnp.float32)] * 2,
        scratch_shapes=[
            pltpu.VMEM(sensitivity.shape, sensitivity.dtype),
            pltpu.SMEM((3, slots), jnp.int32),
            pltpu.SMEM((books,), jnp.int32),
            pltpu.SMEM((books,), jnp.int32),
            pltpu.SemaphoreType.DMA((2,)),
            pltpu.SemaphoreType.DMA((chunks,)),
        ],
        compiler_params=pltpu.CompilerParams(vmem_limit_bytes=52 * 1024 * 1024),
        cost_estimate=pl.CostEstimate(
            flops=2 * slots * rows * block * block,
            bytes_accessed=2 * slots * block * block,
            transcendentals=0,
        ),
    )(block_pairs.T, book_order, shocks, sensitivity)


def shards(returns, vol_hist, vol_now, sensitivity, block_pairs, book_order):
    rescaled = (returns.astype(jnp.float32) * vol_now[None, :] / vol_hist).astype(jnp.bfloat16)
    groups = lax.axis_size("blk")
    own_rows, width = rescaled.shape
    block = sensitivity.shape[1]
    own = width // groups
    outgoing = rescaled.reshape(own_rows, groups, own).transpose(1, 0, 2)
    incoming = lax.all_to_all(outgoing, "blk", 0, 0)
    rows = groups * own_rows
    shocks = incoming.reshape(rows, own // block, block).transpose(1, 0, 2)
    kept, sent = partials(groups, shocks, sensitivity, block_pairs, book_order)
    across = lax.ppermute(sent, "blk", [(i, i ^ 1) for i in range(groups)])
    chip_sum = (kept + across).astype(jnp.bfloat16)
    books = book_order.shape[0] // groups
    same_core = [list(range(core, groups, 2)) for core in range(2)]
    arrived = lax.all_to_all(
        chip_sum.reshape(groups // 2, books, rows, block), "blk", 0, 0, axis_index_groups=same_core
    )
    owned = jnp.sum(arrived.astype(jnp.float32), axis=0)
    profit_loss = owned.transpose(1, 0, 2).reshape(rows, books * block)
    spans = lax.axis_size("scen")
    squares = jnp.sum(owned * owned, axis=1).reshape(-1)
    if spans == 2:
        squares = squares + lax.ppermute(squares, "scen", [(0, 1), (1, 0)])
    else:
        squares = lax.psum(squares, "scen")
    book_rms = jnp.sqrt(squares / (rows * spans) + 1e-06)
    return (profit_loss, book_rms)


def solution(mesh):
    return jax.shard_map(
        shards,
        mesh=mesh,
        in_specs=(
            P(("scen", "blk"), None),
            P(("scen", "blk"), None),
            P(),
            P("blk", None, None),
            P("blk", None),
            P(),
        ),
        out_specs=(P("scen", "blk"), P("blk")),
        check_vma=False,
    )
```

```python
import functools

import jax
import jax.numpy as jnp
from jax import lax
from jax.experimental import pallas as pl
from jax.experimental.pallas import tpu as pltpu
from jax.sharding import PartitionSpec as P

UNROLL = 4
MOST_DIRECT = 16


def accumulate(groups, direct, n_incoming, *refs):
    incoming = refs[:n_incoming]
    pairs_hbm, order_hbm, sens_hbm, kept, sent = refs[n_incoming : n_incoming + 5]
    staged, shocks, sens, pairs, order, position, small, arrived = refs[n_incoming + 5 :]
    slots = sens.shape[0]
    factors, _, block = shocks.shape
    chunks = arrived.shape[0]
    chunk = slots // chunks
    books = order.shape[0]
    half = books // 2
    per_owner = books // groups
    index = lax.axis_index("blk")
    first_factor = index * factors
    chip = index // 2 if direct else 0

    def fetch(c):
        span = pl.ds(c * chunk, chunk)
        return pltpu.make_async_copy(sens_hbm.at[span], sens.at[span], arrived.at[c])

    get_pairs = pltpu.make_async_copy(pairs_hbm, pairs, small.at[0])
    get_order = pltpu.make_async_copy(order_hbm, order, small.at[1])
    get_pairs.start()
    get_order.start()
    fetch(0).start()
    kept[...] = jnp.zeros_like(kept)
    sent[...] = jnp.zeros_like(sent)
    if direct:
        for d in range(groups):
            staged[index ^ d] = incoming[d][...].astype(jnp.float32)
        own_rows = staged.shape[1]
        together = max(1, 16 // own_rows)
        for g in range(groups // together):
            rows = jnp.concatenate([staged[g * together + t] for t in range(together)], axis=0)
            rows = rows.astype(shocks.dtype)
            span = pl.ds(g * together * own_rows, together * own_rows)
            for f in range(factors):
                shocks[f, span] = rows[:, f * block : (f + 1) * block]
    else:
        for f in range(factors):
            shocks[f] = incoming[0][:, f * block : (f + 1) * block]
    get_pairs.wait()

    def fetch_next(c, carry):
        @pl.when(pairs[2, c * chunk] != 0)
        def _():
            fetch(c).start()

        return carry

    lax.fori_loop(1, chunks, fetch_next, 0)
    get_order.wait()

    def place(p, carry):
        owner = p // per_owner
        side = (owner + index) % 2
        position[order[p]] = side * half + ((owner // 2) ^ chip) * per_owner + p % per_owner
        return carry

    lax.fori_loop(0, books, place, 0)

    def group(k):
        terms = []
        for u in range(UNROLL):
            f = pairs[0, k + u] - first_factor
            terms.append(jnp.dot(shocks[f], sens[k + u], preferred_element_type=jnp.float32))
        for u in range(UNROLL):
            live = pairs[2, k + u] != 0
            p = position[pairs[1, k + u]]

            @pl.when(live & (p < half))
            def _():
                kept[p] += terms[u]

            @pl.when(live & (p >= half))
            def _():
                sent[p - half] += terms[u]

    def work(c, carry):
        @pl.when((c == 0) | (pairs[2, c * chunk] != 0))
        def _():
            fetch(c).wait()

            def step(g, inner):
                group(c * chunk + g * UNROLL)
                return inner

            lax.fori_loop(0, chunk // UNROLL, step, 0)

        return carry

    lax.fori_loop(0, chunks, work, 0)


def partials(groups, direct, incoming, sensitivity, block_pairs, book_order):
    slots, block, _ = sensitivity.shape
    own_rows, width = incoming[0].shape
    rows = own_rows * len(incoming)
    books = book_order.shape[0]
    chunks = 16
    hbm = pl.BlockSpec(memory_space=pltpu.HBM)
    vmem = pl.BlockSpec(memory_space=pltpu.VMEM)
    return pl.pallas_call(
        functools.partial(accumulate, groups, direct, len(incoming)),
        in_specs=[vmem] * len(incoming) + [hbm] * 3,
        out_specs=[vmem, vmem],
        out_shape=[jax.ShapeDtypeStruct((books // 2, rows, block), jnp.float32)] * 2,
        scratch_shapes=[
            pltpu.VMEM((len(incoming), own_rows, width) if direct else (8, block), jnp.float32),
            pltpu.VMEM((width // block, rows, block), sensitivity.dtype),
            pltpu.VMEM(sensitivity.shape, sensitivity.dtype),
            pltpu.SMEM((3, slots), jnp.int32),
            pltpu.SMEM((books,), jnp.int32),
            pltpu.SMEM((books,), jnp.int32),
            pltpu.SemaphoreType.DMA((2,)),
            pltpu.SemaphoreType.DMA((chunks,)),
        ],
        compiler_params=pltpu.CompilerParams(vmem_limit_bytes=52 * 1024 * 1024),
        cost_estimate=pl.CostEstimate(
            flops=2 * slots * rows * block * block,
            bytes_accessed=2 * slots * block * block,
            transcendentals=0,
        ),
    )(*incoming, block_pairs.T, book_order, sensitivity)


def shards(returns, vol_hist, vol_now, sensitivity, block_pairs, book_order):
    rescaled = (returns.astype(jnp.float32) * vol_now[None, :] / vol_hist).astype(jnp.bfloat16)
    groups = lax.axis_size("blk")
    index = lax.axis_index("blk")
    own_rows, width = rescaled.shape
    block = sensitivity.shape[1]
    own = width // groups
    rows = groups * own_rows
    direct = groups <= MOST_DIRECT
    if direct:
        incoming = []
        for d in range(groups):
            piece = lax.dynamic_slice_in_dim(rescaled, (index ^ d) * own, own, 1)
            incoming.append(lax.ppermute(piece, "blk", [(i, i ^ d) for i in range(groups)]) if d else piece)
    else:
        outgoing = rescaled.reshape(own_rows, groups, own).transpose(1, 0, 2)
        incoming = [lax.all_to_all(outgoing, "blk", 0, 0).reshape(rows, own)]
    kept, sent = partials(groups, direct, incoming, sensitivity, block_pairs, book_order)
    across = lax.ppermute(sent, "blk", [(i, i ^ 1) for i in range(groups)])
    chips = groups // 2
    books = book_order.shape[0] // groups
    chip_sum = (kept + across).astype(jnp.bfloat16).reshape(chips, books, rows, block)
    if direct:
        owned = chip_sum[0].astype(jnp.float32)
        for d in range(1, chips):
            arrived = lax.ppermute(chip_sum[d], "blk", [(i, i ^ (2 * d)) for i in range(groups)])
            owned = owned + arrived.astype(jnp.float32)
    else:
        same_core = [list(range(core, groups, 2)) for core in range(2)]
        arrived = lax.all_to_all(chip_sum, "blk", 0, 0, axis_index_groups=same_core)
        owned = jnp.sum(arrived.astype(jnp.float32), axis=0)
    profit_loss = owned.transpose(1, 0, 2).reshape(rows, books * block)
    spans = lax.axis_size("scen")
    squares = jnp.sum(owned * owned, axis=1).reshape(-1)
    if spans == 2:
        squares = squares + lax.ppermute(squares, "scen", [(0, 1), (1, 0)])
    else:
        squares = lax.psum(squares, "scen")
    book_rms = jnp.sqrt(squares / (rows * spans) + 1e-06)
    return (profit_loss, book_rms)


def solution(mesh):
    return jax.shard_map(
        shards,
        mesh=mesh,
        in_specs=(
            P(("scen", "blk"), None),
            P(("scen", "blk"), None),
            P(),
            P("blk", None, None),
            P("blk", None),
            P(),
        ),
        out_specs=(P("scen", "blk"), P("blk")),
        check_vma=False,
    )
```

```python
import functools

import jax
import jax.numpy as jnp
from jax import lax
from jax.experimental import pallas as pl
from jax.experimental.pallas import tpu as pltpu
from jax.sharding import PartitionSpec as P

UNROLL = 16
VMEM_LIMIT = 52 * 1024 * 1024


def accumulate(groups, shocks, slots_in, sens_hbm, kept, sent, acc, sens, pairs, position, small, arrived):
    slots = sens.shape[0]
    factors = shocks.shape[0]
    chunks = arrived.shape[0]
    chunk = slots // chunks
    half = kept.shape[0]
    books = 2 * half
    per_owner = books // groups
    index = lax.axis_index("blk")

    def fetch(c):
        span = pl.ds(c * chunk, chunk)
        return pltpu.make_async_copy(sens_hbm.at[span], sens.at[span], arrived.at[c])

    get_pairs = pltpu.make_async_copy(slots_in, pairs, small)
    get_pairs.start()
    fetch(0).start()
    acc[...] = jnp.zeros_like(acc)
    get_pairs.wait()

    def fetch_next(c, count):
        used = pairs[2, c * chunk] != 0

        @pl.when(used)
        def _():
            fetch(c).start()

        return count + used.astype(jnp.int32)

    busy = lax.fori_loop(1, chunks, fetch_next, 1)

    def place(p, carry):
        owner = p // per_owner
        side = (owner + index) % 2
        position[pairs[3, p]] = side * half + (owner // 2) * per_owner + p % per_owner
        return carry

    lax.fori_loop(0, books, place, 0)

    def work(c, carry):
        fetch(c).wait()
        terms = []
        places = []
        for u in range(chunk):
            k = c * chunk + u
            live = pairs[2, k] != 0
            places.append(jnp.where(live, position[pairs[1, k]], books))
            f = pairs[0, k] - index * factors
            terms.append(jnp.dot(shocks[f], sens[k], preferred_element_type=jnp.float32))
        for p, term in zip(places, terms):
            acc[p] += term
        return carry

    lax.fori_loop(0, busy, work, 0)
    kept[...] = acc[:half]
    sent[...] = acc[half:books]


def two_levels(groups):
    low = 1
    while low * low < groups:
        low *= 2
    return groups // low, low


def exchange(blocks, groups):
    high, low = two_levels(groups)
    shape = blocks.shape[1:]
    within = [[h * low + l for l in range(low)] for h in range(high)]
    between = [[h * low + l for h in range(high)] for l in range(low)]
    blocks = blocks.reshape(high, low, *shape).swapaxes(0, 1)
    blocks = lax.all_to_all(blocks, "blk", 0, 0, axis_index_groups=within).swapaxes(0, 1)
    return lax.all_to_all(blocks, "blk", 0, 0, axis_index_groups=between).reshape(groups, *shape)


def shards(returns, vol_hist, vol_now, sensitivity, block_pairs, book_order):
    groups = lax.axis_size("blk")
    own_rows, width = returns.shape
    slots, block, _ = sensitivity.shape
    own = width // groups
    rows = groups * own_rows
    books = book_order.shape[0]
    vmem = pl.BlockSpec(memory_space=pltpu.VMEM)
    hbm = pl.BlockSpec(memory_space=pltpu.HBM)
    rescaled = (returns.astype(jnp.float32) * vol_now[None, :] / vol_hist).astype(jnp.bfloat16)
    outgoing = rescaled.reshape(own_rows, groups, own).swapaxes(0, 1)
    order_row = jnp.pad(book_order, (0, slots - books))[None, :]
    slots_in = jnp.concatenate([block_pairs.T, order_row], axis=0)
    shocks = exchange(outgoing, groups).reshape(rows, own // block, block).transpose(1, 0, 2)
    chunks = slots // UNROLL
    kept, sent = pl.pallas_call(
        functools.partial(accumulate, groups),
        in_specs=[vmem, vmem, hbm],
        out_specs=[vmem, vmem],
        out_shape=[jax.ShapeDtypeStruct((books // 2, rows, block), jnp.float32)] * 2,
        scratch_shapes=[
            pltpu.VMEM((books + 1, rows, block), jnp.float32),
            pltpu.VMEM(sensitivity.shape, sensitivity.dtype),
            pltpu.SMEM((4, slots), jnp.int32),
            pltpu.SMEM((books,), jnp.int32),
            pltpu.SemaphoreType.DMA,
            pltpu.SemaphoreType.DMA((chunks,)),
        ],
        compiler_params=pltpu.CompilerParams(vmem_limit_bytes=VMEM_LIMIT),
        cost_estimate=pl.CostEstimate(
            flops=2 * slots * rows * block * block,
            bytes_accessed=2 * slots * block * block,
            transcendentals=0,
        ),
    )(shocks, slots_in, sensitivity)
    across = lax.ppermute(sent, "blk", [(i, i ^ 1) for i in range(groups)])
    chips = groups // 2
    per_owner = books // groups
    chip_sum = (kept + across).astype(jnp.bfloat16).reshape(chips, per_owner, rows, block)
    same_core = [list(range(core, groups, 2)) for core in range(2)]
    arrived = lax.all_to_all(chip_sum, "blk", 0, 0, axis_index_groups=same_core)
    owned = jnp.sum(arrived.astype(jnp.float32), axis=0)
    profit_loss = owned.transpose(1, 0, 2).reshape(rows, per_owner * block)
    spans = lax.axis_size("scen")
    squares = jnp.sum(owned * owned, axis=1).reshape(-1)
    if spans == 2:
        squares = squares + lax.ppermute(squares, "scen", [(0, 1), (1, 0)])
    else:
        squares = lax.psum(squares, "scen")
    book_rms = jnp.sqrt(squares / (rows * spans) + 1e-06)
    return (profit_loss, book_rms)


def solution(mesh):
    return jax.shard_map(
        shards,
        mesh=mesh,
        in_specs=(
            P(("scen", "blk"), None),
            P(("scen", "blk"), None),
            P(),
            P("blk", None, None),
            P("blk", None),
            P(),
        ),
        out_specs=(P("scen", "blk"), P("blk")),
        check_vma=False,
    )
```

```python
import functools

import jax
import jax.numpy as jnp
from jax import lax
from jax.experimental import pallas as pl
from jax.experimental.pallas import tpu as pltpu
from jax.sharding import PartitionSpec as P

UNROLL = 16
PARTS = 4
VMEM = pl.BlockSpec(memory_space=pltpu.VMEM)
HBM = pl.BlockSpec(memory_space=pltpu.HBM)


def load(first, after, sens_hbm, out, arrived):
    del after
    copy = pltpu.make_async_copy(sens_hbm.at[pl.ds(first, out.shape[0])], out, arrived)
    copy.start()
    copy.wait()


def load_part(part, parts, after, sensitivity):
    slots, block, _ = sensitivity.shape
    size = slots // parts
    return pl.pallas_call(
        functools.partial(load, part * size),
        in_specs=[HBM, HBM],
        out_specs=VMEM,
        out_shape=jax.ShapeDtypeStruct((size, block, block), sensitivity.dtype),
        scratch_shapes=[pltpu.SemaphoreType.DMA],
        compiler_params=pltpu.CompilerParams(vmem_limit_bytes=103 * 512 * 1024),
        cost_estimate=pl.CostEstimate(flops=0, bytes_accessed=4 * size * block * block, transcendentals=0),
    )(after, sensitivity)


def accumulate(groups, parts, shocks, slots_in, *refs):
    sens = refs[:parts]
    kept, sent, acc, pairs, position, small = refs[parts:]
    size = sens[0].shape[0]
    factors = shocks.shape[0]
    half = kept.shape[0]
    books = 2 * half
    per_owner = books // groups
    index = lax.axis_index("blk")

    get_pairs = pltpu.make_async_copy(slots_in, pairs, small)
    get_pairs.start()
    acc[...] = jnp.zeros_like(acc)
    get_pairs.wait()

    def place(p, carry):
        owner = p // per_owner
        side = (owner + index) % 2
        position[pairs[3, p]] = side * half + (owner // 2) * per_owner + p % per_owner
        return carry

    lax.fori_loop(0, books, place, 0)

    for part in range(parts):
        base = part * size

        def count(c, total):
            return total + jnp.where(pairs[2, base + c * UNROLL] != 0, 1, 0)

        def work(c, carry):
            terms = []
            places = []
            for u in range(UNROLL):
                k = c * UNROLL + u
                live = pairs[2, base + k] != 0
                places.append(jnp.where(live, position[pairs[1, base + k]], books))
                f = pairs[0, base + k] - index * factors
                terms.append(jnp.dot(shocks[f], sens[part][k], preferred_element_type=jnp.float32))
            for p, term in zip(places, terms):
                acc[p] += term
            return carry

        lax.fori_loop(0, lax.fori_loop(0, size // UNROLL, count, 0), work, 0)
    kept[...] = acc[:half]
    sent[...] = acc[half:books]


def shards(returns, vol_hist, vol_now, sensitivity, block_pairs, book_order):
    groups = lax.axis_size("blk")
    own_rows, width = returns.shape
    slots, block, _ = sensitivity.shape
    own = width // groups
    rows = groups * own_rows
    books = book_order.shape[0]
    rescaled = (returns.astype(jnp.float32) * vol_now[None, :] / vol_hist).astype(jnp.bfloat16)
    order_row = jnp.pad(book_order, (0, slots - books))[None, :]
    slots_in = jnp.concatenate([block_pairs.T, order_row], axis=0)
    stages = groups.bit_length() - 1
    blocks = rescaled.reshape(own_rows, groups, own).swapaxes(0, 1)
    blocks = blocks.reshape(*[2] * stages, own_rows, own)
    index = lax.axis_index("blk")
    sens = []
    for stage in range(stages):
        shift = stages - 1 - stage
        bit = (index >> shift) & 1
        away = lax.dynamic_index_in_dim(blocks, 1 - bit, stage, keepdims=False)
        stay = lax.dynamic_index_in_dim(blocks, bit, stage, keepdims=False)
        come = lax.ppermute(away, "blk", [(i, i ^ (1 << shift)) for i in range(groups)])
        if stage < PARTS:
            part = load_part(stage, PARTS, stay, sensitivity)
            come, part = lax.optimization_barrier((come, part))
            sens.append(part)
        blocks = jnp.where(bit == 0, jnp.stack([stay, come], stage), jnp.stack([come, stay], stage))
    shocks = blocks.reshape(rows, own // block, block).transpose(1, 0, 2)
    kept, sent = pl.pallas_call(
        functools.partial(accumulate, groups, PARTS),
        in_specs=[VMEM] * (2 + PARTS),
        out_specs=[VMEM, VMEM],
        out_shape=[jax.ShapeDtypeStruct((books // 2, rows, block), jnp.float32)] * 2,
        scratch_shapes=[
            pltpu.VMEM((books + 1, rows, block), jnp.float32),
            pltpu.SMEM((4, slots), jnp.int32),
            pltpu.SMEM((books,), jnp.int32),
            pltpu.SemaphoreType.DMA,
        ],
        compiler_params=pltpu.CompilerParams(vmem_limit_bytes=32 * 1024 * 1024),
        cost_estimate=pl.CostEstimate(
            flops=2 * slots * rows * block * block,
            bytes_accessed=2 * slots * block * block,
            transcendentals=0,
        ),
    )(shocks, slots_in, *sens)
    across = lax.ppermute(sent, "blk", [(i, i ^ 1) for i in range(groups)])
    chips = groups // 2
    per_owner = books // groups
    chip_sum = (kept + across).astype(jnp.bfloat16).reshape(chips, per_owner, rows, block)
    same_core = [list(range(core, groups, 2)) for core in range(2)]
    arrived = lax.all_to_all(chip_sum, "blk", 0, 0, axis_index_groups=same_core)
    owned = jnp.sum(arrived.astype(jnp.float32), axis=0)
    profit_loss = owned.transpose(1, 0, 2).reshape(rows, per_owner * block)
    spans = lax.axis_size("scen")
    squares = jnp.sum(owned * owned, axis=1).reshape(-1)
    if spans == 2:
        squares = squares + lax.ppermute(squares, "scen", [(0, 1), (1, 0)])
    else:
        squares = lax.psum(squares, "scen")
    book_rms = jnp.sqrt(squares / (rows * spans) + 1e-06)
    return (profit_loss, book_rms)


def solution(mesh):
    return jax.shard_map(
        shards,
        mesh=mesh,
        in_specs=(
            P(("scen", "blk"), None),
            P(("scen", "blk"), None),
            P(),
            P("blk", None, None),
            P("blk", None),
            P(),
        ),
        out_specs=(P("scen", "blk"), P("blk")),
        check_vma=False,
    )
```

```python
import functools

import jax
import jax.numpy as jnp
from jax import lax
from jax.experimental import pallas as pl
from jax.experimental.pallas import tpu as pltpu
from jax.sharding import PartitionSpec as P

UNROLL = 32
VMEM_LIMIT = 52 * 1024 * 1024
VMEM = pl.BlockSpec(memory_space=pltpu.VMEM)
HBM = pl.BlockSpec(memory_space=pltpu.HBM)


def accumulate(groups, shocks, slots_in, sens_hbm, kept, sent, acc, sens, pairs, position, small, arrived):
    slots = sens.shape[0]
    factors = shocks.shape[0]
    chunks = arrived.shape[0]
    chunk = slots // chunks
    half = kept.shape[0]
    books = 2 * half
    per_owner = books // groups
    index = lax.axis_index("blk")
    core = index & 1

    def fetch(c):
        span = pl.ds(c * chunk, chunk)
        return pltpu.make_async_copy(sens_hbm.at[span], sens.at[span], arrived.at[c])

    get_pairs = pltpu.make_async_copy(slots_in, pairs, small)
    get_pairs.start()
    for c in range(chunks):
        fetch(c).start()
    acc[...] = jnp.zeros_like(acc)
    get_pairs.wait()
    for p in range(books):
        owner = p // per_owner
        place = (owner // 2) * per_owner + p % per_owner
        position[pairs[3, p]] = place + half * ((owner & 1) ^ core)
    position[books] = books
    first_factor = index * factors

    def work(c, carry):
        fetch(c).wait()

        @pl.when(pairs[2, c * chunk] != 0)
        def _():
            terms = []
            places = []
            for u in range(chunk):
                k = c * chunk + u
                book = jnp.where(pairs[2, k] != 0, pairs[1, k], books)
                places.append(position[book])
                f = pairs[0, k] - first_factor
                terms.append(jnp.dot(shocks[f], sens[k], preferred_element_type=jnp.float32))
            for p, term in zip(places, terms):
                acc[p] += term

        return carry

    lax.fori_loop(0, chunks, work, 0)
    kept[...] = acc[:half]
    sent[...] = acc[half:books].astype(sent.dtype)


def shards(returns, vol_hist, vol_now, sensitivity, block_pairs, book_order):
    groups = lax.axis_size("blk")
    own_rows, width = returns.shape
    slots, block, _ = sensitivity.shape
    own = width // groups
    rows = groups * own_rows
    books = book_order.shape[0]
    chips = groups // 2
    core = lax.axis_index("blk") & 1
    same_core = [list(range(c, groups, 2)) for c in range(2)]
    siblings = [(i, i ^ 1) for i in range(groups)]
    rescaled = (returns.astype(jnp.float32) * vol_now[None, :] / vol_hist).astype(jnp.bfloat16)
    outgoing = rescaled.reshape(own_rows, groups, own).swapaxes(0, 1).reshape(chips, 2, own_rows, own)
    at_chip = lax.all_to_all(outgoing, "blk", 0, 0, axis_index_groups=same_core)
    stay = lax.dynamic_index_in_dim(at_chip, core, 1, keepdims=False)
    come = lax.ppermute(lax.dynamic_index_in_dim(at_chip, 1 - core, 1, keepdims=False), "blk", siblings)
    incoming = jnp.where(core == 0, jnp.stack([stay, come], 1), jnp.stack([come, stay], 1))
    shocks = incoming.reshape(rows, own // block, block).transpose(1, 0, 2)
    slots_in = jnp.pad(block_pairs.T, ((0, 1), (0, 0))) + jnp.pad(book_order[None, :], ((3, 0), (0, slots - books)))
    chunks = slots // UNROLL
    kept, sent = pl.pallas_call(
        functools.partial(accumulate, groups),
        in_specs=[VMEM, VMEM, HBM],
        out_specs=[VMEM, VMEM],
        out_shape=[
            jax.ShapeDtypeStruct((books // 2, rows, block), jnp.float32),
            jax.ShapeDtypeStruct((books // 2, rows, block), jnp.bfloat16),
        ],
        scratch_shapes=[
            pltpu.VMEM((books + 1, rows, block), jnp.float32),
            pltpu.VMEM(sensitivity.shape, sensitivity.dtype),
            pltpu.SMEM((4, slots), jnp.int32),
            pltpu.SMEM((books + 1,), jnp.int32),
            pltpu.SemaphoreType.DMA,
            pltpu.SemaphoreType.DMA((chunks,)),
        ],
        compiler_params=pltpu.CompilerParams(vmem_limit_bytes=VMEM_LIMIT),
        cost_estimate=pl.CostEstimate(
            flops=2 * slots * rows * block * block,
            bytes_accessed=2 * slots * block * block,
            transcendentals=0,
        ),
    )(shocks, slots_in, sensitivity)
    across = lax.ppermute(sent, "blk", siblings)
    per_owner = books // groups
    chip_sum = (kept + across.astype(jnp.float32)).astype(jnp.bfloat16).reshape(chips, per_owner, rows, block)
    arrived = lax.all_to_all(chip_sum, "blk", 0, 0, axis_index_groups=same_core)
    owned = jnp.sum(arrived.astype(jnp.float32), axis=0)
    profit_loss = owned.transpose(1, 0, 2).reshape(rows, per_owner * block)
    spans = lax.axis_size("scen")
    squares = jnp.sum(owned * owned, axis=1).reshape(-1)
    if spans == 2:
        squares = squares + lax.ppermute(squares, "scen", [(0, 1), (1, 0)])
    else:
        squares = lax.psum(squares, "scen")
    book_rms = jnp.sqrt(squares / (rows * spans) + 1e-06)
    return (profit_loss, book_rms)


def solution(mesh):
    return jax.shard_map(
        shards,
        mesh=mesh,
        in_specs=(
            P(("scen", "blk"), None),
            P(("scen", "blk"), None),
            P(),
            P("blk", None, None),
            P("blk", None),
            P(),
        ),
        out_specs=(P("scen", "blk"), P("blk")),
        check_vma=False,
    )
```

```python
import functools

import jax
import jax.numpy as jnp
from jax import lax
from jax.experimental import pallas as pl
from jax.experimental.pallas import tpu as pltpu
from jax.sharding import PartitionSpec as P

UNROLL = 32
VMEM_LIMIT = 52 * 1024 * 1024
VMEM = pl.BlockSpec(memory_space=pltpu.VMEM)
HBM = pl.BlockSpec(memory_space=pltpu.HBM)


def accumulate(groups, shocks, slots_in, sens_hbm, kept, sent, acc, sens, pairs, position, small, arrived):
    slots = sens.shape[0]
    factors = shocks.shape[0]
    chunks = arrived.shape[0]
    chunk = slots // chunks
    half = kept.shape[0]
    books = 2 * half
    per_owner = books // groups
    index = lax.axis_index("blk")
    core = index & 1

    def fetch(c):
        span = pl.ds(c * chunk, chunk)
        return pltpu.make_async_copy(sens_hbm.at[span], sens.at[span], arrived.at[c])

    get_pairs = pltpu.make_async_copy(slots_in, pairs, small)
    get_pairs.start()
    for c in range(chunks):
        fetch(c).start()
    acc[...] = jnp.zeros_like(acc)
    get_pairs.wait()
    for p in range(books):
        owner = p // per_owner
        place = (owner // 2) * per_owner + p % per_owner
        position[pairs[3, p]] = place + half * ((owner & 1) ^ core)
    position[books] = books
    first_factor = index * factors

    def work(c, carry):
        fetch(c).wait()

        @pl.when(pairs[2, c * chunk] != 0)
        def _():
            terms = []
            places = []
            for u in range(chunk):
                k = c * chunk + u
                book = jnp.where(pairs[2, k] != 0, pairs[1, k], books)
                places.append(position[book])
                f = pairs[0, k] - first_factor
                terms.append(jnp.dot(shocks[f], sens[k], preferred_element_type=jnp.float32))
            for p, term in zip(places, terms):
                acc[p] += term

        return carry

    lax.fori_loop(0, chunks, work, 0)
    kept[...] = acc[:half]
    sent[...] = acc[half:books].astype(sent.dtype)


def shards(returns, vol_hist, vol_now, sensitivity, block_pairs, book_order):
    groups = lax.axis_size("blk")
    own_rows, width = returns.shape
    slots, block, _ = sensitivity.shape
    own = width // groups
    rows = groups * own_rows
    books = book_order.shape[0]
    chips = groups // 2
    core = lax.axis_index("blk") & 1
    same_core = [list(range(c, groups, 2)) for c in range(2)]
    siblings = [(i, i ^ 1) for i in range(groups)]
    rescaled = (returns.astype(jnp.float32) * vol_now[None, :] / vol_hist).astype(jnp.bfloat16)
    outgoing = rescaled.reshape(own_rows, groups, own).swapaxes(0, 1).reshape(chips, 2, own_rows, own)
    at_chip = lax.all_to_all(outgoing, "blk", 0, 0, axis_index_groups=same_core)
    at_chip, block_pairs, book_order = lax.optimization_barrier((at_chip, block_pairs, book_order))
    stay = lax.dynamic_index_in_dim(at_chip, core, 1, keepdims=False)
    come = lax.ppermute(lax.dynamic_index_in_dim(at_chip, 1 - core, 1, keepdims=False), "blk", siblings)
    incoming = jnp.where(core == 0, jnp.stack([stay, come], 1), jnp.stack([come, stay], 1))
    shocks = incoming.reshape(rows, own // block, block).transpose(1, 0, 2)
    slots_in = jnp.pad(block_pairs.T, ((0, 1), (0, 0))) + jnp.pad(book_order[None, :], ((3, 0), (0, slots - books)))
    chunks = slots // UNROLL
    kept, sent = pl.pallas_call(
        functools.partial(accumulate, groups),
        in_specs=[VMEM, VMEM, HBM],
        out_specs=[VMEM, VMEM],
        out_shape=[
            jax.ShapeDtypeStruct((books // 2, rows, block), jnp.float32),
            jax.ShapeDtypeStruct((books // 2, rows, block), jnp.bfloat16),
        ],
        scratch_shapes=[
            pltpu.VMEM((books + 1, rows, block), jnp.float32),
            pltpu.VMEM(sensitivity.shape, sensitivity.dtype),
            pltpu.SMEM((4, slots), jnp.int32),
            pltpu.SMEM((books + 1,), jnp.int32),
            pltpu.SemaphoreType.DMA,
            pltpu.SemaphoreType.DMA((chunks,)),
        ],
        compiler_params=pltpu.CompilerParams(vmem_limit_bytes=VMEM_LIMIT),
        cost_estimate=pl.CostEstimate(
            flops=2 * slots * rows * block * block,
            bytes_accessed=2 * slots * block * block,
            transcendentals=0,
        ),
    )(shocks, slots_in, sensitivity)
    across = lax.ppermute(sent, "blk", siblings)
    per_owner = books // groups
    chip_sum = (kept + across.astype(jnp.float32)).astype(jnp.bfloat16).reshape(chips, per_owner, rows, block)
    arrived = lax.all_to_all(chip_sum, "blk", 0, 0, axis_index_groups=same_core)
    owned = jnp.sum(arrived.astype(jnp.float32), axis=0)
    profit_loss = owned.transpose(1, 0, 2).reshape(rows, per_owner * block)
    spans = lax.axis_size("scen")
    squares = jnp.sum(owned * owned, axis=1).reshape(-1)
    if spans == 2:
        squares = squares + lax.ppermute(squares, "scen", [(0, 1), (1, 0)])
    else:
        squares = lax.psum(squares, "scen")
    book_rms = jnp.sqrt(squares / (rows * spans) + 1e-06)
    return (profit_loss, book_rms)


def solution(mesh):
    return jax.shard_map(
        shards,
        mesh=mesh,
        in_specs=(
            P(("scen", "blk"), None),
            P(("scen", "blk"), None),
            P(),
            P("blk", None, None),
            P("blk", None),
            P(),
        ),
        out_specs=(P("scen", "blk"), P("blk")),
        check_vma=False,
    )
```

```python
import functools

import jax
import jax.numpy as jnp
from jax import lax
from jax.experimental import pallas as pl
from jax.experimental.pallas import tpu as pltpu
from jax.sharding import PartitionSpec as P

UNROLL = 32
VMEM_LIMIT = 52 * 1024 * 1024
VMEM = pl.BlockSpec(memory_space=pltpu.VMEM)
HBM = pl.BlockSpec(memory_space=pltpu.HBM)


def accumulate(groups, shocks, slots_in, sens_hbm, kept, sent, acc, sens, pairs, position, small, arrived):
    slots = sens.shape[0]
    factors = shocks.shape[0]
    chunks = arrived.shape[0]
    chunk = slots // chunks
    half = kept.shape[0]
    books = 2 * half
    per_owner = books // groups
    index = lax.axis_index("blk")
    core = index & 1

    def fetch(c):
        span = pl.ds(c * chunk, chunk)
        return pltpu.make_async_copy(sens_hbm.at[span], sens.at[span], arrived.at[c])

    get_pairs = pltpu.make_async_copy(slots_in, pairs, small)
    get_pairs.start()
    for c in range(chunks):
        fetch(c).start()
    acc[...] = jnp.zeros_like(acc)
    get_pairs.wait()
    for p in range(books):
        owner = p // per_owner
        place = (owner // 2) * per_owner + p % per_owner
        position[pairs[3, p]] = place + half * ((owner & 1) ^ core)
    position[books] = books
    first_factor = index * factors

    def work(c, carry):
        fetch(c).wait()

        @pl.when(pairs[2, c * chunk] != 0)
        def _():
            terms = []
            places = []
            for u in range(chunk):
                k = c * chunk + u
                book = jnp.where(pairs[2, k] != 0, pairs[1, k], books)
                places.append(position[book])
                f = pairs[0, k] - first_factor
                terms.append(jnp.dot(shocks[f], sens[k], preferred_element_type=jnp.float32))
            for p, term in zip(places, terms):
                acc[p] += term

        return carry

    lax.fori_loop(0, chunks, work, 0)
    kept[...] = acc[:half]
    sent[...] = acc[half:books].astype(sent.dtype)


def shards(returns, vol_hist, vol_now, sensitivity, block_pairs, book_order):
    groups = lax.axis_size("blk")
    own_rows, width = returns.shape
    slots, block, _ = sensitivity.shape
    own = width // groups
    rows = groups * own_rows
    books = book_order.shape[0]
    siblings = [(i, i ^ 1) for i in range(groups)]
    rescaled = (returns.astype(jnp.float32) * vol_now[None, :] / vol_hist).astype(jnp.bfloat16)
    outgoing = rescaled.reshape(own_rows, groups, own).swapaxes(0, 1)
    incoming = lax.all_to_all(outgoing, "blk", 0, 0)
    shocks = incoming.reshape(rows, own // block, block).transpose(1, 0, 2)
    slots_in = jnp.pad(block_pairs.T, ((0, 1), (0, 0))) + jnp.pad(book_order[None, :], ((3, 0), (0, slots - books)))
    chunks = slots // UNROLL
    kept, sent = pl.pallas_call(
        functools.partial(accumulate, groups),
        in_specs=[VMEM, VMEM, HBM],
        out_specs=[VMEM, VMEM],
        out_shape=[
            jax.ShapeDtypeStruct((books // 2, rows, block), jnp.float32),
            jax.ShapeDtypeStruct((books // 2, rows, block), jnp.bfloat16),
        ],
        scratch_shapes=[
            pltpu.VMEM((books + 1, rows, block), jnp.float32),
            pltpu.VMEM(sensitivity.shape, sensitivity.dtype),
            pltpu.SMEM((4, slots), jnp.int32),
            pltpu.SMEM((books + 1,), jnp.int32),
            pltpu.SemaphoreType.DMA,
            pltpu.SemaphoreType.DMA((chunks,)),
        ],
        compiler_params=pltpu.CompilerParams(vmem_limit_bytes=VMEM_LIMIT),
        cost_estimate=pl.CostEstimate(
            flops=2 * slots * rows * block * block,
            bytes_accessed=2 * slots * block * block,
            transcendentals=0,
        ),
    )(shocks, slots_in, sensitivity)
    across = lax.ppermute(sent, "blk", siblings)
    per_owner = books // groups
    quads = groups // 4
    chip_sum = (kept + across.astype(jnp.float32)).reshape(quads, 2, per_owner, rows, block)
    side = (lax.axis_index("blk") >> 1) & 1
    away = lax.dynamic_index_in_dim(chip_sum, 1 - side, 1, keepdims=False).astype(jnp.bfloat16)
    stay = lax.dynamic_index_in_dim(chip_sum, side, 1, keepdims=False)
    come = lax.ppermute(away, "blk", [(i, i ^ 2) for i in range(groups)])
    quad_sum = (stay + come.astype(jnp.float32)).astype(jnp.bfloat16)
    columns = [list(range(c, groups, 4)) for c in range(4)]
    arrived = lax.all_to_all(quad_sum, "blk", 0, 0, axis_index_groups=columns)
    owned = jnp.sum(arrived.astype(jnp.float32), axis=0)
    profit_loss = owned.transpose(1, 0, 2).reshape(rows, per_owner * block)
    spans = lax.axis_size("scen")
    squares = jnp.sum(owned * owned, axis=1).reshape(-1)
    if spans == 2:
        squares = squares + lax.ppermute(squares, "scen", [(0, 1), (1, 0)])
    else:
        squares = lax.psum(squares, "scen")
    book_rms = jnp.sqrt(squares / (rows * spans) + 1e-06)
    return (profit_loss, book_rms)


def solution(mesh):
    return jax.shard_map(
        shards,
        mesh=mesh,
        in_specs=(
            P(("scen", "blk"), None),
            P(("scen", "blk"), None),
            P(),
            P("blk", None, None),
            P("blk", None),
            P(),
        ),
        out_specs=(P("scen", "blk"), P("blk")),
        check_vma=False,
    )
```

```python
import functools

import jax
import jax.numpy as jnp
from jax import lax
from jax.experimental import pallas as pl
from jax.experimental.pallas import tpu as pltpu
from jax.sharding import PartitionSpec as P

UNROLL = 32
VMEM_LIMIT = 52 * 1024 * 1024
VMEM = pl.BlockSpec(memory_space=pltpu.VMEM)
HBM = pl.BlockSpec(memory_space=pltpu.HBM)


def accumulate(groups, shocks, slots_in, sens_hbm, kept, sent, acc, sens, pairs, position, small, arrived):
    slots = sens.shape[0]
    factors, _, block = shocks.shape
    chunks = arrived.shape[0]
    chunk = slots // chunks
    half = kept.shape[0]
    books = 2 * half
    per_owner = books // groups
    index = lax.axis_index("blk")
    core = index & 1

    def fetch(c):
        span = pl.ds(c * chunk, chunk)
        return pltpu.make_async_copy(sens_hbm.at[span], sens.at[span], arrived.at[c])

    get_pairs = pltpu.make_async_copy(slots_in, pairs, small)
    get_pairs.start()
    for c in range(chunks):
        fetch(c).start()
    acc[...] = jnp.zeros_like(acc)
    get_pairs.wait()
    for p in range(books):
        owner = p // per_owner
        place = (owner // 2) * per_owner + p % per_owner
        position[pairs[3, p]] = place + half * ((owner & 1) ^ core)
    position[books] = books
    first_factor = index * factors
    none = jnp.zeros(sens.shape[1:], sens.dtype)

    def work(c, carry):
        fetch(c).wait()

        @pl.when(pairs[2, c * chunk] != 0)
        def _():
            terms = []
            places = []
            for u in range(0, chunk, 2):
                k = c * chunk + u
                for t in range(2):
                    book = jnp.where(pairs[2, k + t] != 0, pairs[1, k + t], books)
                    places.append(position[book])
                scenarios = [shocks[pairs[0, k + t] - first_factor] for t in range(2)]
                first = jnp.concatenate([sens[k], none], axis=1)
                second = jnp.concatenate([none, sens[k + 1]], axis=1)
                both = jnp.dot(
                    jnp.concatenate(scenarios, axis=1),
                    jnp.concatenate([first, second], axis=0),
                    preferred_element_type=jnp.float32,
                )
                terms += [both[:, :block], both[:, block:]]
            for p, term in zip(places, terms):
                acc[p] += term

        return carry

    lax.fori_loop(0, chunks, work, 0)
    kept[...] = acc[:half]
    sent[...] = acc[half:books].astype(sent.dtype)


def shards(returns, vol_hist, vol_now, sensitivity, block_pairs, book_order):
    groups = lax.axis_size("blk")
    own_rows, width = returns.shape
    slots, block, _ = sensitivity.shape
    own = width // groups
    rows = groups * own_rows
    books = book_order.shape[0]
    siblings = [(i, i ^ 1) for i in range(groups)]
    rescaled = (returns.astype(jnp.float32) * vol_now[None, :] / vol_hist).astype(jnp.bfloat16)
    outgoing = rescaled.reshape(own_rows, groups, own).swapaxes(0, 1)
    incoming = lax.all_to_all(outgoing, "blk", 0, 0)
    incoming, block_pairs, book_order = lax.optimization_barrier((incoming, block_pairs, book_order))
    shocks = incoming.reshape(rows, own // block, block).transpose(1, 0, 2)
    slots_in = jnp.pad(block_pairs.T, ((0, 1), (0, 0))) + jnp.pad(book_order[None, :], ((3, 0), (0, slots - books)))
    chunks = slots // UNROLL
    kept, sent = pl.pallas_call(
        functools.partial(accumulate, groups),
        in_specs=[VMEM, VMEM, HBM],
        out_specs=[VMEM, VMEM],
        out_shape=[
            jax.ShapeDtypeStruct((books // 2, rows, block), jnp.float32),
            jax.ShapeDtypeStruct((books // 2, rows, block), jnp.bfloat16),
        ],
        scratch_shapes=[
            pltpu.VMEM((books + 1, rows, block), jnp.float32),
            pltpu.VMEM(sensitivity.shape, sensitivity.dtype),
            pltpu.SMEM((4, slots), jnp.int32),
            pltpu.SMEM((books + 1,), jnp.int32),
            pltpu.SemaphoreType.DMA,
            pltpu.SemaphoreType.DMA((chunks,)),
        ],
        compiler_params=pltpu.CompilerParams(vmem_limit_bytes=VMEM_LIMIT),
        cost_estimate=pl.CostEstimate(
            flops=2 * slots * rows * block * block,
            bytes_accessed=2 * slots * block * block,
            transcendentals=0,
        ),
    )(shocks, slots_in, sensitivity)
    across = lax.ppermute(sent, "blk", siblings)
    per_owner = books // groups
    chips = groups // 2
    chip_sum = (kept + across.astype(jnp.float32)).astype(jnp.bfloat16).reshape(chips, per_owner, rows, block)
    same_core = [list(range(c, groups, 2)) for c in range(2)]
    arrived = lax.all_to_all(chip_sum, "blk", 0, 0, axis_index_groups=same_core)
    owned = jnp.sum(arrived.astype(jnp.float32), axis=0)
    profit_loss = owned.transpose(1, 0, 2).reshape(rows, per_owner * block)
    spans = lax.axis_size("scen")
    squares = jnp.sum(owned * owned, axis=1).reshape(-1)
    if spans == 2:
        squares = squares + lax.ppermute(squares, "scen", [(0, 1), (1, 0)])
    else:
        squares = lax.psum(squares, "scen")
    book_rms = jnp.sqrt(squares / (rows * spans) + 1e-06)
    return (profit_loss, book_rms)


def solution(mesh):
    return jax.shard_map(
        shards,
        mesh=mesh,
        in_specs=(
            P(("scen", "blk"), None),
            P(("scen", "blk"), None),
            P(),
            P("blk", None, None),
            P("blk", None),
            P(),
        ),
        out_specs=(P("scen", "blk"), P("blk")),
        check_vma=False,
    )
```

```python
import functools

import jax
import jax.numpy as jnp
from jax import lax
from jax.experimental import pallas as pl
from jax.experimental.pallas import tpu as pltpu
from jax.sharding import PartitionSpec as P

UNROLL = 32
VMEM_LIMIT = 52 * 1024 * 1024
VMEM = pl.BlockSpec(memory_space=pltpu.VMEM)
HBM = pl.BlockSpec(memory_space=pltpu.HBM)


def accumulate(
    groups, mine, other, slots_in, sens_hbm, kept, sent, shocks, acc, sens, pairs, position, small, arrived
):
    slots = sens.shape[0]
    factors, _, block = shocks.shape
    chunks = arrived.shape[0]
    chunk = slots // chunks
    half = kept.shape[0]
    books = 2 * half
    per_owner = books // groups
    index = lax.axis_index("blk")
    core = index & 1

    def fetch(c):
        span = pl.ds(c * chunk, chunk)
        return pltpu.make_async_copy(sens_hbm.at[span], sens.at[span], arrived.at[c])

    get_pairs = pltpu.make_async_copy(slots_in, pairs, small)
    get_pairs.start()
    for c in range(chunks):
        fetch(c).start()
    acc[...] = jnp.zeros_like(acc)
    chips, _, own_rows, _ = mine.shape
    together = max(1, 16 // (2 * own_rows))
    for first_chip in range(0, chips, together):
        pieces = []
        for chip in range(first_chip, first_chip + together):
            same = mine[chip, core].astype(jnp.float32)
            cross = other[chip, core].astype(jnp.float32)
            pieces += [jnp.where(core == 0, same, cross), jnp.where(core == 0, cross, same)]
        span = pl.ds(first_chip * 2 * own_rows, together * 2 * own_rows)
        days = jnp.concatenate(pieces, axis=0).astype(shocks.dtype)
        for f in range(factors):
            shocks[f, span] = days[:, f * block : (f + 1) * block]
    get_pairs.wait()
    for p in range(books):
        owner = p // per_owner
        place = (owner // 2) * per_owner + p % per_owner
        position[pairs[3, p]] = place + half * ((owner & 1) ^ core)
    position[books] = books
    first_factor = index * factors

    def work(c, carry):
        fetch(c).wait()

        @pl.when(pairs[2, c * chunk] != 0)
        def _():
            terms = []
            places = []
            for u in range(chunk):
                k = c * chunk + u
                book = jnp.where(pairs[2, k] != 0, pairs[1, k], books)
                places.append(position[book])
                f = pairs[0, k] - first_factor
                terms.append(jnp.dot(shocks[f], sens[k], preferred_element_type=jnp.float32))
            for p, term in zip(places, terms):
                acc[p] += term

        return carry

    lax.fori_loop(0, chunks, work, 0)
    kept[...] = acc[:half]
    sent[...] = acc[half:books].astype(sent.dtype)


def shards(returns, vol_hist, vol_now, sensitivity, block_pairs, book_order):
    groups = lax.axis_size("blk")
    own_rows, width = returns.shape
    slots, block, _ = sensitivity.shape
    own = width // groups
    rows = groups * own_rows
    books = book_order.shape[0]
    siblings = [(i, i ^ 1) for i in range(groups)]
    rescaled = (returns.astype(jnp.float32) * vol_now[None, :] / vol_hist).astype(jnp.bfloat16)
    chips = groups // 2
    same_core = [list(range(c, groups, 2)) for c in range(2)]
    outgoing = rescaled.reshape(own_rows, groups, own).swapaxes(0, 1).reshape(chips, 2, own_rows, own)
    mine = lax.all_to_all(outgoing, "blk", 0, 0, axis_index_groups=same_core)
    mine, block_pairs, book_order = lax.optimization_barrier((mine, block_pairs, book_order))
    other = lax.ppermute(mine, "blk", siblings)
    slots_in = jnp.pad(block_pairs.T, ((0, 1), (0, 0))) + jnp.pad(book_order[None, :], ((3, 0), (0, slots - books)))
    chunks = slots // UNROLL
    kept, sent = pl.pallas_call(
        functools.partial(accumulate, groups),
        in_specs=[VMEM, VMEM, VMEM, HBM],
        out_specs=[VMEM, VMEM],
        out_shape=[
            jax.ShapeDtypeStruct((books // 2, rows, block), jnp.float32),
            jax.ShapeDtypeStruct((books // 2, rows, block), jnp.bfloat16),
        ],
        scratch_shapes=[
            pltpu.VMEM((own // block, rows, block), jnp.bfloat16),
            pltpu.VMEM((books + 1, rows, block), jnp.float32),
            pltpu.VMEM(sensitivity.shape, sensitivity.dtype),
            pltpu.SMEM((4, slots), jnp.int32),
            pltpu.SMEM((books + 1,), jnp.int32),
            pltpu.SemaphoreType.DMA,
            pltpu.SemaphoreType.DMA((chunks,)),
        ],
        compiler_params=pltpu.CompilerParams(vmem_limit_bytes=VMEM_LIMIT),
        cost_estimate=pl.CostEstimate(
            flops=2 * slots * rows * block * block,
            bytes_accessed=2 * slots * block * block,
            transcendentals=0,
        ),
    )(mine, other, slots_in, sensitivity)
    across = lax.ppermute(sent, "blk", siblings)
    per_owner = books // groups
    chip_sum = (kept + across.astype(jnp.float32)).astype(jnp.bfloat16).reshape(chips, per_owner, rows, block)
    arrived = lax.all_to_all(chip_sum, "blk", 0, 0, axis_index_groups=same_core)
    owned = jnp.sum(arrived.astype(jnp.float32), axis=0)
    profit_loss = owned.transpose(1, 0, 2).reshape(rows, per_owner * block)
    spans = lax.axis_size("scen")
    squares = jnp.sum(owned * owned, axis=1).reshape(-1)
    if spans == 2:
        squares = squares + lax.ppermute(squares, "scen", [(0, 1), (1, 0)])
    else:
        squares = lax.psum(squares, "scen")
    book_rms = jnp.sqrt(squares / (rows * spans) + 1e-06)
    return (profit_loss, book_rms)


def solution(mesh):
    return jax.shard_map(
        shards,
        mesh=mesh,
        in_specs=(
            P(("scen", "blk"), None),
            P(("scen", "blk"), None),
            P(),
            P("blk", None, None),
            P("blk", None),
            P(),
        ),
        out_specs=(P("scen", "blk"), P("blk")),
        check_vma=False,
    )
```

```python
import functools

import jax
import jax.numpy as jnp
from jax import lax
from jax.experimental import pallas as pl
from jax.experimental.pallas import tpu as pltpu
from jax.sharding import PartitionSpec as P

UNROLL = 16
CHUNKS = 8
PREPARE_VMEM = 44 * 1024 * 1024
PRODUCT_VMEM = 16 * 1024 * 1024
VMEM = pl.BlockSpec(memory_space=pltpu.VMEM)
SMEM = pl.BlockSpec(memory_space=pltpu.SMEM)
HBM = pl.BlockSpec(memory_space=pltpu.HBM)


def prepare(groups, factors, after, pairs_hbm, order_hbm, sens_hbm, sens, table, pairs, order, position, small, arrived):
    del after
    slots = sens.shape[0]
    books = order.shape[0]
    half = books // 2
    per_owner = books // groups
    index = lax.axis_index("blk")
    core = index & 1
    first_factor = index * factors
    get_pairs = pltpu.make_async_copy(pairs_hbm, pairs, small.at[0])
    get_order = pltpu.make_async_copy(order_hbm, order, small.at[1])
    get_pairs.start()
    get_order.start()
    chunk = slots // CHUNKS
    fetches = []
    for c in range(CHUNKS):
        span = pl.ds(c * chunk, chunk)
        fetches.append(pltpu.make_async_copy(sens_hbm.at[span], sens.at[span], arrived.at[c]))
        fetches[c].start()
    get_order.wait()
    for p in range(books):
        owner = p // per_owner
        place = (owner // 2) * per_owner + p % per_owner
        position[order[p]] = place + half * ((owner & 1) ^ core)
    position[books] = books
    get_pairs.wait()

    def write(n, f, k, column):
        book = jnp.where(pairs[2, k] != 0, pairs[1, k], books)
        table[column, n] = k
        table[2 + column, n] = position[book]
        table[4, n] = f

    def match(k, carry):
        n, *pending = carry
        f = pairs[0, k] - first_factor
        live = pairs[2, k] != 0
        waiting = pending[0]
        for i in range(1, factors):
            waiting = jnp.where(f == i, pending[i], waiting)
        found = live & (waiting >= 0)
        write(n, f, jnp.maximum(waiting, 0), 0)
        write(n, f, k, 1)
        kept = jnp.where(waiting >= 0, -1, k)
        pending = [jnp.where(live & (f == i), kept, pending[i]) for i in range(factors)]
        return (n + found.astype(jnp.int32), *pending)

    n, *pending = lax.fori_loop(0, slots, match, (jnp.int32(0),) + (jnp.int32(-1),) * factors, unroll=8)
    for i in range(factors):
        write(n, i, jnp.maximum(pending[i], 0), 0)
        table[1, n] = 0
        table[3, n] = books
        n = n + (pending[i] >= 0).astype(jnp.int32)
    table[5, 0] = n
    for i in range(UNROLL):
        for row, value in enumerate((0, 0, books, books, 0)):
            table[row, n + i] = value
    for fetch in fetches:
        fetch.wait()


def accumulate(shocks, table, sens, kept, sent, acc):
    half = kept.shape[0]
    block = sens.shape[1]
    acc[...] = jnp.zeros_like(acc)

    def work(g, carry):
        terms = []
        for u in range(UNROLL):
            i = g * UNROLL + u
            both = jnp.concatenate([sens[table[0, i]], sens[table[1, i]]], axis=1)
            terms.append(jnp.dot(shocks[table[4, i]], both, preferred_element_type=jnp.float32))
        for u, term in enumerate(terms):
            i = g * UNROLL + u
            acc[table[2, i]] += term[:, :block]
            acc[table[3, i]] += term[:, block:]
        return carry

    lax.fori_loop(0, (table[5, 0] + UNROLL - 1) // UNROLL, work, 0)
    kept[...] = acc[:half]
    sent[...] = acc[half : 2 * half].astype(sent.dtype)


def shards(returns, vol_hist, vol_now, sensitivity, block_pairs, book_order):
    groups = lax.axis_size("blk")
    own_rows, width = returns.shape
    slots, block, _ = sensitivity.shape
    own = width // groups
    rows = groups * own_rows
    books = book_order.shape[0]
    siblings = [(i, i ^ 1) for i in range(groups)]
    rescaled = (returns.astype(jnp.float32) * vol_now[None, :] / vol_hist).astype(jnp.bfloat16)
    outgoing = rescaled.reshape(own_rows, groups, own).swapaxes(0, 1)
    incoming = lax.all_to_all(outgoing, "blk", 0, 0)
    factors = own // block
    pair_rows = slots // 2 + factors + 2 * UNROLL
    sens, table = pl.pallas_call(
        functools.partial(prepare, groups, factors),
        in_specs=[HBM, HBM, HBM, HBM],
        out_specs=[VMEM, SMEM],
        out_shape=[
            jax.ShapeDtypeStruct(sensitivity.shape, sensitivity.dtype),
            jax.ShapeDtypeStruct((6, pair_rows), jnp.int32),
        ],
        scratch_shapes=[
            pltpu.SMEM((3, slots), jnp.int32),
            pltpu.SMEM((books,), jnp.int32),
            pltpu.SMEM((books + 1,), jnp.int32),
            pltpu.SemaphoreType.DMA((2,)),
            pltpu.SemaphoreType.DMA((CHUNKS,)),
        ],
        compiler_params=pltpu.CompilerParams(vmem_limit_bytes=PREPARE_VMEM),
        cost_estimate=pl.CostEstimate(flops=0, bytes_accessed=4 * slots * block * block, transcendentals=0),
    )(outgoing, block_pairs.T, book_order, sensitivity)
    incoming, sens, table = lax.optimization_barrier((incoming, sens, table))
    shocks = incoming.reshape(rows, factors, block).transpose(1, 0, 2)
    kept, sent = pl.pallas_call(
        accumulate,
        in_specs=[VMEM, SMEM, VMEM],
        out_specs=[VMEM, VMEM],
        out_shape=[
            jax.ShapeDtypeStruct((books // 2, rows, block), jnp.float32),
            jax.ShapeDtypeStruct((books // 2, rows, block), jnp.bfloat16),
        ],
        scratch_shapes=[pltpu.VMEM((books + 1, rows, block), jnp.float32)],
        compiler_params=pltpu.CompilerParams(vmem_limit_bytes=PRODUCT_VMEM),
        cost_estimate=pl.CostEstimate(
            flops=2 * slots * rows * block * block,
            bytes_accessed=2 * slots * block * block,
            transcendentals=0,
        ),
    )(shocks, table, sens)
    across = lax.ppermute(sent, "blk", siblings)
    per_owner = books // groups
    chips = groups // 2
    chip_sum = (kept + across.astype(jnp.float32)).astype(jnp.bfloat16).reshape(chips, per_owner, rows, block)
    same_core = [list(range(c, groups, 2)) for c in range(2)]
    arrived = lax.all_to_all(chip_sum, "blk", 0, 0, axis_index_groups=same_core)
    owned = jnp.sum(arrived.astype(jnp.float32), axis=0)
    profit_loss = owned.transpose(1, 0, 2).reshape(rows, per_owner * block)
    spans = lax.axis_size("scen")
    squares = jnp.sum(owned * owned, axis=1).reshape(-1)
    if spans == 2:
        squares = squares + lax.ppermute(squares, "scen", [(0, 1), (1, 0)])
    else:
        squares = lax.psum(squares, "scen")
    book_rms = jnp.sqrt(squares / (rows * spans) + 1e-06)
    return (profit_loss, book_rms)


def solution(mesh):
    return jax.shard_map(
        shards,
        mesh=mesh,
        in_specs=(
            P(("scen", "blk"), None),
            P(("scen", "blk"), None),
            P(),
            P("blk", None, None),
            P("blk", None),
            P(),
        ),
        out_specs=(P("scen", "blk"), P("blk")),
        check_vma=False,
    )
```

```python
import functools

import jax
import jax.numpy as jnp
from jax import lax
from jax.experimental import pallas as pl
from jax.experimental.pallas import tpu as pltpu
from jax.sharding import PartitionSpec as P

UNROLL = 32
VMEM_LIMIT = 52 * 1024 * 1024
VMEM = pl.BlockSpec(memory_space=pltpu.VMEM)
HBM = pl.BlockSpec(memory_space=pltpu.HBM)


def accumulate(groups, shocks, slots_in, sens_hbm, kept, sent, acc, sens, pairs, position, small, arrived):
    slots = sens.shape[0]
    factors, _, block = shocks.shape
    chunks = arrived.shape[0]
    chunk = slots // chunks
    half = kept.shape[0]
    books = 2 * half
    per_owner = books // groups
    index = lax.axis_index("blk")
    core = index & 1

    def fetch(c):
        span = pl.ds(c * chunk, chunk)
        return pltpu.make_async_copy(sens_hbm.at[span], sens.at[span], arrived.at[c])

    get_pairs = pltpu.make_async_copy(slots_in, pairs, small)
    get_pairs.start()
    for c in range(chunks):
        fetch(c).start()
    acc[...] = jnp.zeros_like(acc)
    get_pairs.wait()
    for p in range(books):
        owner = p // per_owner
        place = (owner // 2) * per_owner + p % per_owner
        position[pairs[3, p]] = place + half * ((owner & 1) ^ core)
    position[books] = books
    first_factor = index * factors

    def work(c, carry):
        fetch(c).wait()

        @pl.when(pairs[2, c * chunk] != 0)
        def _():
            for u in range(chunk):
                k = c * chunk + u
                book = jnp.where(pairs[2, k] != 0, pairs[1, k], books)
                f = pairs[0, k] - first_factor
                acc[position[book]] += jnp.dot(shocks[f], sens[k], preferred_element_type=jnp.float32)

        return carry

    lax.fori_loop(0, chunks, work, 0)
    kept[...] = acc[:half]
    sent[...] = acc[half:books].astype(sent.dtype)


def shards(returns, vol_hist, vol_now, sensitivity, block_pairs, book_order):
    groups = lax.axis_size("blk")
    own_rows, width = returns.shape
    slots, block, _ = sensitivity.shape
    own = width // groups
    rows = groups * own_rows
    books = book_order.shape[0]
    siblings = [(i, i ^ 1) for i in range(groups)]
    rescaled = (returns.astype(jnp.float32) * vol_now[None, :] / vol_hist).astype(jnp.bfloat16)
    outgoing = rescaled.reshape(own_rows, groups, own).swapaxes(0, 1)
    incoming = lax.all_to_all(outgoing, "blk", 0, 0)
    incoming, block_pairs, book_order = lax.optimization_barrier((incoming, block_pairs, book_order))
    shocks = incoming.reshape(rows, own // block, block).transpose(1, 0, 2)
    slots_in = jnp.pad(block_pairs.T, ((0, 1), (0, 0))) + jnp.pad(book_order[None, :], ((3, 0), (0, slots - books)))
    chunks = slots // UNROLL
    kept, sent = pl.pallas_call(
        functools.partial(accumulate, groups),
        in_specs=[VMEM, VMEM, HBM],
        out_specs=[VMEM, VMEM],
        out_shape=[
            jax.ShapeDtypeStruct((books // 2, rows, block), jnp.float32),
            jax.ShapeDtypeStruct((books // 2, rows, block), jnp.bfloat16),
        ],
        scratch_shapes=[
            pltpu.VMEM((books + 1, rows, block), jnp.float32),
            pltpu.VMEM(sensitivity.shape, sensitivity.dtype),
            pltpu.SMEM((4, slots), jnp.int32),
            pltpu.SMEM((books + 1,), jnp.int32),
            pltpu.SemaphoreType.DMA,
            pltpu.SemaphoreType.DMA((chunks,)),
        ],
        compiler_params=pltpu.CompilerParams(vmem_limit_bytes=VMEM_LIMIT),
        cost_estimate=pl.CostEstimate(
            flops=2 * slots * rows * block * block,
            bytes_accessed=2 * slots * block * block,
            transcendentals=0,
        ),
    )(shocks, slots_in, sensitivity)
    across = lax.ppermute(sent, "blk", siblings)
    per_owner = books // groups
    chips = groups // 2
    chip_sum = (kept + across.astype(jnp.float32)).astype(jnp.bfloat16).reshape(chips, per_owner, rows, block)
    same_core = [list(range(c, groups, 2)) for c in range(2)]
    arrived = lax.all_to_all(chip_sum, "blk", 0, 0, axis_index_groups=same_core)
    owned = jnp.sum(arrived.astype(jnp.float32), axis=0)
    profit_loss = owned.transpose(1, 0, 2).reshape(rows, per_owner * block)
    spans = lax.axis_size("scen")
    squares = jnp.sum(owned * owned, axis=1).reshape(-1)
    if spans == 2:
        squares = squares + lax.ppermute(squares, "scen", [(0, 1), (1, 0)])
    else:
        squares = lax.psum(squares, "scen")
    book_rms = jnp.sqrt(squares / (rows * spans) + 1e-06)
    return (profit_loss, book_rms)


def solution(mesh):
    return jax.shard_map(
        shards,
        mesh=mesh,
        in_specs=(
            P(("scen", "blk"), None),
            P(("scen", "blk"), None),
            P(),
            P("blk", None, None),
            P("blk", None),
            P(),
        ),
        out_specs=(P("scen", "blk"), P("blk")),
        check_vma=False,
    )
```

```python
import functools

import jax
import jax.numpy as jnp
from jax import lax
from jax.experimental import pallas as pl
from jax.experimental.pallas import tpu as pltpu
from jax.sharding import PartitionSpec as P

UNROLL = 32
LAG = 6
VMEM_LIMIT = 52 * 1024 * 1024
VMEM = pl.BlockSpec(memory_space=pltpu.VMEM)
HBM = pl.BlockSpec(memory_space=pltpu.HBM)


def accumulate(groups, shocks, slots_in, sens_hbm, kept, sent, acc, sens, pairs, position, small, arrived):
    slots = sens.shape[0]
    factors, _, block = shocks.shape
    chunks = arrived.shape[0]
    chunk = slots // chunks
    half = kept.shape[0]
    books = 2 * half
    per_owner = books // groups
    index = lax.axis_index("blk")
    core = index & 1

    def fetch(c):
        span = pl.ds(c * chunk, chunk)
        return pltpu.make_async_copy(sens_hbm.at[span], sens.at[span], arrived.at[c])

    get_pairs = pltpu.make_async_copy(slots_in, pairs, small)
    get_pairs.start()
    for c in range(chunks):
        fetch(c).start()
    acc[...] = jnp.zeros_like(acc)
    get_pairs.wait()
    for p in range(books):
        owner = p // per_owner
        place = (owner // 2) * per_owner + p % per_owner
        position[pairs[3, p]] = place + half * ((owner & 1) ^ core)
    position[books] = books
    first_factor = index * factors
    none = jnp.zeros(sens.shape[1:], sens.dtype)

    def work(units, c, carry):
        fetch(c).wait()

        @pl.when(pairs[2, c * chunk] != 0)
        def _():
            def stage(i):
                k = c * chunk + 2 * i
                first = jnp.concatenate([sens[k], none], axis=1)
                second = jnp.concatenate([none, sens[k + 1]], axis=1)
                pltpu.matmul_push_rhs(jnp.concatenate([first, second], axis=0), (i // 2) % 2, i % 2)

            def multiply(i):
                k = c * chunk + 2 * i
                scenarios = [shocks[pairs[0, k + t] - first_factor] for t in range(2)]
                lhs = jnp.concatenate(scenarios, axis=1)
                pltpu.matmul_acc_lhs(units[i], lhs, load_staged_rhs=(i // 2) % 2)

            def collect(i):
                both = pltpu.matmul_pop(units[i])
                for t in range(2):
                    k = c * chunk + 2 * i + t
                    book = jnp.where(pairs[2, k] != 0, pairs[1, k], books)
                    acc[position[book]] += both[:, t * block : (t + 1) * block]

            many = chunk // 2
            for i in range(many + LAG):
                if i < many:
                    stage(i)
                if 2 <= i < many + 2:
                    multiply(i - 2)
                if i >= LAG:
                    collect(i - LAG)

        return carry

    def on_units(*units):
        lax.fori_loop(0, chunks, functools.partial(work, units), 0)

    rows = shocks.shape[1]
    pl.run_scoped(on_units, *[pltpu.ACC(i % 2)((rows, 2 * block), jnp.float32) for i in range(chunk // 2)])
    kept[...] = acc[:half]
    sent[...] = acc[half:books].astype(sent.dtype)


def shards(returns, vol_hist, vol_now, sensitivity, block_pairs, book_order):
    groups = lax.axis_size("blk")
    own_rows, width = returns.shape
    slots, block, _ = sensitivity.shape
    own = width // groups
    rows = groups * own_rows
    books = book_order.shape[0]
    siblings = [(i, i ^ 1) for i in range(groups)]
    rescaled = (returns.astype(jnp.float32) * vol_now[None, :] / vol_hist).astype(jnp.bfloat16)
    outgoing = rescaled.reshape(own_rows, groups, own).swapaxes(0, 1)
    incoming = lax.all_to_all(outgoing, "blk", 0, 0)
    incoming, block_pairs, book_order = lax.optimization_barrier((incoming, block_pairs, book_order))
    shocks = incoming.reshape(rows, own // block, block).transpose(1, 0, 2)
    slots_in = jnp.pad(block_pairs.T, ((0, 1), (0, 0))) + jnp.pad(book_order[None, :], ((3, 0), (0, slots - books)))
    chunks = slots // UNROLL
    kept, sent = pl.pallas_call(
        functools.partial(accumulate, groups),
        in_specs=[VMEM, VMEM, HBM],
        out_specs=[VMEM, VMEM],
        out_shape=[
            jax.ShapeDtypeStruct((books // 2, rows, block), jnp.float32),
            jax.ShapeDtypeStruct((books // 2, rows, block), jnp.bfloat16),
        ],
        scratch_shapes=[
            pltpu.VMEM((books + 1, rows, block), jnp.float32),
            pltpu.VMEM(sensitivity.shape, sensitivity.dtype),
            pltpu.SMEM((4, slots), jnp.int32),
            pltpu.SMEM((books + 1,), jnp.int32),
            pltpu.SemaphoreType.DMA,
            pltpu.SemaphoreType.DMA((chunks,)),
        ],
        compiler_params=pltpu.CompilerParams(vmem_limit_bytes=VMEM_LIMIT),
        cost_estimate=pl.CostEstimate(
            flops=2 * slots * rows * block * block,
            bytes_accessed=2 * slots * block * block,
            transcendentals=0,
        ),
    )(shocks, slots_in, sensitivity)
    across = lax.ppermute(sent, "blk", siblings)
    per_owner = books // groups
    chips = groups // 2
    chip_sum = (kept + across.astype(jnp.float32)).astype(jnp.bfloat16).reshape(chips, per_owner, rows, block)
    same_core = [list(range(c, groups, 2)) for c in range(2)]
    arrived = lax.all_to_all(chip_sum, "blk", 0, 0, axis_index_groups=same_core)
    owned = jnp.sum(arrived.astype(jnp.float32), axis=0)
    profit_loss = owned.transpose(1, 0, 2).reshape(rows, per_owner * block)
    spans = lax.axis_size("scen")
    squares = jnp.sum(owned * owned, axis=1).reshape(-1)
    if spans == 2:
        squares = squares + lax.ppermute(squares, "scen", [(0, 1), (1, 0)])
    else:
        squares = lax.psum(squares, "scen")
    book_rms = jnp.sqrt(squares / (rows * spans) + 1e-06)
    return (profit_loss, book_rms)


def solution(mesh):
    def on_mesh(*args):
        with jax.sharding.use_abstract_mesh(mesh.abstract_mesh):
            return whole(*args)

    whole = jax.shard_map(
        shards,
        mesh=mesh,
        in_specs=(
            P(("scen", "blk"), None),
            P(("scen", "blk"), None),
            P(),
            P("blk", None, None),
            P("blk", None),
            P(),
        ),
        out_specs=(P("scen", "blk"), P("blk")),
        check_vma=False,
    )
    return on_mesh
```

```python
import functools

import jax
import jax.numpy as jnp
from jax import lax
from jax.experimental import pallas as pl
from jax.experimental.pallas import tpu as pltpu
from jax.sharding import PartitionSpec as P

UNROLL = 32
LAG = 4
VMEM_LIMIT = 52 * 1024 * 1024
VMEM = pl.BlockSpec(memory_space=pltpu.VMEM)
HBM = pl.BlockSpec(memory_space=pltpu.HBM)


def accumulate(groups, shocks, slots_in, sens_hbm, kept, sent, acc, sens, pairs, position, small, arrived):
    slots = sens.shape[0]
    factors, _, block = shocks.shape
    chunks = arrived.shape[0]
    chunk = slots // chunks
    half = kept.shape[0]
    books = 2 * half
    per_owner = books // groups
    index = lax.axis_index("blk")
    core = index & 1

    def fetch(c):
        span = pl.ds(c * chunk, chunk)
        return pltpu.make_async_copy(sens_hbm.at[span], sens.at[span], arrived.at[c])

    get_pairs = pltpu.make_async_copy(slots_in, pairs, small)
    get_pairs.start()
    for c in range(chunks):
        fetch(c).start()
    acc[...] = jnp.zeros_like(acc)
    get_pairs.wait()
    for p in range(books):
        owner = p // per_owner
        place = (owner // 2) * per_owner + p % per_owner
        position[pairs[3, p]] = place + half * ((owner & 1) ^ core)
    position[books] = books
    first_factor = index * factors
    none = jnp.zeros(shocks.shape[1:], shocks.dtype)

    def work(units, c, carry):
        fetch(c).wait()

        @pl.when(pairs[2, c * chunk] != 0)
        def _():
            def stage(q):
                k = c * chunk + 4 * q
                upper = jnp.concatenate([sens[k], sens[k + 1]], axis=1)
                lower = jnp.concatenate([sens[k + 2], sens[k + 3]], axis=1)
                pltpu.matmul_push_rhs(jnp.concatenate([upper, lower], axis=0), (q // 2) % 2, q % 2)

            def multiply(q):
                for t in range(4):
                    scenarios = shocks[pairs[0, c * chunk + 4 * q + t] - first_factor]
                    halves = [scenarios, none] if t < 2 else [none, scenarios]
                    staged = (q // 2) % 2 if t == 0 else None
                    pltpu.matmul_acc_lhs(units[4 * q + t], jnp.concatenate(halves, axis=1), load_staged_rhs=staged)

            def collect(q):
                for t in range(4):
                    k = c * chunk + 4 * q + t
                    book = jnp.where(pairs[2, k] != 0, pairs[1, k], books)
                    side = (t % 2) * block
                    acc[position[book]] += pltpu.matmul_pop(units[4 * q + t])[:, side : side + block]

            many = chunk // 4
            for q in range(many + LAG):
                if q < many:
                    stage(q)
                if 2 <= q < many + 2:
                    multiply(q - 2)
                if q >= LAG:
                    collect(q - LAG)

        return carry

    def on_units(*units):
        lax.fori_loop(0, chunks, functools.partial(work, units), 0)

    rows = shocks.shape[1]
    pl.run_scoped(on_units, *[pltpu.ACC(k // 4 % 2)((rows, 2 * block), jnp.float32) for k in range(chunk)])
    kept[...] = acc[:half]
    sent[...] = acc[half:books].astype(sent.dtype)


def shards(returns, vol_hist, vol_now, sensitivity, block_pairs, book_order):
    groups = lax.axis_size("blk")
    own_rows, width = returns.shape
    slots, block, _ = sensitivity.shape
    own = width // groups
    rows = groups * own_rows
    books = book_order.shape[0]
    siblings = [(i, i ^ 1) for i in range(groups)]
    rescaled = (returns.astype(jnp.float32) * vol_now[None, :] / vol_hist).astype(jnp.bfloat16)
    outgoing = rescaled.reshape(own_rows, groups, own).swapaxes(0, 1)
    incoming = lax.all_to_all(outgoing, "blk", 0, 0)
    incoming, block_pairs, book_order = lax.optimization_barrier((incoming, block_pairs, book_order))
    shocks = incoming.reshape(rows, own // block, block).transpose(1, 0, 2)
    slots_in = jnp.pad(block_pairs.T, ((0, 1), (0, 0))) + jnp.pad(book_order[None, :], ((3, 0), (0, slots - books)))
    chunks = slots // UNROLL
    kept, sent = pl.pallas_call(
        functools.partial(accumulate, groups),
        in_specs=[VMEM, VMEM, HBM],
        out_specs=[VMEM, VMEM],
        out_shape=[
            jax.ShapeDtypeStruct((books // 2, rows, block), jnp.float32),
            jax.ShapeDtypeStruct((books // 2, rows, block), jnp.bfloat16),
        ],
        scratch_shapes=[
            pltpu.VMEM((books + 1, rows, block), jnp.float32),
            pltpu.VMEM(sensitivity.shape, sensitivity.dtype),
            pltpu.SMEM((4, slots), jnp.int32),
            pltpu.SMEM((books + 1,), jnp.int32),
            pltpu.SemaphoreType.DMA,
            pltpu.SemaphoreType.DMA((chunks,)),
        ],
        compiler_params=pltpu.CompilerParams(vmem_limit_bytes=VMEM_LIMIT),
        cost_estimate=pl.CostEstimate(
            flops=2 * slots * rows * block * block,
            bytes_accessed=2 * slots * block * block,
            transcendentals=0,
        ),
    )(shocks, slots_in, sensitivity)
    across = lax.ppermute(sent, "blk", siblings)
    per_owner = books // groups
    chips = groups // 2
    chip_sum = (kept + across.astype(jnp.float32)).astype(jnp.bfloat16).reshape(chips, per_owner, rows, block)
    same_core = [list(range(c, groups, 2)) for c in range(2)]
    arrived = lax.all_to_all(chip_sum, "blk", 0, 0, axis_index_groups=same_core)
    owned = jnp.sum(arrived.astype(jnp.float32), axis=0)
    profit_loss = owned.transpose(1, 0, 2).reshape(rows, per_owner * block)
    spans = lax.axis_size("scen")
    squares = jnp.sum(owned * owned, axis=1).reshape(-1)
    if spans == 2:
        squares = squares + lax.ppermute(squares, "scen", [(0, 1), (1, 0)])
    else:
        squares = lax.psum(squares, "scen")
    book_rms = jnp.sqrt(squares / (rows * spans) + 1e-06)
    return (profit_loss, book_rms)


def solution(mesh):
    def on_mesh(*args):
        with jax.sharding.use_abstract_mesh(mesh.abstract_mesh):
            return whole(*args)

    whole = jax.shard_map(
        shards,
        mesh=mesh,
        in_specs=(
            P(("scen", "blk"), None),
            P(("scen", "blk"), None),
            P(),
            P("blk", None, None),
            P("blk", None),
            P(),
        ),
        out_specs=(P("scen", "blk"), P("blk")),
        check_vma=False,
    )
    return on_mesh
```

```python
import functools

import jax
import jax.numpy as jnp
from jax import lax
from jax.experimental import pallas as pl
from jax.experimental.pallas import tpu as pltpu
from jax.sharding import PartitionSpec as P

UNROLL = 32
VMEM_LIMIT = 32 * 1024 * 1024
VMEM = pl.BlockSpec(memory_space=pltpu.VMEM)
HBM = pl.BlockSpec(memory_space=pltpu.HBM)


def accumulate(
    groups, shocks, pairs_hbm, order_hbm, sens_hbm, kept, sent, acc, sens, pairs, order, position, small, arrived
):
    slots = sens.shape[0]
    factors, _, block = shocks.shape
    chunks = arrived.shape[0]
    chunk = slots // chunks
    half = kept.shape[0]
    books = 2 * half
    per_owner = books // groups
    index = lax.axis_index("blk")
    core = index & 1

    def fetch(c):
        span = pl.ds(c * chunk, chunk)
        return pltpu.make_async_copy(sens_hbm.at[span], sens.at[span], arrived.at[c])

    get_order = pltpu.make_async_copy(order_hbm, order, small.at[0])
    get_pairs = pltpu.make_async_copy(pairs_hbm, pairs, small.at[1])
    get_order.start()
    get_pairs.start()
    for c in range(chunks):
        fetch(c).start()
    acc[...] = jnp.zeros_like(acc)
    get_order.wait()
    for p in range(books):
        owner = p // per_owner
        place = (owner // 2) * per_owner + p % per_owner
        position[order[p]] = place + half * ((owner & 1) ^ core)
    position[books] = books
    get_pairs.wait()
    first_factor = index * factors

    def work(c, carry):
        fetch(c).wait()

        @pl.when(pairs[2, c * chunk] != 0)
        def _():
            for u in range(chunk):
                k = c * chunk + u
                book = jnp.where(pairs[2, k] != 0, pairs[1, k], books)
                f = pairs[0, k] - first_factor
                acc[position[book]] += jnp.dot(shocks[f], sens[k], preferred_element_type=jnp.float32)

        return carry

    lax.fori_loop(0, chunks, work, 0)
    kept[...] = acc[:half]
    sent[...] = acc[half:books].astype(sent.dtype)


def shards(returns, vol_hist, vol_now, sensitivity, block_pairs, book_order):
    groups = lax.axis_size("blk")
    own_rows, width = returns.shape
    slots, block, _ = sensitivity.shape
    own = width // groups
    rows = groups * own_rows
    books = book_order.shape[0]
    siblings = [(i, i ^ 1) for i in range(groups)]
    rescaled = (returns.astype(jnp.float32) * vol_now[None, :] / vol_hist).astype(jnp.bfloat16)
    outgoing = rescaled.reshape(own_rows, groups, own).swapaxes(0, 1)
    incoming = lax.all_to_all(outgoing, "blk", 0, 0)
    shocks = incoming.reshape(rows, own // block, block).transpose(1, 0, 2)
    chunks = slots // UNROLL
    kept, sent = pl.pallas_call(
        functools.partial(accumulate, groups),
        in_specs=[VMEM, HBM, HBM, HBM],
        out_specs=[VMEM, VMEM],
        out_shape=[
            jax.ShapeDtypeStruct((books // 2, rows, block), jnp.float32),
            jax.ShapeDtypeStruct((books // 2, rows, block), jnp.bfloat16),
        ],
        scratch_shapes=[
            pltpu.VMEM((books + 1, rows, block), jnp.float32),
            pltpu.VMEM(sensitivity.shape, sensitivity.dtype),
            pltpu.SMEM((3, slots), jnp.int32),
            pltpu.SMEM((books,), jnp.int32),
            pltpu.SMEM((books + 1,), jnp.int32),
            pltpu.SemaphoreType.DMA((2,)),
            pltpu.SemaphoreType.DMA((chunks,)),
        ],
        compiler_params=pltpu.CompilerParams(vmem_limit_bytes=VMEM_LIMIT),
        cost_estimate=pl.CostEstimate(
            flops=2 * slots * rows * block * block,
            bytes_accessed=2 * slots * block * block,
            transcendentals=0,
        ),
    )(shocks, *(pltpu.with_memory_space_constraint(x, pltpu.HBM) for x in (block_pairs.T, book_order, sensitivity)))
    across = lax.ppermute(sent, "blk", siblings)
    per_owner = books // groups
    chips = groups // 2
    chip_sum = (kept + across.astype(jnp.float32)).astype(jnp.bfloat16).reshape(chips, per_owner, rows, block)
    same_core = [list(range(c, groups, 2)) for c in range(2)]
    arrived = lax.all_to_all(chip_sum, "blk", 0, 0, axis_index_groups=same_core)
    owned = jnp.sum(arrived.astype(jnp.float32), axis=0)
    profit_loss = owned.transpose(1, 0, 2).reshape(rows, per_owner * block)
    spans = lax.axis_size("scen")
    squares = jnp.sum(owned * owned, axis=1).reshape(-1)
    if spans == 2:
        squares = squares + lax.ppermute(squares, "scen", [(0, 1), (1, 0)])
    else:
        squares = lax.psum(squares, "scen")
    book_rms = jnp.sqrt(squares / (rows * spans) + 1e-06)
    return (profit_loss, book_rms)


def solution(mesh):
    return jax.shard_map(
        shards,
        mesh=mesh,
        in_specs=(
            P(("scen", "blk"), None),
            P(("scen", "blk"), None),
            P(),
            P("blk", None, None),
            P("blk", None),
            P(),
        ),
        out_specs=(P("scen", "blk"), P("blk")),
        check_vma=False,
    )
```

```python
import functools

import jax
import jax.numpy as jnp
from jax import lax
from jax.experimental import pallas as pl
from jax.experimental.pallas import tpu as pltpu
from jax.sharding import PartitionSpec as P

CHUNK = 16
UNROLL = 64
VMEM_LIMIT = 32 * 1024 * 1024
VMEM = pl.BlockSpec(memory_space=pltpu.VMEM)
HBM = pl.BlockSpec(memory_space=pltpu.HBM)


def accumulate(
    groups, shocks, pairs_hbm, order_hbm, sens_hbm, kept, sent, acc, sens, pairs, order, position, small, arrived
):
    slots = sens.shape[0]
    factors, _, block = shocks.shape
    chunks = arrived.shape[0]
    chunk = slots // chunks
    half = kept.shape[0]
    books = 2 * half
    per_owner = books // groups
    index = lax.axis_index("blk")
    core = index & 1

    def fetch(c):
        span = pl.ds(c * chunk, chunk)
        return pltpu.make_async_copy(sens_hbm.at[span], sens.at[span], arrived.at[c])

    get_order = pltpu.make_async_copy(order_hbm, order, small.at[0])
    get_pairs = pltpu.make_async_copy(pairs_hbm, pairs, small.at[1])
    get_order.start()
    get_pairs.start()
    for c in range(chunks):
        fetch(c).start()
    acc[...] = jnp.zeros_like(acc)
    get_order.wait()
    for p in range(books):
        owner = p // per_owner
        place = (owner // 2) * per_owner + p % per_owner
        position[order[p]] = place + half * ((owner & 1) ^ core)
    position[books] = books
    get_pairs.wait()
    first_factor = index * factors

    def work(g, carry):
        @pl.when(pairs[2, g * UNROLL] != 0)
        def _():
            for u in range(UNROLL):
                if u % chunk == 0:
                    fetch(g * (UNROLL // chunk) + u // chunk).wait()
                k = g * UNROLL + u
                book = jnp.where(pairs[2, k] != 0, pairs[1, k], books)
                f = pairs[0, k] - first_factor
                acc[position[book]] += jnp.dot(shocks[f], sens[k], preferred_element_type=jnp.float32)

        @pl.when(pairs[2, g * UNROLL] == 0)
        def _():
            for c in range(UNROLL // chunk):
                fetch(g * (UNROLL // chunk) + c).wait()

        return carry

    lax.fori_loop(0, slots // UNROLL, work, 0)
    kept[...] = acc[:half]
    sent[...] = acc[half:books].astype(sent.dtype)


def shards(returns, vol_hist, vol_now, sensitivity, block_pairs, book_order):
    groups = lax.axis_size("blk")
    own_rows, width = returns.shape
    slots, block, _ = sensitivity.shape
    own = width // groups
    rows = groups * own_rows
    books = book_order.shape[0]
    siblings = [(i, i ^ 1) for i in range(groups)]
    rescaled = (returns.astype(jnp.float32) * vol_now[None, :] / vol_hist).astype(jnp.bfloat16)
    outgoing = rescaled.reshape(own_rows, groups, own).swapaxes(0, 1)
    incoming = lax.all_to_all(outgoing, "blk", 0, 0)
    shocks = incoming.reshape(rows, own // block, block).transpose(1, 0, 2)
    chunks = slots // CHUNK
    kept, sent = pl.pallas_call(
        functools.partial(accumulate, groups),
        in_specs=[VMEM, HBM, HBM, HBM],
        out_specs=[VMEM, VMEM],
        out_shape=[
            jax.ShapeDtypeStruct((books // 2, rows, block), jnp.float32),
            jax.ShapeDtypeStruct((books // 2, rows, block), jnp.bfloat16),
        ],
        scratch_shapes=[
            pltpu.VMEM((books + 1, rows, block), jnp.float32),
            pltpu.VMEM(sensitivity.shape, sensitivity.dtype),
            pltpu.SMEM((3, slots), jnp.int32),
            pltpu.SMEM((books,), jnp.int32),
            pltpu.SMEM((books + 1,), jnp.int32),
            pltpu.SemaphoreType.DMA((2,)),
            pltpu.SemaphoreType.DMA((chunks,)),
        ],
        compiler_params=pltpu.CompilerParams(vmem_limit_bytes=VMEM_LIMIT),
        cost_estimate=pl.CostEstimate(
            flops=2 * slots * rows * block * block,
            bytes_accessed=2 * slots * block * block,
            transcendentals=0,
        ),
    )(shocks, *(pltpu.with_memory_space_constraint(x, pltpu.HBM) for x in (block_pairs.T, book_order, sensitivity)))
    across = lax.ppermute(sent, "blk", siblings)
    per_owner = books // groups
    chips = groups // 2
    chip_sum = (kept + across.astype(jnp.float32)).astype(jnp.bfloat16).reshape(chips, per_owner, rows, block)
    same_core = [list(range(c, groups, 2)) for c in range(2)]
    arrived = lax.all_to_all(chip_sum, "blk", 0, 0, axis_index_groups=same_core)
    owned = jnp.sum(arrived.astype(jnp.float32), axis=0)
    profit_loss = owned.transpose(1, 0, 2).reshape(rows, per_owner * block)
    spans = lax.axis_size("scen")
    squares = jnp.sum(owned * owned, axis=1).reshape(-1)
    if spans == 2:
        squares = squares + lax.ppermute(squares, "scen", [(0, 1), (1, 0)])
    else:
        squares = lax.psum(squares, "scen")
    book_rms = jnp.sqrt(squares / (rows * spans) + 1e-06)
    return (profit_loss, book_rms)


def solution(mesh):
    return jax.shard_map(
        shards,
        mesh=mesh,
        in_specs=(
            P(("scen", "blk"), None),
            P(("scen", "blk"), None),
            P(),
            P("blk", None, None),
            P("blk", None),
            P(),
        ),
        out_specs=(P("scen", "blk"), P("blk")),
        check_vma=False,
    )
```

```python
import functools

import jax
import jax.numpy as jnp
from jax import lax
from jax.experimental import pallas as pl
from jax.experimental.pallas import tpu as pltpu
from jax.sharding import PartitionSpec as P

UNROLL = 128
VMEM_LIMIT = 16 * 1024 * 1024
VMEM = pl.BlockSpec(memory_space=pltpu.VMEM)
HBM = pl.BlockSpec(memory_space=pltpu.HBM)


def accumulate(
    groups, shocks, pairs_hbm, order_hbm, sens, kept, sent, acc, pairs, order, position, small
):
    slots = sens.shape[0]
    factors, _, block = shocks.shape
    chunk = UNROLL
    chunks = slots // chunk
    half = kept.shape[0]
    books = 2 * half
    per_owner = books // groups
    index = lax.axis_index("blk")
    core = index & 1

    get_order = pltpu.make_async_copy(order_hbm, order, small.at[0])
    get_pairs = pltpu.make_async_copy(pairs_hbm, pairs, small.at[1])
    get_order.start()
    get_pairs.start()
    acc[...] = jnp.zeros_like(acc)
    get_order.wait()
    for p in range(books):
        owner = p // per_owner
        place = (owner // 2) * per_owner + p % per_owner
        position[order[p]] = place + half * ((owner & 1) ^ core)
    position[books] = books
    get_pairs.wait()
    first_factor = index * factors

    def work(c, carry):
        @pl.when(pairs[2, c * chunk] != 0)
        def _():
            for u in range(chunk):
                k = c * chunk + u
                book = jnp.where(pairs[2, k] != 0, pairs[1, k], books)
                f = pairs[0, k] - first_factor
                acc[position[book]] += jnp.dot(shocks[f], sens[k], preferred_element_type=jnp.float32)

        return carry

    lax.fori_loop(0, chunks, work, 0)
    kept[...] = acc[:half]
    sent[...] = acc[half:books].astype(sent.dtype)


def shards(returns, vol_hist, vol_now, sensitivity, block_pairs, book_order):
    groups = lax.axis_size("blk")
    own_rows, width = returns.shape
    slots, block, _ = sensitivity.shape
    own = width // groups
    rows = groups * own_rows
    books = book_order.shape[0]
    siblings = [(i, i ^ 1) for i in range(groups)]
    rescaled = (returns.astype(jnp.float32) * vol_now[None, :] / vol_hist).astype(jnp.bfloat16)
    sensitivity = lax.ppermute(sensitivity, "blk", [(i, i) for i in range(groups)])
    outgoing = rescaled.reshape(own_rows, groups, own).swapaxes(0, 1)
    incoming = lax.all_to_all(outgoing, "blk", 0, 0)
    shocks = incoming.reshape(rows, own // block, block).transpose(1, 0, 2)
    kept, sent = pl.pallas_call(
        functools.partial(accumulate, groups),
        in_specs=[VMEM, HBM, HBM, VMEM],
        out_specs=[VMEM, VMEM],
        out_shape=[
            jax.ShapeDtypeStruct((books // 2, rows, block), jnp.float32),
            jax.ShapeDtypeStruct((books // 2, rows, block), jnp.bfloat16),
        ],
        scratch_shapes=[
            pltpu.VMEM((books + 1, rows, block), jnp.float32),
            pltpu.SMEM((3, slots), jnp.int32),
            pltpu.SMEM((books,), jnp.int32),
            pltpu.SMEM((books + 1,), jnp.int32),
            pltpu.SemaphoreType.DMA((2,)),
        ],
        compiler_params=pltpu.CompilerParams(vmem_limit_bytes=VMEM_LIMIT),
        cost_estimate=pl.CostEstimate(
            flops=2 * slots * rows * block * block,
            bytes_accessed=2 * slots * block * block,
            transcendentals=0,
        ),
    )(shocks, *(pltpu.with_memory_space_constraint(x, pltpu.HBM) for x in (block_pairs.T, book_order)), pltpu.with_memory_space_constraint(sensitivity, pltpu.VMEM))
    across = lax.ppermute(sent, "blk", siblings)
    per_owner = books // groups
    chips = groups // 2
    chip_sum = (kept + across.astype(jnp.float32)).astype(jnp.bfloat16).reshape(chips, per_owner, rows, block)
    same_core = [list(range(c, groups, 2)) for c in range(2)]
    arrived = lax.all_to_all(chip_sum, "blk", 0, 0, axis_index_groups=same_core)
    owned = jnp.sum(arrived.astype(jnp.float32), axis=0)
    profit_loss = owned.transpose(1, 0, 2).reshape(rows, per_owner * block)
    spans = lax.axis_size("scen")
    squares = jnp.sum(owned * owned, axis=1).reshape(-1)
    if spans == 2:
        squares = squares + lax.ppermute(squares, "scen", [(0, 1), (1, 0)])
    else:
        squares = lax.psum(squares, "scen")
    book_rms = jnp.sqrt(squares / (rows * spans) + 1e-06)
    return (profit_loss, book_rms)


def solution(mesh):
    return jax.shard_map(
        shards,
        mesh=mesh,
        in_specs=(
            P(("scen", "blk"), None),
            P(("scen", "blk"), None),
            P(),
            P("blk", None, None),
            P("blk", None),
            P(),
        ),
        out_specs=(P("scen", "blk"), P("blk")),
        check_vma=False,
    )
```

```python
import functools

import jax
import jax.numpy as jnp
from jax import lax
from jax.experimental import pallas as pl
from jax.experimental.pallas import tpu as pltpu
from jax.sharding import PartitionSpec as P

UNROLL = 16
VMEM_LIMIT = 32 * 1024 * 1024
VMEM = pl.BlockSpec(memory_space=pltpu.VMEM)
HBM = pl.BlockSpec(memory_space=pltpu.HBM)


def accumulate(
    groups, shocks, pairs_hbm, order_hbm, sens_hbm, kept, sent, acc, sens, pairs, order, position, small, arrived
):
    slots = sens_hbm.shape[0]
    factors = shocks.shape[0]
    chunks = arrived.shape[0]
    chunk = slots // chunks
    half = kept.shape[0]
    books = 2 * half
    per_owner = books // groups
    index = lax.axis_index("blk")
    core = index & 1

    def fetch(c):
        span = pl.ds(c * chunk, chunk)
        return pltpu.make_async_copy(sens_hbm.at[span], sens.at[span], arrived.at[c])

    span = pl.ds(0, slots)
    get_order = pltpu.make_async_copy(order_hbm, order, small.at[0])
    get_pairs = pltpu.make_async_copy(pairs_hbm, pairs.at[:, span], small.at[1])
    get_order.start()
    get_pairs.start()
    for c in range(chunks):
        fetch(c).start()
    first_factor = index * factors
    for u in range(chunk):
        pairs[0, slots + u] = first_factor
        pairs[1, slots + u] = 0
        pairs[2, slots + u] = 0
    position[books] = books
    sens[pl.ds(slots, chunk)] = jnp.zeros((chunk,) + sens.shape[1:], sens.dtype)
    acc[...] = jnp.zeros_like(acc)

    def work(step, carry):
        c = jnp.where(step == 0, chunks, step - 1)

        @pl.when(step == 1)
        def _():
            get_order.wait()
            for p in range(books):
                owner = p // per_owner
                place = (owner // 2) * per_owner + p % per_owner
                position[order[p]] = place + half * ((owner & 1) ^ core)
            get_pairs.wait()

        @pl.when(step > 0)
        def _():
            fetch(step - 1).wait()

        @pl.when((step == 0) | (pairs[2, c * chunk] != 0))
        def _():
            for u in range(chunk):
                k = c * chunk + u
                book = jnp.where(pairs[2, k] != 0, pairs[1, k], books)
                f = pairs[0, k] - first_factor
                acc[position[book]] += jnp.dot(shocks[f], sens[k], preferred_element_type=jnp.float32)

        return carry

    lax.fori_loop(0, chunks + 1, work, 0)
    kept[...] = acc[:half]
    sent[...] = acc[half:books].astype(sent.dtype)


def shards(returns, vol_hist, vol_now, sensitivity, block_pairs, book_order):
    groups = lax.axis_size("blk")
    own_rows, width = returns.shape
    slots, block, _ = sensitivity.shape
    own = width // groups
    rows = groups * own_rows
    books = book_order.shape[0]
    siblings = [(i, i ^ 1) for i in range(groups)]
    rescaled = (returns.astype(jnp.float32) * vol_now[None, :] / vol_hist).astype(jnp.bfloat16)
    outgoing = rescaled.reshape(own_rows, groups, own).swapaxes(0, 1)
    incoming = lax.all_to_all(outgoing, "blk", 0, 0)
    shocks = incoming.reshape(rows, own // block, block).transpose(1, 0, 2)
    chunks = slots // UNROLL
    kept, sent = pl.pallas_call(
        functools.partial(accumulate, groups),
        in_specs=[VMEM, HBM, HBM, HBM],
        out_specs=[VMEM, VMEM],
        out_shape=[
            jax.ShapeDtypeStruct((books // 2, rows, block), jnp.float32),
            jax.ShapeDtypeStruct((books // 2, rows, block), jnp.bfloat16),
        ],
        scratch_shapes=[
            pltpu.VMEM((books + 1, rows, block), jnp.float32),
            pltpu.VMEM((slots + UNROLL, block, block), sensitivity.dtype),
            pltpu.SMEM((3, slots + UNROLL), jnp.int32),
            pltpu.SMEM((books,), jnp.int32),
            pltpu.SMEM((books + 1,), jnp.int32),
            pltpu.SemaphoreType.DMA((2,)),
            pltpu.SemaphoreType.DMA((chunks,)),
        ],
        compiler_params=pltpu.CompilerParams(vmem_limit_bytes=VMEM_LIMIT),
        cost_estimate=pl.CostEstimate(
            flops=2 * slots * rows * block * block,
            bytes_accessed=2 * slots * block * block,
            transcendentals=0,
        ),
    )(shocks, *(pltpu.with_memory_space_constraint(x, pltpu.HBM) for x in (block_pairs.T, book_order, sensitivity)))
    across = lax.ppermute(sent, "blk", siblings)
    per_owner = books // groups
    chips = groups // 2
    chip_sum = (kept + across.astype(jnp.float32)).astype(jnp.bfloat16).reshape(chips, per_owner, rows, block)
    same_core = [list(range(c, groups, 2)) for c in range(2)]
    arrived = lax.all_to_all(chip_sum, "blk", 0, 0, axis_index_groups=same_core)
    owned = jnp.sum(arrived.astype(jnp.float32), axis=0)
    profit_loss = owned.transpose(1, 0, 2).reshape(rows, per_owner * block)
    spans = lax.axis_size("scen")
    squares = jnp.sum(owned * owned, axis=1).reshape(-1)
    if spans == 2:
        squares = squares + lax.ppermute(squares, "scen", [(0, 1), (1, 0)])
    else:
        squares = lax.psum(squares, "scen")
    book_rms = jnp.sqrt(squares / (rows * spans) + 1e-06)
    return (profit_loss, book_rms)


def solution(mesh):
    return jax.shard_map(
        shards,
        mesh=mesh,
        in_specs=(
            P(("scen", "blk"), None),
            P(("scen", "blk"), None),
            P(),
            P("blk", None, None),
            P("blk", None),
            P(),
        ),
        out_specs=(P("scen", "blk"), P("blk")),
        check_vma=False,
    )
```

```python
import functools

import jax
import jax.numpy as jnp
from jax import lax
from jax.experimental import pallas as pl
from jax.experimental.pallas import tpu as pltpu
from jax.sharding import PartitionSpec as P

UNROLL = 32
VMEM_LIMIT = 32 * 1024 * 1024
VMEM = pl.BlockSpec(memory_space=pltpu.VMEM)
HBM = pl.BlockSpec(memory_space=pltpu.HBM)


def accumulate(
    groups, shocks, pairs_hbm, order_hbm, sens_hbm, kept, sent, acc, sens, pairs, order, position, small, arrived
):
    slots = sens.shape[0]
    factors = shocks.shape[0]
    chunks = arrived.shape[0]
    chunk = slots // chunks
    half = kept.shape[0]
    books = 2 * half
    per_owner = books // groups
    index = lax.axis_index("blk")
    core = index & 1

    def fetch(c):
        span = pl.ds(c * chunk, chunk)
        return pltpu.make_async_copy(sens_hbm.at[span], sens.at[span], arrived.at[c])

    get_order = pltpu.make_async_copy(order_hbm, order, small.at[0])
    get_pairs = pltpu.make_async_copy(pairs_hbm, pairs.at[:, pl.ds(0, slots)], small.at[1])
    get_order.start()
    get_pairs.start()
    for c in range(chunks):
        fetch(c).start()
    acc[...] = jnp.zeros_like(acc)
    get_order.wait()
    for p in range(books):
        owner = p // per_owner
        place = (owner // 2) * per_owner + p % per_owner
        position[order[p]] = place + half * ((owner & 1) ^ core)
    position[books] = books
    first_factor = index * factors
    get_pairs.wait()
    for u in range(chunk):
        pairs[0, slots + u] = first_factor
        pairs[1, slots + u] = 0
        pairs[2, slots + u] = 0
    padding = chunks
    quads = chunk // 4
    rows, block = shocks.shape[1:]
    none = jnp.zeros((rows, block), shocks.dtype)

    def count(c, busy):
        return busy + jnp.where(pairs[2, c * chunk] != 0, 1, 0)

    busy = lax.fori_loop(0, chunks, count, 0)

    def on_units(*units):
        def push(q, rhs):
            pltpu.matmul_push_rhs(rhs, (q // 2) % 2, q % 2)

        def stage(c, q):
            k = c * chunk + 4 * q
            upper = jnp.concatenate([sens[k], sens[k + 1]], axis=1)
            lower = jnp.concatenate([sens[k + 2], sens[k + 3]], axis=1)
            push(q, jnp.concatenate([upper, lower], axis=0))

        def multiply(c, q):
            for t in range(4):
                scenarios = shocks[pairs[0, c * chunk + 4 * q + t] - first_factor]
                halves = [scenarios, none] if t < 2 else [none, scenarios]
                staged = (q // 2) % 2 if t == 0 else None
                pltpu.matmul_acc_lhs(units[4 * q + t], jnp.concatenate(halves, axis=1), load_staged_rhs=staged)

        def collect(c, q):
            for t in range(4):
                k = c * chunk + 4 * q + t
                book = jnp.where(pairs[2, k] != 0, pairs[1, k], books)
                side = (t % 2) * block
                acc[position[book]] += pltpu.matmul_pop(units[4 * q + t])[:, side : side + block]

        zeros = jnp.zeros((2 * block, 2 * block), sens.dtype)
        for q in range(quads - 4, quads):
            push(q, zeros)
            if q < quads - 2:
                multiply(padding, q)

        def work(c, carry):
            fetch(c).wait()
            before = jnp.where(c == 0, padding, c - 1)
            for q in range(quads):
                stage(c, q)
                multiply(*((before, q - 2 + quads) if q < 2 else (c, q - 2)))
                collect(*((before, q - 4 + quads) if q < 4 else (c, q - 4)))
            return carry

        lax.fori_loop(0, busy, work, 0)
        last = jnp.where(busy == 0, padding, busy - 1)
        for q in range(quads - 4, quads):
            if q >= quads - 2:
                multiply(last, q)
        for q in range(quads - 4, quads):
            collect(last, q)

    pl.run_scoped(on_units, *[pltpu.ACC(k // 4 % 2)((rows, 2 * block), jnp.float32) for k in range(chunk)])

    def drop(c, carry):
        fetch(c).wait()
        return carry

    lax.fori_loop(busy, chunks, drop, 0)
    kept[...] = acc[:half]
    sent[...] = acc[half:books].astype(sent.dtype)


def shards(returns, vol_hist, vol_now, sensitivity, block_pairs, book_order):
    groups = lax.axis_size("blk")
    own_rows, width = returns.shape
    slots, block, _ = sensitivity.shape
    own = width // groups
    rows = groups * own_rows
    books = book_order.shape[0]
    siblings = [(i, i ^ 1) for i in range(groups)]
    rescaled = (returns.astype(jnp.float32) * vol_now[None, :] / vol_hist).astype(jnp.bfloat16)
    outgoing = rescaled.reshape(own_rows, groups, own).swapaxes(0, 1)
    incoming = lax.all_to_all(outgoing, "blk", 0, 0)
    shocks = incoming.reshape(rows, own // block, block).transpose(1, 0, 2)
    chunks = slots // UNROLL
    kept, sent = pl.pallas_call(
        functools.partial(accumulate, groups),
        in_specs=[VMEM, HBM, HBM, HBM],
        out_specs=[VMEM, VMEM],
        out_shape=[
            jax.ShapeDtypeStruct((books // 2, rows, block), jnp.float32),
            jax.ShapeDtypeStruct((books // 2, rows, block), jnp.bfloat16),
        ],
        scratch_shapes=[
            pltpu.VMEM((books + 1, rows, block), jnp.float32),
            pltpu.VMEM(sensitivity.shape, sensitivity.dtype),
            pltpu.SMEM((3, slots + UNROLL), jnp.int32),
            pltpu.SMEM((books,), jnp.int32),
            pltpu.SMEM((books + 1,), jnp.int32),
            pltpu.SemaphoreType.DMA((2,)),
            pltpu.SemaphoreType.DMA((chunks,)),
        ],
        compiler_params=pltpu.CompilerParams(vmem_limit_bytes=VMEM_LIMIT),
        cost_estimate=pl.CostEstimate(
            flops=2 * slots * rows * block * block,
            bytes_accessed=2 * slots * block * block,
            transcendentals=0,
        ),
    )(shocks, *(pltpu.with_memory_space_constraint(x, pltpu.HBM) for x in (block_pairs.T, book_order, sensitivity)))
    across = lax.ppermute(sent, "blk", siblings)
    per_owner = books // groups
    chips = groups // 2
    chip_sum = (kept + across.astype(jnp.float32)).astype(jnp.bfloat16).reshape(chips, per_owner, rows, block)
    same_core = [list(range(c, groups, 2)) for c in range(2)]
    arrived = lax.all_to_all(chip_sum, "blk", 0, 0, axis_index_groups=same_core)
    owned = jnp.sum(arrived.astype(jnp.float32), axis=0)
    profit_loss = owned.transpose(1, 0, 2).reshape(rows, per_owner * block)
    spans = lax.axis_size("scen")
    squares = jnp.sum(owned * owned, axis=1).reshape(-1)
    if spans == 2:
        squares = squares + lax.ppermute(squares, "scen", [(0, 1), (1, 0)])
    else:
        squares = lax.psum(squares, "scen")
    book_rms = jnp.sqrt(squares / (rows * spans) + 1e-06)
    return (profit_loss, book_rms)


def solution(mesh):
    def on_mesh(*args):
        with jax.sharding.use_abstract_mesh(mesh.abstract_mesh):
            return whole(*args)

    whole = jax.shard_map(
        shards,
        mesh=mesh,
        in_specs=(
            P(("scen", "blk"), None),
            P(("scen", "blk"), None),
            P(),
            P("blk", None, None),
            P("blk", None),
            P(),
        ),
        out_specs=(P("scen", "blk"), P("blk")),
        check_vma=False,
    )
    return on_mesh
```

```python
import functools

import jax
import jax.numpy as jnp
from jax import lax
from jax.experimental import pallas as pl
from jax.experimental.pallas import tpu as pltpu
from jax.sharding import PartitionSpec as P

UNROLL = 32
SIZES = (4, 2, 2, 4, 2, 2)
LAG = 6
VMEM_LIMIT = 32 * 1024 * 1024
VMEM = pl.BlockSpec(memory_space=pltpu.VMEM)
HBM = pl.BlockSpec(memory_space=pltpu.HBM)


def accumulate(
    groups, shocks, pairs_hbm, order_hbm, sens_hbm, kept, sent, acc, sens, pairs, order, position, small, arrived
):
    slots = sens.shape[0]
    factors = shocks.shape[0]
    chunks = arrived.shape[0]
    chunk = slots // chunks
    half = kept.shape[0]
    books = 2 * half
    per_owner = books // groups
    index = lax.axis_index("blk")
    core = index & 1

    def fetch(c):
        span = pl.ds(c * chunk, chunk)
        return pltpu.make_async_copy(sens_hbm.at[span], sens.at[span], arrived.at[c])

    get_order = pltpu.make_async_copy(order_hbm, order, small.at[0])
    get_pairs = pltpu.make_async_copy(pairs_hbm, pairs.at[:, pl.ds(0, slots)], small.at[1])
    get_order.start()
    get_pairs.start()
    for c in range(chunks):
        fetch(c).start()
    acc[...] = jnp.zeros_like(acc)
    get_order.wait()
    for p in range(books):
        owner = p // per_owner
        place = (owner // 2) * per_owner + p % per_owner
        position[order[p]] = place + half * ((owner & 1) ^ core)
    position[books] = books
    first_factor = index * factors
    get_pairs.wait()
    for u in range(chunk):
        pairs[0, slots + u] = first_factor
        pairs[1, slots + u] = 0
        pairs[2, slots + u] = 0
    padding = chunks
    rows, block = shocks.shape[1:]
    none = jnp.zeros((rows, block), shocks.dtype)
    blank = jnp.zeros((block, block), sens.dtype)

    packs = []
    for j, size in enumerate(SIZES):
        for unit in range(2):
            first = unit * (chunk // 2) + sum(SIZES[:j])
            packs.append((first, size, unit, j % 2))
    many = len(packs)

    def count(c, busy):
        return busy + jnp.where(pairs[2, c * chunk] != 0, 1, 0)

    busy = lax.fori_loop(0, chunks, count, 0)

    def on_units(*units):
        def push(i, rhs):
            _, _, unit, staged = packs[i]
            pltpu.matmul_push_rhs(rhs, staged, unit)

        def stage(c, i):
            k = c * chunk + packs[i][0]
            if packs[i][1] == 4:
                tiles = [[sens[k], sens[k + 1]], [sens[k + 2], sens[k + 3]]]
            else:
                tiles = [[sens[k], blank], [blank, sens[k + 1]]]
            push(i, jnp.concatenate([jnp.concatenate(row, axis=1) for row in tiles], axis=0))

        def multiply(c, i):
            first, size, _, staged = packs[i]
            scenarios = [shocks[pairs[0, c * chunk + first + t] - first_factor] for t in range(size)]
            if size == 4:
                passes = [[x, none] if t < 2 else [none, x] for t, x in enumerate(scenarios)]
            else:
                passes = [scenarios]
            for t, halves in enumerate(passes):
                target = units[spot[i] + t]
                pltpu.matmul_acc_lhs(target, jnp.concatenate(halves, axis=1), load_staged_rhs=None if t else staged)

        def collect(c, i):
            first, size, _, _ = packs[i]
            popped = [pltpu.matmul_pop(units[spot[i] + t]) for t in range(4 if size == 4 else 1)]
            for t in range(size):
                k = c * chunk + first + t
                book = jnp.where(pairs[2, k] != 0, pairs[1, k], books)
                side = (t % 2) * block
                acc[position[book]] += popped[t if size == 4 else 0][:, side : side + block]

        zeros = jnp.zeros((2 * block, 2 * block), sens.dtype)
        for i in range(many - LAG, many):
            push(i, zeros)
            if i < many - 2:
                multiply(padding, i)

        def work(c, carry):
            fetch(c).wait()
            before = jnp.where(c == 0, padding, c - 1)
            for i in range(many):
                stage(c, i)
                multiply(*((before, i - 2 + many) if i < 2 else (c, i - 2)))
                collect(*((before, i - LAG + many) if i < LAG else (c, i - LAG)))
            return carry

        lax.fori_loop(0, busy, work, 0)
        last = jnp.where(busy == 0, padding, busy - 1)
        for i in range(many - 2, many):
            multiply(last, i)
        for i in range(many - LAG, many):
            collect(last, i)

    spot = []
    held = []
    for _, size, unit, _ in packs:
        spot.append(len(held))
        held += [pltpu.ACC(unit)((rows, 2 * block), jnp.float32)] * (4 if size == 4 else 1)
    pl.run_scoped(on_units, *held)

    def drop(c, carry):
        fetch(c).wait()
        return carry

    lax.fori_loop(busy, chunks, drop, 0)
    kept[...] = acc[:half]
    sent[...] = acc[half:books].astype(sent.dtype)


def shards(returns, vol_hist, vol_now, sensitivity, block_pairs, book_order):
    groups = lax.axis_size("blk")
    own_rows, width = returns.shape
    slots, block, _ = sensitivity.shape
    own = width // groups
    rows = groups * own_rows
    books = book_order.shape[0]
    siblings = [(i, i ^ 1) for i in range(groups)]
    rescaled = (returns.astype(jnp.float32) * vol_now[None, :] / vol_hist).astype(jnp.bfloat16)
    outgoing = rescaled.reshape(own_rows, groups, own).swapaxes(0, 1)
    incoming = lax.all_to_all(outgoing, "blk", 0, 0)
    shocks = incoming.reshape(rows, own // block, block).transpose(1, 0, 2)
    chunks = slots // UNROLL
    kept, sent = pl.pallas_call(
        functools.partial(accumulate, groups),
        in_specs=[VMEM, HBM, HBM, HBM],
        out_specs=[VMEM, VMEM],
        out_shape=[
            jax.ShapeDtypeStruct((books // 2, rows, block), jnp.float32),
            jax.ShapeDtypeStruct((books // 2, rows, block), jnp.bfloat16),
        ],
        scratch_shapes=[
            pltpu.VMEM((books + 1, rows, block), jnp.float32),
            pltpu.VMEM(sensitivity.shape, sensitivity.dtype),
            pltpu.SMEM((3, slots + UNROLL), jnp.int32),
            pltpu.SMEM((books,), jnp.int32),
            pltpu.SMEM((books + 1,), jnp.int32),
            pltpu.SemaphoreType.DMA((2,)),
            pltpu.SemaphoreType.DMA((chunks,)),
        ],
        compiler_params=pltpu.CompilerParams(vmem_limit_bytes=VMEM_LIMIT),
        cost_estimate=pl.CostEstimate(
            flops=2 * slots * rows * block * block,
            bytes_accessed=2 * slots * block * block,
            transcendentals=0,
        ),
    )(shocks, *(pltpu.with_memory_space_constraint(x, pltpu.HBM) for x in (block_pairs.T, book_order, sensitivity)))
    across = lax.ppermute(sent, "blk", siblings)
    per_owner = books // groups
    chips = groups // 2
    chip_sum = (kept + across.astype(jnp.float32)).astype(jnp.bfloat16).reshape(chips, per_owner, rows, block)
    same_core = [list(range(c, groups, 2)) for c in range(2)]
    arrived = lax.all_to_all(chip_sum, "blk", 0, 0, axis_index_groups=same_core)
    owned = jnp.sum(arrived.astype(jnp.float32), axis=0)
    profit_loss = owned.transpose(1, 0, 2).reshape(rows, per_owner * block)
    spans = lax.axis_size("scen")
    squares = jnp.sum(owned * owned, axis=1).reshape(-1)
    if spans == 2:
        squares = squares + lax.ppermute(squares, "scen", [(0, 1), (1, 0)])
    else:
        squares = lax.psum(squares, "scen")
    book_rms = jnp.sqrt(squares / (rows * spans) + 1e-06)
    return (profit_loss, book_rms)


def solution(mesh):
    def on_mesh(*args):
        with jax.sharding.use_abstract_mesh(mesh.abstract_mesh):
            return whole(*args)

    whole = jax.shard_map(
        shards,
        mesh=mesh,
        in_specs=(
            P(("scen", "blk"), None),
            P(("scen", "blk"), None),
            P(),
            P("blk", None, None),
            P("blk", None),
            P(),
        ),
        out_specs=(P("scen", "blk"), P("blk")),
        check_vma=False,
    )
    return on_mesh
```

```python
import functools

import jax
import jax.numpy as jnp
from jax import lax
from jax.experimental import pallas as pl
from jax.experimental.pallas import tpu as pltpu
from jax.sharding import PartitionSpec as P

UNROLL = 32
SIZES = (4, 2, 2, 4, 2, 2)
LAG = 6
VMEM_LIMIT = 32 * 1024 * 1024
VMEM = pl.BlockSpec(memory_space=pltpu.VMEM)
HBM = pl.BlockSpec(memory_space=pltpu.HBM)


def accumulate(
    groups, shocks, pairs_hbm, order_hbm, sens_hbm, kept, sent, acc, sens, pairs, order, position, small, arrived
):
    slots = sens.shape[0]
    factors = shocks.shape[0]
    chunks = arrived.shape[0]
    chunk = slots // chunks
    half = kept.shape[0]
    books = 2 * half
    per_owner = books // groups
    index = lax.axis_index("blk")
    core = index & 1

    def fetch(c):
        span = pl.ds(c * chunk, chunk)
        return pltpu.make_async_copy(sens_hbm.at[span], sens.at[span], arrived.at[c])

    get_order = pltpu.make_async_copy(order_hbm, order, small.at[0])
    get_pairs = pltpu.make_async_copy(pairs_hbm, pairs.at[:, pl.ds(0, slots)], small.at[1])
    get_order.start()
    get_pairs.start()
    for c in range(chunks):
        fetch(c).start()
    acc[...] = jnp.zeros_like(acc)
    position[books] = books
    first_factor = index * factors
    for u in range(chunk):
        pairs[0, slots + u] = first_factor
        pairs[1, slots + u] = 0
        pairs[2, slots + u] = 0
    padding = chunks
    rows, block = shocks.shape[1:]
    none = jnp.zeros((rows, block), shocks.dtype)
    blank = jnp.zeros((block, block), sens.dtype)

    packs = []
    for j, size in enumerate(SIZES):
        for unit in range(2):
            first = unit * (chunk // 2) + sum(SIZES[:j])
            packs.append((first, size, unit, j % 2))
    many = len(packs)

    def on_units(*units):
        def push(i, rhs):
            _, _, unit, staged = packs[i]
            pltpu.matmul_push_rhs(rhs, staged, unit)

        def stage(c, i):
            k = c * chunk + packs[i][0]
            if packs[i][1] == 4:
                tiles = [[sens[k], sens[k + 1]], [sens[k + 2], sens[k + 3]]]
            else:
                tiles = [[sens[k], blank], [blank, sens[k + 1]]]
            push(i, jnp.concatenate([jnp.concatenate(row, axis=1) for row in tiles], axis=0))

        def multiply(c, i):
            first, size, _, staged = packs[i]
            scenarios = [shocks[pairs[0, c * chunk + first + t] - first_factor] for t in range(size)]
            if size == 4:
                passes = [[x, none] if t < 2 else [none, x] for t, x in enumerate(scenarios)]
            else:
                passes = [scenarios]
            for t, halves in enumerate(passes):
                target = units[spot[i] + t]
                pltpu.matmul_acc_lhs(target, jnp.concatenate(halves, axis=1), load_staged_rhs=None if t else staged)

        def collect(c, i):
            first, size, _, _ = packs[i]
            popped = [pltpu.matmul_pop(units[spot[i] + t]) for t in range(4 if size == 4 else 1)]
            for t in range(size):
                k = c * chunk + first + t
                book = jnp.where(pairs[2, k] != 0, pairs[1, k], books)
                side = (t % 2) * block
                acc[position[book]] += popped[t if size == 4 else 0][:, side : side + block]

        zeros = jnp.zeros((2 * block, 2 * block), sens.dtype)
        for i in range(many - LAG, many):
            push(i, zeros)
            if i < many - 2:
                multiply(padding, i)

        def work(c, carry):
            fetch(c).wait()
            before = jnp.where(c == 0, padding, c - 1)
            for i in range(many):
                stage(c, i)
                multiply(*((before, i - 2 + many) if i < 2 else (c, i - 2)))
                collect(*((before, i - LAG + many) if i < LAG else (c, i - LAG)))
            return carry

        get_order.wait()
        for p in range(books):
            owner = p // per_owner
            place = (owner // 2) * per_owner + p % per_owner
            position[order[p]] = place + half * ((owner & 1) ^ core)
        get_pairs.wait()

        def count(c, busy):
            return busy + jnp.where(pairs[2, c * chunk] != 0, 1, 0)

        busy = lax.fori_loop(0, chunks, count, 0)
        lax.fori_loop(0, busy, work, 0)
        last = jnp.where(busy == 0, padding, busy - 1)
        for i in range(many - 2, many):
            multiply(last, i)
        for i in range(many - LAG, many):
            collect(last, i)

        def drop(c, carry):
            fetch(c).wait()
            return carry

        lax.fori_loop(busy, chunks, drop, 0)

    spot = []
    held = []
    for _, size, unit, _ in packs:
        spot.append(len(held))
        held += [pltpu.ACC(unit)((rows, 2 * block), jnp.float32)] * (4 if size == 4 else 1)
    pl.run_scoped(on_units, *held)
    kept[...] = acc[:half]
    sent[...] = acc[half:books].astype(sent.dtype)


def shards(returns, vol_hist, vol_now, sensitivity, block_pairs, book_order):
    groups = lax.axis_size("blk")
    own_rows, width = returns.shape
    slots, block, _ = sensitivity.shape
    own = width // groups
    rows = groups * own_rows
    books = book_order.shape[0]
    siblings = [(i, i ^ 1) for i in range(groups)]
    rescaled = (returns.astype(jnp.float32) * vol_now[None, :] / vol_hist).astype(jnp.bfloat16)
    outgoing = rescaled.reshape(own_rows, groups, own).swapaxes(0, 1)
    incoming = lax.all_to_all(outgoing, "blk", 0, 0)
    shocks = incoming.reshape(rows, own // block, block).transpose(1, 0, 2)
    chunks = slots // UNROLL
    kept, sent = pl.pallas_call(
        functools.partial(accumulate, groups),
        in_specs=[VMEM, HBM, HBM, HBM],
        out_specs=[VMEM, VMEM],
        out_shape=[
            jax.ShapeDtypeStruct((books // 2, rows, block), jnp.float32),
            jax.ShapeDtypeStruct((books // 2, rows, block), jnp.bfloat16),
        ],
        scratch_shapes=[
            pltpu.VMEM((books + 1, rows, block), jnp.float32),
            pltpu.VMEM(sensitivity.shape, sensitivity.dtype),
            pltpu.SMEM((3, slots + UNROLL), jnp.int32),
            pltpu.SMEM((books,), jnp.int32),
            pltpu.SMEM((books + 1,), jnp.int32),
            pltpu.SemaphoreType.DMA((2,)),
            pltpu.SemaphoreType.DMA((chunks,)),
        ],
        compiler_params=pltpu.CompilerParams(vmem_limit_bytes=VMEM_LIMIT),
        cost_estimate=pl.CostEstimate(
            flops=2 * slots * rows * block * block,
            bytes_accessed=2 * slots * block * block,
            transcendentals=0,
        ),
    )(shocks, *(pltpu.with_memory_space_constraint(x, pltpu.HBM) for x in (block_pairs.T, book_order, sensitivity)))
    across = lax.ppermute(sent, "blk", siblings)
    per_owner = books // groups
    chips = groups // 2
    chip_sum = (kept + across.astype(jnp.float32)).astype(jnp.bfloat16).reshape(chips, per_owner, rows, block)
    same_core = [list(range(c, groups, 2)) for c in range(2)]
    arrived = lax.all_to_all(chip_sum, "blk", 0, 0, axis_index_groups=same_core)
    owned = jnp.sum(arrived.astype(jnp.float32), axis=0)
    profit_loss = owned.transpose(1, 0, 2).reshape(rows, per_owner * block)
    spans = lax.axis_size("scen")
    squares = jnp.sum(owned * owned, axis=1).reshape(-1)
    if spans == 2:
        squares = squares + lax.ppermute(squares, "scen", [(0, 1), (1, 0)])
    else:
        squares = lax.psum(squares, "scen")
    book_rms = jnp.sqrt(squares / (rows * spans) + 1e-06)
    return (profit_loss, book_rms)


def solution(mesh):
    def on_mesh(*args):
        with jax.sharding.use_abstract_mesh(mesh.abstract_mesh):
            return whole(*args)

    whole = jax.shard_map(
        shards,
        mesh=mesh,
        in_specs=(
            P(("scen", "blk"), None),
            P(("scen", "blk"), None),
            P(),
            P("blk", None, None),
            P("blk", None),
            P(),
        ),
        out_specs=(P("scen", "blk"), P("blk")),
        check_vma=False,
    )
    return on_mesh
```

```python
import functools

import jax
import jax.numpy as jnp
from jax import lax
from jax.experimental import pallas as pl
from jax.experimental.pallas import tpu as pltpu
from jax.sharding import PartitionSpec as P

UNROLL = 16
SIZES = (4, 4)
LAG = 4
VMEM_LIMIT = 32 * 1024 * 1024
VMEM = pl.BlockSpec(memory_space=pltpu.VMEM)
HBM = pl.BlockSpec(memory_space=pltpu.HBM)


def accumulate(
    groups, shocks, pairs_hbm, order_hbm, sens_hbm, kept, sent, acc, sens, pairs, order, position, small, arrived
):
    slots = sens.shape[0]
    factors = shocks.shape[0]
    chunks = arrived.shape[0]
    chunk = slots // chunks
    half = kept.shape[0]
    books = 2 * half
    per_owner = books // groups
    index = lax.axis_index("blk")
    core = index & 1

    def fetch(c):
        span = pl.ds(c * chunk, chunk)
        return pltpu.make_async_copy(sens_hbm.at[span], sens.at[span], arrived.at[c])

    get_order = pltpu.make_async_copy(order_hbm, order, small.at[0])
    get_pairs = pltpu.make_async_copy(pairs_hbm, pairs.at[:, pl.ds(0, slots)], small.at[1])
    get_order.start()
    get_pairs.start()
    for c in range(chunks):
        fetch(c).start()
    acc[...] = jnp.zeros_like(acc)
    position[books] = books
    first_factor = index * factors
    for u in range(chunk):
        pairs[0, slots + u] = first_factor
        pairs[1, slots + u] = 0
        pairs[2, slots + u] = 0
    padding = chunks
    rows, block = shocks.shape[1:]
    none = jnp.zeros((rows, block), shocks.dtype)
    blank = jnp.zeros((block, block), sens.dtype)

    packs = []
    for j, size in enumerate(SIZES):
        for unit in range(2):
            first = unit * (chunk // 2) + sum(SIZES[:j])
            packs.append((first, size, unit, j % 2))
    many = len(packs)

    def on_units(*units):
        def push(i, rhs):
            _, _, unit, staged = packs[i]
            pltpu.matmul_push_rhs(rhs, staged, unit)

        def stage(c, i):
            k = c * chunk + packs[i][0]
            if packs[i][1] == 4:
                tiles = [[sens[k], sens[k + 1]], [sens[k + 2], sens[k + 3]]]
            else:
                tiles = [[sens[k], blank], [blank, sens[k + 1]]]
            push(i, jnp.concatenate([jnp.concatenate(row, axis=1) for row in tiles], axis=0))

        def multiply(c, i):
            first, size, _, staged = packs[i]
            scenarios = [shocks[pairs[0, c * chunk + first + t] - first_factor] for t in range(size)]
            if size == 4:
                passes = [[x, none] if t < 2 else [none, x] for t, x in enumerate(scenarios)]
            else:
                passes = [scenarios]
            for t, halves in enumerate(passes):
                target = units[spot[i] + t]
                pltpu.matmul_acc_lhs(target, jnp.concatenate(halves, axis=1), load_staged_rhs=None if t else staged)

        def collect(c, i):
            first, size, _, _ = packs[i]
            popped = [pltpu.matmul_pop(units[spot[i] + t]) for t in range(4 if size == 4 else 1)]
            for t in range(size):
                k = c * chunk + first + t
                book = jnp.where(pairs[2, k] != 0, pairs[1, k], books)
                side = (t % 2) * block
                acc[position[book]] += popped[t if size == 4 else 0][:, side : side + block]

        zeros = jnp.zeros((2 * block, 2 * block), sens.dtype)
        for i in range(many - LAG, many):
            push(i, zeros)
            if i < many - 2:
                multiply(padding, i)

        def work(c, carry):
            fetch(c).wait()
            before = jnp.where(c == 0, padding, c - 1)
            for i in range(many):
                stage(c, i)
                multiply(*((before, i - 2 + many) if i < 2 else (c, i - 2)))
                collect(*((before, i - LAG + many) if i < LAG else (c, i - LAG)))
            return carry

        get_order.wait()
        for p in range(books):
            owner = p // per_owner
            place = (owner // 2) * per_owner + p % per_owner
            position[order[p]] = place + half * ((owner & 1) ^ core)
        get_pairs.wait()

        def count(c, busy):
            return busy + jnp.where(pairs[2, c * chunk] != 0, 1, 0)

        busy = lax.fori_loop(0, chunks, count, 0)
        lax.fori_loop(0, busy, work, 0)
        last = jnp.where(busy == 0, padding, busy - 1)
        for i in range(many - 2, many):
            multiply(last, i)
        for i in range(many - LAG, many):
            collect(last, i)

        def drop(c, carry):
            fetch(c).wait()
            return carry

        lax.fori_loop(busy, chunks, drop, 0)

    spot = []
    held = []
    for _, size, unit, _ in packs:
        spot.append(len(held))
        held += [pltpu.ACC(unit)((rows, 2 * block), jnp.float32)] * (4 if size == 4 else 1)
    pl.run_scoped(on_units, *held)
    kept[...] = acc[:half]
    sent[...] = acc[half:books].astype(sent.dtype)


def shards(returns, vol_hist, vol_now, sensitivity, block_pairs, book_order):
    groups = lax.axis_size("blk")
    own_rows, width = returns.shape
    slots, block, _ = sensitivity.shape
    own = width // groups
    rows = groups * own_rows
    books = book_order.shape[0]
    siblings = [(i, i ^ 1) for i in range(groups)]
    rescaled = (returns.astype(jnp.float32) * vol_now[None, :] / vol_hist).astype(jnp.bfloat16)
    outgoing = rescaled.reshape(own_rows, groups, own).swapaxes(0, 1)
    incoming = lax.all_to_all(outgoing, "blk", 0, 0)
    shocks = incoming.reshape(rows, own // block, block).transpose(1, 0, 2)
    chunks = slots // UNROLL
    kept, sent = pl.pallas_call(
        functools.partial(accumulate, groups),
        in_specs=[VMEM, HBM, HBM, HBM],
        out_specs=[VMEM, VMEM],
        out_shape=[
            jax.ShapeDtypeStruct((books // 2, rows, block), jnp.float32),
            jax.ShapeDtypeStruct((books // 2, rows, block), jnp.bfloat16),
        ],
        scratch_shapes=[
            pltpu.VMEM((books + 1, rows, block), jnp.float32),
            pltpu.VMEM(sensitivity.shape, sensitivity.dtype),
            pltpu.SMEM((3, slots + UNROLL), jnp.int32),
            pltpu.SMEM((books,), jnp.int32),
            pltpu.SMEM((books + 1,), jnp.int32),
            pltpu.SemaphoreType.DMA((2,)),
            pltpu.SemaphoreType.DMA((chunks,)),
        ],
        compiler_params=pltpu.CompilerParams(vmem_limit_bytes=VMEM_LIMIT),
        cost_estimate=pl.CostEstimate(
            flops=2 * slots * rows * block * block,
            bytes_accessed=2 * slots * block * block,
            transcendentals=0,
        ),
    )(shocks, *(pltpu.with_memory_space_constraint(x, pltpu.HBM) for x in (block_pairs.T, book_order, sensitivity)))
    across = lax.ppermute(sent, "blk", siblings)
    per_owner = books // groups
    chips = groups // 2
    chip_sum = (kept + across.astype(jnp.float32)).astype(jnp.bfloat16).reshape(chips, per_owner, rows, block)
    same_core = [list(range(c, groups, 2)) for c in range(2)]
    arrived = lax.all_to_all(chip_sum, "blk", 0, 0, axis_index_groups=same_core)
    owned = jnp.sum(arrived.astype(jnp.float32), axis=0)
    profit_loss = owned.transpose(1, 0, 2).reshape(rows, per_owner * block)
    spans = lax.axis_size("scen")
    squares = jnp.sum(owned * owned, axis=1).reshape(-1)
    if spans == 2:
        squares = squares + lax.ppermute(squares, "scen", [(0, 1), (1, 0)])
    else:
        squares = lax.psum(squares, "scen")
    book_rms = jnp.sqrt(squares / (rows * spans) + 1e-06)
    return (profit_loss, book_rms)


def solution(mesh):
    def on_mesh(*args):
        with jax.sharding.use_abstract_mesh(mesh.abstract_mesh):
            return whole(*args)

    whole = jax.shard_map(
        shards,
        mesh=mesh,
        in_specs=(
            P(("scen", "blk"), None),
            P(("scen", "blk"), None),
            P(),
            P("blk", None, None),
            P("blk", None),
            P(),
        ),
        out_specs=(P("scen", "blk"), P("blk")),
        check_vma=False,
    )
    return on_mesh
```

```python
import functools

import jax
import jax.numpy as jnp
from jax import lax
from jax.experimental import pallas as pl
from jax.experimental.pallas import tpu as pltpu
from jax.sharding import PartitionSpec as P

UNROLL = 32
SIZES = (4, 2, 2, 4, 2, 2)
LAG = 6
AHEAD = 3
VMEM_LIMIT = 32 * 1024 * 1024
VMEM = pl.BlockSpec(memory_space=pltpu.VMEM)
HBM = pl.BlockSpec(memory_space=pltpu.HBM)


def accumulate(
    groups, shocks, pairs_hbm, order_hbm, sens_hbm, kept, sent, acc, sens, pairs, order, position, small, arrived
):
    slots = sens.shape[0]
    factors = shocks.shape[0]
    chunks = arrived.shape[0]
    chunk = slots // chunks
    half = kept.shape[0]
    books = 2 * half
    per_owner = books // groups
    index = lax.axis_index("blk")
    core = index & 1

    def fetch(c):
        span = pl.ds(c * chunk, chunk)
        return pltpu.make_async_copy(sens_hbm.at[span], sens.at[span], arrived.at[c])

    get_order = pltpu.make_async_copy(order_hbm, order, small.at[0])
    get_pairs = pltpu.make_async_copy(pairs_hbm, pairs.at[:, pl.ds(0, slots)], small.at[1])
    get_order.start()
    get_pairs.start()
    for c in range(AHEAD):
        fetch(c).start()
    acc[...] = jnp.zeros_like(acc)
    position[books] = books
    first_factor = index * factors
    for u in range(chunk):
        pairs[0, slots + u] = first_factor
        pairs[1, slots + u] = 0
        pairs[2, slots + u] = 0
    padding = chunks
    rows, block = shocks.shape[1:]
    none = jnp.zeros((rows, block), shocks.dtype)
    blank = jnp.zeros((block, block), sens.dtype)

    packs = []
    for j, size in enumerate(SIZES):
        for unit in range(2):
            first = unit * (chunk // 2) + sum(SIZES[:j])
            packs.append((first, size, unit, j % 2))
    many = len(packs)

    def on_units(*units):
        def push(i, rhs):
            _, _, unit, staged = packs[i]
            pltpu.matmul_push_rhs(rhs, staged, unit)

        def stage(c, i):
            k = c * chunk + packs[i][0]
            if packs[i][1] == 4:
                tiles = [[sens[k], sens[k + 1]], [sens[k + 2], sens[k + 3]]]
            else:
                tiles = [[sens[k], blank], [blank, sens[k + 1]]]
            push(i, jnp.concatenate([jnp.concatenate(row, axis=1) for row in tiles], axis=0))

        def multiply(c, i):
            first, size, _, staged = packs[i]
            scenarios = [shocks[pairs[0, c * chunk + first + t] - first_factor] for t in range(size)]
            if size == 4:
                passes = [[x, none] if t < 2 else [none, x] for t, x in enumerate(scenarios)]
            else:
                passes = [scenarios]
            for t, halves in enumerate(passes):
                target = units[spot[i] + t]
                pltpu.matmul_acc_lhs(target, jnp.concatenate(halves, axis=1), load_staged_rhs=None if t else staged)

        def collect(c, i):
            first, size, _, _ = packs[i]
            popped = [pltpu.matmul_pop(units[spot[i] + t]) for t in range(4 if size == 4 else 1)]
            for t in range(size):
                k = c * chunk + first + t
                book = jnp.where(pairs[2, k] != 0, pairs[1, k], books)
                side = (t % 2) * block
                acc[position[book]] += popped[t if size == 4 else 0][:, side : side + block]

        zeros = jnp.zeros((2 * block, 2 * block), sens.dtype)
        for i in range(many - LAG, many):
            push(i, zeros)
            if i < many - 2:
                multiply(padding, i)

        def work(c, carry):
            fetch(c).wait()

            @pl.when(c + AHEAD < busy)
            def _():
                fetch(c + AHEAD).start()

            before = jnp.where(c == 0, padding, c - 1)
            for i in range(many):
                stage(c, i)
                multiply(*((before, i - 2 + many) if i < 2 else (c, i - 2)))
                collect(*((before, i - LAG + many) if i < LAG else (c, i - LAG)))
            return carry

        get_order.wait()
        for p in range(books):
            owner = p // per_owner
            place = (owner // 2) * per_owner + p % per_owner
            position[order[p]] = place + half * ((owner & 1) ^ core)
        get_pairs.wait()

        def count(c, busy):
            return busy + jnp.where(pairs[2, c * chunk] != 0, 1, 0)

        busy = lax.fori_loop(0, chunks, count, 0)
        lax.fori_loop(0, busy, work, 0)
        last = jnp.where(busy == 0, padding, busy - 1)
        for i in range(many - 2, many):
            multiply(last, i)
        for i in range(many - LAG, many):
            collect(last, i)

        def drop(c, carry):
            fetch(c).wait()
            return carry

        lax.fori_loop(busy, AHEAD, drop, 0)

    spot = []
    held = []
    for _, size, unit, _ in packs:
        spot.append(len(held))
        held += [pltpu.ACC(unit)((rows, 2 * block), jnp.float32)] * (4 if size == 4 else 1)
    pl.run_scoped(on_units, *held)
    kept[...] = acc[:half]
    sent[...] = acc[half:books].astype(sent.dtype)


def shards(returns, vol_hist, vol_now, sensitivity, block_pairs, book_order):
    groups = lax.axis_size("blk")
    own_rows, width = returns.shape
    slots, block, _ = sensitivity.shape
    own = width // groups
    rows = groups * own_rows
    books = book_order.shape[0]
    siblings = [(i, i ^ 1) for i in range(groups)]
    rescaled = (returns.astype(jnp.float32) * vol_now[None, :] / vol_hist).astype(jnp.bfloat16)
    outgoing = rescaled.reshape(own_rows, groups, own).swapaxes(0, 1)
    incoming = lax.all_to_all(outgoing, "blk", 0, 0)
    shocks = incoming.reshape(rows, own // block, block).transpose(1, 0, 2)
    chunks = slots // UNROLL
    kept, sent = pl.pallas_call(
        functools.partial(accumulate, groups),
        in_specs=[VMEM, HBM, HBM, HBM],
        out_specs=[VMEM, VMEM],
        out_shape=[
            jax.ShapeDtypeStruct((books // 2, rows, block), jnp.float32),
            jax.ShapeDtypeStruct((books // 2, rows, block), jnp.bfloat16),
        ],
        scratch_shapes=[
            pltpu.VMEM((books + 1, rows, block), jnp.float32),
            pltpu.VMEM(sensitivity.shape, sensitivity.dtype),
            pltpu.SMEM((3, slots + UNROLL), jnp.int32),
            pltpu.SMEM((books,), jnp.int32),
            pltpu.SMEM((books + 1,), jnp.int32),
            pltpu.SemaphoreType.DMA((2,)),
            pltpu.SemaphoreType.DMA((chunks,)),
        ],
        compiler_params=pltpu.CompilerParams(vmem_limit_bytes=VMEM_LIMIT),
        cost_estimate=pl.CostEstimate(
            flops=2 * slots * rows * block * block,
            bytes_accessed=2 * slots * block * block,
            transcendentals=0,
        ),
    )(shocks, *(pltpu.with_memory_space_constraint(x, pltpu.HBM) for x in (block_pairs.T, book_order, sensitivity)))
    across = lax.ppermute(sent, "blk", siblings)
    per_owner = books // groups
    chips = groups // 2
    chip_sum = (kept + across.astype(jnp.float32)).astype(jnp.bfloat16).reshape(chips, per_owner, rows, block)
    same_core = [list(range(c, groups, 2)) for c in range(2)]
    arrived = lax.all_to_all(chip_sum, "blk", 0, 0, axis_index_groups=same_core)
    owned = jnp.sum(arrived.astype(jnp.float32), axis=0)
    profit_loss = owned.transpose(1, 0, 2).reshape(rows, per_owner * block)
    spans = lax.axis_size("scen")
    squares = jnp.sum(owned * owned, axis=1).reshape(-1)
    if spans == 2:
        squares = squares + lax.ppermute(squares, "scen", [(0, 1), (1, 0)])
    else:
        squares = lax.psum(squares, "scen")
    book_rms = jnp.sqrt(squares / (rows * spans) + 1e-06)
    return (profit_loss, book_rms)


def solution(mesh):
    def on_mesh(*args):
        with jax.sharding.use_abstract_mesh(mesh.abstract_mesh):
            return whole(*args)

    whole = jax.shard_map(
        shards,
        mesh=mesh,
        in_specs=(
            P(("scen", "blk"), None),
            P(("scen", "blk"), None),
            P(),
            P("blk", None, None),
            P("blk", None),
            P(),
        ),
        out_specs=(P("scen", "blk"), P("blk")),
        check_vma=False,
    )
    return on_mesh
```

```python
import functools

import jax
import jax.numpy as jnp
from jax import lax
from jax.experimental import pallas as pl
from jax.experimental.pallas import tpu as pltpu
from jax.sharding import PartitionSpec as P

UNROLL = 32
SIZES = (4, 2, 2, 4, 2, 2)
LAG = 6
AHEAD = 2
VMEM_LIMIT = 32 * 1024 * 1024
VMEM = pl.BlockSpec(memory_space=pltpu.VMEM)
HBM = pl.BlockSpec(memory_space=pltpu.HBM)


def accumulate(
    groups, shocks, pairs_hbm, order_hbm, sens_hbm, kept, sent, acc, sens, pairs, order, position, small, arrived
):
    slots = sens.shape[0]
    factors = shocks.shape[0]
    chunks = arrived.shape[0]
    chunk = slots // chunks
    half = kept.shape[0]
    books = 2 * half
    per_owner = books // groups
    index = lax.axis_index("blk")
    core = index & 1

    def fetch(c):
        span = pl.ds(c * chunk, chunk)
        return pltpu.make_async_copy(sens_hbm.at[span], sens.at[span], arrived.at[c])

    get_order = pltpu.make_async_copy(order_hbm, order, small.at[0])
    get_pairs = pltpu.make_async_copy(pairs_hbm, pairs.at[:, pl.ds(0, slots)], small.at[1])
    get_order.start()
    get_pairs.start()
    for c in range(AHEAD):
        fetch(c).start()
    acc[...] = jnp.zeros_like(acc)
    position[books] = books
    first_factor = index * factors
    for u in range(chunk):
        pairs[0, slots + u] = first_factor
        pairs[1, slots + u] = 0
        pairs[2, slots + u] = 0
    padding = chunks
    rows, block = shocks.shape[1:]
    none = jnp.zeros((rows, block), shocks.dtype)
    blank = jnp.zeros((block, block), sens.dtype)

    packs = []
    for j, size in enumerate(SIZES):
        for unit in range(2):
            first = unit * (chunk // 2) + sum(SIZES[:j])
            packs.append((first, size, unit, j % 2))
    many = len(packs)

    def on_units(*units):
        def push(i, rhs):
            _, _, unit, staged = packs[i]
            pltpu.matmul_push_rhs(rhs, staged, unit)

        def stage(c, i):
            k = c * chunk + packs[i][0]
            if packs[i][1] == 4:
                tiles = [[sens[k], sens[k + 1]], [sens[k + 2], sens[k + 3]]]
            else:
                tiles = [[sens[k], blank], [blank, sens[k + 1]]]
            push(i, jnp.concatenate([jnp.concatenate(row, axis=1) for row in tiles], axis=0))

        def multiply(c, i):
            first, size, _, staged = packs[i]
            scenarios = [shocks[pairs[0, c * chunk + first + t] - first_factor] for t in range(size)]
            if size == 4:
                passes = [[x, none] if t < 2 else [none, x] for t, x in enumerate(scenarios)]
            else:
                passes = [scenarios]
            for t, halves in enumerate(passes):
                target = units[spot[i] + t]
                pltpu.matmul_acc_lhs(target, jnp.concatenate(halves, axis=1), load_staged_rhs=None if t else staged)

        def collect(c, i):
            first, size, _, _ = packs[i]
            popped = [pltpu.matmul_pop(units[spot[i] + t]) for t in range(4 if size == 4 else 1)]
            for t in range(size):
                k = c * chunk + first + t
                book = jnp.where(pairs[2, k] != 0, pairs[1, k], books)
                side = (t % 2) * block
                acc[position[book]] += popped[t if size == 4 else 0][:, side : side + block]

        zeros = jnp.zeros((2 * block, 2 * block), sens.dtype)
        for i in range(many - LAG, many):
            push(i, zeros)
            if i < many - 2:
                multiply(padding, i)

        def work(c, carry):
            fetch(c).wait()
            before = jnp.where(c == 0, padding, c - 1)
            for i in range(many):
                stage(c, i)
                multiply(*((before, i - 2 + many) if i < 2 else (c, i - 2)))
                collect(*((before, i - LAG + many) if i < LAG else (c, i - LAG)))
            return carry

        get_pairs.wait()

        def count(c, busy):
            return busy + jnp.where(pairs[2, c * chunk] != 0, 1, 0)

        busy = lax.fori_loop(0, chunks, count, 0)

        def begin(c, carry):
            fetch(c).start()
            return carry

        lax.fori_loop(AHEAD, busy, begin, 0)
        get_order.wait()
        for p in range(books):
            owner = p // per_owner
            place = (owner // 2) * per_owner + p % per_owner
            position[order[p]] = place + half * ((owner & 1) ^ core)
        lax.fori_loop(0, busy, work, 0)
        last = jnp.where(busy == 0, padding, busy - 1)
        for i in range(many - 2, many):
            multiply(last, i)
        for i in range(many - LAG, many):
            collect(last, i)

        def drop(c, carry):
            fetch(c).wait()
            return carry

        lax.fori_loop(busy, AHEAD, drop, 0)

    spot = []
    held = []
    for _, size, unit, _ in packs:
        spot.append(len(held))
        held += [pltpu.ACC(unit)((rows, 2 * block), jnp.float32)] * (4 if size == 4 else 1)
    pl.run_scoped(on_units, *held)
    kept[...] = acc[:half]
    sent[...] = acc[half:books].astype(sent.dtype)


def shards(returns, vol_hist, vol_now, sensitivity, block_pairs, book_order):
    groups = lax.axis_size("blk")
    own_rows, width = returns.shape
    slots, block, _ = sensitivity.shape
    own = width // groups
    rows = groups * own_rows
    books = book_order.shape[0]
    siblings = [(i, i ^ 1) for i in range(groups)]
    rescaled = (returns.astype(jnp.float32) * vol_now[None, :] / vol_hist).astype(jnp.bfloat16)
    outgoing = rescaled.reshape(own_rows, groups, own).swapaxes(0, 1)
    incoming = lax.all_to_all(outgoing, "blk", 0, 0)
    shocks = incoming.reshape(rows, own // block, block).transpose(1, 0, 2)
    chunks = slots // UNROLL
    kept, sent = pl.pallas_call(
        functools.partial(accumulate, groups),
        in_specs=[VMEM, HBM, HBM, HBM],
        out_specs=[VMEM, VMEM],
        out_shape=[
            jax.ShapeDtypeStruct((books // 2, rows, block), jnp.float32),
            jax.ShapeDtypeStruct((books // 2, rows, block), jnp.bfloat16),
        ],
        scratch_shapes=[
            pltpu.VMEM((books + 1, rows, block), jnp.float32),
            pltpu.VMEM(sensitivity.shape, sensitivity.dtype),
            pltpu.SMEM((3, slots + UNROLL), jnp.int32),
            pltpu.SMEM((books,), jnp.int32),
            pltpu.SMEM((books + 1,), jnp.int32),
            pltpu.SemaphoreType.DMA((2,)),
            pltpu.SemaphoreType.DMA((chunks,)),
        ],
        compiler_params=pltpu.CompilerParams(vmem_limit_bytes=VMEM_LIMIT),
        cost_estimate=pl.CostEstimate(
            flops=2 * slots * rows * block * block,
            bytes_accessed=2 * slots * block * block,
            transcendentals=0,
        ),
    )(shocks, *(pltpu.with_memory_space_constraint(x, pltpu.HBM) for x in (block_pairs.T, book_order, sensitivity)))
    across = lax.ppermute(sent, "blk", siblings)
    per_owner = books // groups
    chips = groups // 2
    chip_sum = (kept + across.astype(jnp.float32)).astype(jnp.bfloat16).reshape(chips, per_owner, rows, block)
    same_core = [list(range(c, groups, 2)) for c in range(2)]
    arrived = lax.all_to_all(chip_sum, "blk", 0, 0, axis_index_groups=same_core)
    owned = jnp.sum(arrived.astype(jnp.float32), axis=0)
    profit_loss = owned.transpose(1, 0, 2).reshape(rows, per_owner * block)
    spans = lax.axis_size("scen")
    squares = jnp.sum(owned * owned, axis=1).reshape(-1)
    if spans == 2:
        squares = squares + lax.ppermute(squares, "scen", [(0, 1), (1, 0)])
    else:
        squares = lax.psum(squares, "scen")
    book_rms = jnp.sqrt(squares / (rows * spans) + 1e-06)
    return (profit_loss, book_rms)


def solution(mesh):
    def on_mesh(*args):
        with jax.sharding.use_abstract_mesh(mesh.abstract_mesh):
            return whole(*args)

    whole = jax.shard_map(
        shards,
        mesh=mesh,
        in_specs=(
            P(("scen", "blk"), None),
            P(("scen", "blk"), None),
            P(),
            P("blk", None, None),
            P("blk", None),
            P(),
        ),
        out_specs=(P("scen", "blk"), P("blk")),
        check_vma=False,
    )
    return on_mesh
```

```python
import functools

import jax
import jax.numpy as jnp
from jax import lax
from jax.experimental import pallas as pl
from jax.experimental.pallas import tpu as pltpu
from jax.sharding import PartitionSpec as P

UNROLL = 32
AHEAD = 2
VMEM_LIMIT = 32 * 1024 * 1024
VMEM = pl.BlockSpec(memory_space=pltpu.VMEM)
HBM = pl.BlockSpec(memory_space=pltpu.HBM)


def accumulate(
    groups, shocks, pairs_hbm, order_hbm, sens_hbm, kept, sent, acc, sens, pairs, order, position, small, arrived
):
    slots = sens.shape[0]
    factors, _, block = shocks.shape
    chunks = arrived.shape[0]
    chunk = slots // chunks
    half = kept.shape[0]
    books = 2 * half
    per_owner = books // groups
    index = lax.axis_index("blk")
    core = index & 1

    def fetch(c):
        span = pl.ds(c * chunk, chunk)
        return pltpu.make_async_copy(sens_hbm.at[span], sens.at[span], arrived.at[c])

    get_order = pltpu.make_async_copy(order_hbm, order, small.at[0])
    get_pairs = pltpu.make_async_copy(pairs_hbm, pairs, small.at[1])
    get_order.start()
    get_pairs.start()
    for c in range(AHEAD):
        fetch(c).start()
    acc[...] = jnp.zeros_like(acc)
    first_factor = index * factors
    get_pairs.wait()

    def count(c, busy):
        return busy + jnp.where(pairs[2, c * chunk] != 0, 1, 0)

    busy = lax.fori_loop(0, chunks, count, 0)

    def begin(c, carry):
        fetch(c).start()
        return carry

    lax.fori_loop(AHEAD, busy, begin, 0)
    get_order.wait()
    for p in range(books):
        owner = p // per_owner
        place = (owner // 2) * per_owner + p % per_owner
        position[order[p]] = place + half * ((owner & 1) ^ core)
    position[books] = books

    def work(c, carry):
        fetch(c).wait()
        for u in range(chunk):
            k = c * chunk + u
            book = jnp.where(pairs[2, k] != 0, pairs[1, k], books)
            f = pairs[0, k] - first_factor
            acc[position[book]] += jnp.dot(shocks[f], sens[k], preferred_element_type=jnp.float32)
        return carry

    def drop(c, carry):
        fetch(c).wait()
        return carry

    lax.fori_loop(0, busy, work, 0)
    lax.fori_loop(busy, AHEAD, drop, 0)
    kept[...] = acc[:half]
    sent[...] = acc[half:books].astype(sent.dtype)


def shards(returns, vol_hist, vol_now, sensitivity, block_pairs, book_order):
    groups = lax.axis_size("blk")
    own_rows, width = returns.shape
    slots, block, _ = sensitivity.shape
    own = width // groups
    rows = groups * own_rows
    books = book_order.shape[0]
    siblings = [(i, i ^ 1) for i in range(groups)]
    rescaled = (returns.astype(jnp.float32) * vol_now[None, :] / vol_hist).astype(jnp.bfloat16)
    outgoing = rescaled.reshape(own_rows, groups, own).swapaxes(0, 1)
    incoming = lax.all_to_all(outgoing, "blk", 0, 0)
    shocks = incoming.reshape(rows, own // block, block).transpose(1, 0, 2)
    chunks = slots // UNROLL
    kept, sent = pl.pallas_call(
        functools.partial(accumulate, groups),
        in_specs=[VMEM, HBM, HBM, HBM],
        out_specs=[VMEM, VMEM],
        out_shape=[
            jax.ShapeDtypeStruct((books // 2, rows, block), jnp.float32),
            jax.ShapeDtypeStruct((books // 2, rows, block), jnp.bfloat16),
        ],
        scratch_shapes=[
            pltpu.VMEM((books + 1, rows, block), jnp.float32),
            pltpu.VMEM(sensitivity.shape, sensitivity.dtype),
            pltpu.SMEM((3, slots), jnp.int32),
            pltpu.SMEM((books,), jnp.int32),
            pltpu.SMEM((books + 1,), jnp.int32),
            pltpu.SemaphoreType.DMA((2,)),
            pltpu.SemaphoreType.DMA((chunks,)),
        ],
        compiler_params=pltpu.CompilerParams(vmem_limit_bytes=VMEM_LIMIT),
        cost_estimate=pl.CostEstimate(
            flops=2 * slots * rows * block * block,
            bytes_accessed=2 * slots * block * block,
            transcendentals=0,
        ),
    )(shocks, *(pltpu.with_memory_space_constraint(x, pltpu.HBM) for x in (block_pairs.T, book_order, sensitivity)))
    across = lax.ppermute(sent, "blk", siblings)
    per_owner = books // groups
    chips = groups // 2
    chip_sum = (kept + across.astype(jnp.float32)).astype(jnp.bfloat16).reshape(chips, per_owner, rows, block)
    same_core = [list(range(c, groups, 2)) for c in range(2)]
    arrived = lax.all_to_all(chip_sum, "blk", 0, 0, axis_index_groups=same_core)
    owned = jnp.sum(arrived.astype(jnp.float32), axis=0)
    profit_loss = owned.transpose(1, 0, 2).reshape(rows, per_owner * block)
    spans = lax.axis_size("scen")
    squares = jnp.sum(owned * owned, axis=1).reshape(-1)
    if spans == 2:
        squares = squares + lax.ppermute(squares, "scen", [(0, 1), (1, 0)])
    else:
        squares = lax.psum(squares, "scen")
    book_rms = jnp.sqrt(squares / (rows * spans) + 1e-06)
    return (profit_loss, book_rms)


def solution(mesh):
    return jax.shard_map(
        shards,
        mesh=mesh,
        in_specs=(
            P(("scen", "blk"), None),
            P(("scen", "blk"), None),
            P(),
            P("blk", None, None),
            P("blk", None),
            P(),
        ),
        out_specs=(P("scen", "blk"), P("blk")),
        check_vma=False,
    )
```

```python
import jax
import jax.numpy as jnp
from jax import lax
from jax.experimental import pallas as pl
from jax.experimental.pallas import tpu as pltpu
from jax.sharding import PartitionSpec as P

UNROLL = 32
SIZES = (4, 2, 2, 4, 2, 2)
LAG = 6
AHEAD = 2
VMEM_LIMIT = 32 * 1024 * 1024
VMEM = pl.BlockSpec(memory_space=pltpu.VMEM)
HBM = pl.BlockSpec(memory_space=pltpu.HBM)


def accumulate(
    shocks, pairs_hbm, order_hbm, sens_hbm, kept, sent, acc, sens, pairs, order, position, small, arrived
):
    slots = sens.shape[0]
    factors = shocks.shape[0]
    chunks = arrived.shape[0]
    chunk = slots // chunks
    books, half, _ = kept.shape
    index = lax.axis_index("blk")
    core = index & 1

    def fetch(c):
        span = pl.ds(c * chunk, chunk)
        return pltpu.make_async_copy(sens_hbm.at[span], sens.at[span], arrived.at[c])

    get_order = pltpu.make_async_copy(order_hbm, order, small.at[0])
    get_pairs = pltpu.make_async_copy(pairs_hbm, pairs.at[:, pl.ds(0, slots)], small.at[1])
    get_order.start()
    get_pairs.start()
    for c in range(AHEAD):
        fetch(c).start()
    acc[...] = jnp.zeros_like(acc)
    position[books] = books
    first_factor = index * factors
    for u in range(chunk):
        pairs[0, slots + u] = first_factor
        pairs[1, slots + u] = 0
        pairs[2, slots + u] = 0
    padding = chunks
    rows, block = shocks.shape[1:]
    none = jnp.zeros((rows, block), shocks.dtype)
    blank = jnp.zeros((block, block), sens.dtype)

    packs = []
    for j, size in enumerate(SIZES):
        for unit in range(2):
            first = unit * (chunk // 2) + sum(SIZES[:j])
            packs.append((first, size, unit, j % 2))
    many = len(packs)

    def on_units(*units):
        def push(i, rhs):
            _, _, unit, staged = packs[i]
            pltpu.matmul_push_rhs(rhs, staged, unit)

        def stage(c, i):
            k = c * chunk + packs[i][0]
            if packs[i][1] == 4:
                tiles = [[sens[k], sens[k + 1]], [sens[k + 2], sens[k + 3]]]
            else:
                tiles = [[sens[k], blank], [blank, sens[k + 1]]]
            push(i, jnp.concatenate([jnp.concatenate(row, axis=1) for row in tiles], axis=0))

        def multiply(c, i):
            first, size, _, staged = packs[i]
            scenarios = [shocks[pairs[0, c * chunk + first + t] - first_factor] for t in range(size)]
            if size == 4:
                passes = [[x, none] if t < 2 else [none, x] for t, x in enumerate(scenarios)]
            else:
                passes = [scenarios]
            for t, halves in enumerate(passes):
                target = units[spot[i] + t]
                pltpu.matmul_acc_lhs(target, jnp.concatenate(halves, axis=1), load_staged_rhs=None if t else staged)

        def collect(c, i):
            first, size, _, _ = packs[i]
            popped = [pltpu.matmul_pop(units[spot[i] + t]) for t in range(4 if size == 4 else 1)]
            for t in range(size):
                k = c * chunk + first + t
                book = jnp.where(pairs[2, k] != 0, pairs[1, k], books)
                side = (t % 2) * block
                acc[position[book]] += popped[t if size == 4 else 0][:, side : side + block]

        zeros = jnp.zeros((2 * block, 2 * block), sens.dtype)
        for i in range(many - LAG, many):
            push(i, zeros)
            if i < many - 2:
                multiply(padding, i)

        def work(c, carry):
            fetch(c).wait()
            before = jnp.where(c == 0, padding, c - 1)
            for i in range(many):
                stage(c, i)
                multiply(*((before, i - 2 + many) if i < 2 else (c, i - 2)))
                collect(*((before, i - LAG + many) if i < LAG else (c, i - LAG)))
            return carry

        get_pairs.wait()

        def count(c, busy):
            return busy + jnp.where(pairs[2, c * chunk] != 0, 1, 0)

        busy = lax.fori_loop(0, chunks, count, 0)

        def begin(c, carry):
            fetch(c).start()
            return carry

        lax.fori_loop(AHEAD, busy, begin, 0)
        get_order.wait()
        for p in range(books):
            position[order[p]] = p
        lax.fori_loop(0, busy, work, 0)
        last = jnp.where(busy == 0, padding, busy - 1)
        for i in range(many - 2, many):
            multiply(last, i)
        for i in range(many - LAG, many):
            collect(last, i)

        def drop(c, carry):
            fetch(c).wait()
            return carry

        lax.fori_loop(busy, AHEAD, drop, 0)

    spot = []
    held = []
    for _, size, unit, _ in packs:
        spot.append(len(held))
        held += [pltpu.ACC(unit)((rows, 2 * block), jnp.float32)] * (4 if size == 4 else 1)
    pl.run_scoped(on_units, *held)
    kept[...] = acc[:books, pl.ds(pl.multiple_of(core * half, half), half)]
    sent[...] = acc[:books, pl.ds(pl.multiple_of((1 - core) * half, half), half)].astype(sent.dtype)


def shards(returns, vol_hist, vol_now, sensitivity, block_pairs, book_order):
    groups = lax.axis_size("blk")
    own_rows, width = returns.shape
    slots, block, _ = sensitivity.shape
    own = width // groups
    rows = groups * own_rows
    books = book_order.shape[0]
    siblings = [(i, i ^ 1) for i in range(groups)]
    rescaled = (returns.astype(jnp.float32) * vol_now[None, :] / vol_hist).astype(jnp.bfloat16)
    outgoing = rescaled.reshape(own_rows, groups, own).swapaxes(0, 1)
    incoming = lax.all_to_all(outgoing, "blk", 0, 0)
    shocks = incoming.reshape(rows, own // block, block).transpose(1, 0, 2)
    chunks = slots // UNROLL
    kept, sent = pl.pallas_call(
        accumulate,
        in_specs=[VMEM, HBM, HBM, HBM],
        out_specs=[VMEM, VMEM],
        out_shape=[
            jax.ShapeDtypeStruct((books, rows // 2, block), jnp.float32),
            jax.ShapeDtypeStruct((books, rows // 2, block), jnp.bfloat16),
        ],
        scratch_shapes=[
            pltpu.VMEM((books + 1, rows, block), jnp.float32),
            pltpu.VMEM(sensitivity.shape, sensitivity.dtype),
            pltpu.SMEM((3, slots + UNROLL), jnp.int32),
            pltpu.SMEM((books,), jnp.int32),
            pltpu.SMEM((books + 1,), jnp.int32),
            pltpu.SemaphoreType.DMA((2,)),
            pltpu.SemaphoreType.DMA((chunks,)),
        ],
        compiler_params=pltpu.CompilerParams(vmem_limit_bytes=VMEM_LIMIT),
        cost_estimate=pl.CostEstimate(
            flops=2 * slots * rows * block * block,
            bytes_accessed=2 * slots * block * block,
            transcendentals=0,
        ),
    )(shocks, *(pltpu.with_memory_space_constraint(x, pltpu.HBM) for x in (block_pairs.T, book_order, sensitivity)))
    across = lax.ppermute(sent, "blk", siblings)
    per_owner = books // groups
    chip_sum = (kept + across.astype(jnp.float32)).astype(jnp.bfloat16)
    arrived = lax.all_to_all(chip_sum.reshape(groups, per_owner, rows // 2, block), "blk", 0, 0)
    arrived = arrived.reshape(groups // 2, 2, per_owner, rows // 2, block)
    owned = jnp.sum(arrived.astype(jnp.float32), axis=0).swapaxes(0, 1).reshape(per_owner, rows, block)
    profit_loss = owned.transpose(1, 0, 2).reshape(rows, per_owner * block)
    spans = lax.axis_size("scen")
    squares = jnp.sum(owned * owned, axis=1).reshape(-1)
    if spans == 2:
        squares = squares + lax.ppermute(squares, "scen", [(0, 1), (1, 0)])
    else:
        squares = lax.psum(squares, "scen")
    book_rms = jnp.sqrt(squares / (rows * spans) + 1e-06)
    return (profit_loss, book_rms)


def solution(mesh):
    def on_mesh(*args):
        with jax.sharding.use_abstract_mesh(mesh.abstract_mesh):
            return whole(*args)

    whole = jax.shard_map(
        shards,
        mesh=mesh,
        in_specs=(
            P(("scen", "blk"), None),
            P(("scen", "blk"), None),
            P(),
            P("blk", None, None),
            P("blk", None),
            P(),
        ),
        out_specs=(P("scen", "blk"), P("blk")),
        check_vma=False,
    )
    return on_mesh
```

```python
import functools

import jax
import jax.numpy as jnp
from jax import lax
from jax.experimental import pallas as pl
from jax.experimental.pallas import tpu as pltpu
from jax.sharding import PartitionSpec as P

UNROLL = 32
SIZES = (4, 2, 2, 4, 2, 2)
LAG = 6
AHEAD = 2
VMEM_LIMIT = 32 * 1024 * 1024
VMEM = pl.BlockSpec(memory_space=pltpu.VMEM)
HBM = pl.BlockSpec(memory_space=pltpu.HBM)


def accumulate(
    groups, shocks, pairs_hbm, order_hbm, sens_hbm, kept, sent, acc, sens, pairs, order, position, small, arrived
):
    slots = sens.shape[0]
    factors = shocks.shape[0]
    chunks = arrived.shape[0]
    chunk = slots // chunks
    half = kept.shape[0]
    books = 2 * half
    per_owner = books // groups
    index = lax.axis_index("blk")
    core = index & 1

    def fetch(c):
        span = pl.ds(c * chunk, chunk)
        return pltpu.make_async_copy(sens_hbm.at[span], sens.at[span], arrived.at[c])

    get_order = pltpu.make_async_copy(order_hbm, order, small.at[0])
    get_pairs = pltpu.make_async_copy(pairs_hbm, pairs.at[:, pl.ds(0, slots)], small.at[1])
    get_order.start()
    get_pairs.start()
    for c in range(AHEAD):
        fetch(c).start()
    acc[...] = jnp.zeros_like(acc)
    position[books] = books
    first_factor = index * factors
    for u in range(chunk):
        pairs[0, slots + u] = first_factor
        pairs[1, slots + u] = 0
        pairs[2, slots + u] = 0
    padding = chunks
    rank = reversed_bits(groups // 2)
    rows, block = shocks.shape[1:]
    none = jnp.zeros((rows, block), shocks.dtype)
    blank = jnp.zeros((block, block), sens.dtype)

    packs = []
    for j, size in enumerate(SIZES):
        for unit in range(2):
            first = unit * (chunk // 2) + sum(SIZES[:j])
            packs.append((first, size, unit, j % 2))
    many = len(packs)

    def on_units(*units):
        def push(i, rhs):
            _, _, unit, staged = packs[i]
            pltpu.matmul_push_rhs(rhs, staged, unit)

        def stage(c, i):
            k = c * chunk + packs[i][0]
            if packs[i][1] == 4:
                tiles = [[sens[k], sens[k + 1]], [sens[k + 2], sens[k + 3]]]
            else:
                tiles = [[sens[k], blank], [blank, sens[k + 1]]]
            push(i, jnp.concatenate([jnp.concatenate(row, axis=1) for row in tiles], axis=0))

        def multiply(c, i):
            first, size, _, staged = packs[i]
            scenarios = [shocks[pairs[0, c * chunk + first + t] - first_factor] for t in range(size)]
            if size == 4:
                passes = [[x, none] if t < 2 else [none, x] for t, x in enumerate(scenarios)]
            else:
                passes = [scenarios]
            for t, halves in enumerate(passes):
                target = units[spot[i] + t]
                pltpu.matmul_acc_lhs(target, jnp.concatenate(halves, axis=1), load_staged_rhs=None if t else staged)

        def collect(c, i):
            first, size, _, _ = packs[i]
            popped = [pltpu.matmul_pop(units[spot[i] + t]) for t in range(4 if size == 4 else 1)]
            for t in range(size):
                k = c * chunk + first + t
                book = jnp.where(pairs[2, k] != 0, pairs[1, k], books)
                side = (t % 2) * block
                acc[position[book]] += popped[t if size == 4 else 0][:, side : side + block]

        zeros = jnp.zeros((2 * block, 2 * block), sens.dtype)
        for i in range(many - LAG, many):
            push(i, zeros)
            if i < many - 2:
                multiply(padding, i)

        def work(c, carry):
            fetch(c).wait()
            before = jnp.where(c == 0, padding, c - 1)
            for i in range(many):
                stage(c, i)
                multiply(*((before, i - 2 + many) if i < 2 else (c, i - 2)))
                collect(*((before, i - LAG + many) if i < LAG else (c, i - LAG)))
            return carry

        get_pairs.wait()

        def count(c, busy):
            return busy + jnp.where(pairs[2, c * chunk] != 0, 1, 0)

        busy = lax.fori_loop(0, chunks, count, 0)

        def begin(c, carry):
            fetch(c).start()
            return carry

        lax.fori_loop(AHEAD, busy, begin, 0)
        get_order.wait()
        for p in range(books):
            owner = p // per_owner
            place = rank.index(owner // 2) * per_owner + p % per_owner
            position[order[p]] = place + half * ((owner & 1) ^ core)
        lax.fori_loop(0, busy, work, 0)
        last = jnp.where(busy == 0, padding, busy - 1)
        for i in range(many - 2, many):
            multiply(last, i)
        for i in range(many - LAG, many):
            collect(last, i)

        def drop(c, carry):
            fetch(c).wait()
            return carry

        lax.fori_loop(busy, AHEAD, drop, 0)

    spot = []
    held = []
    for _, size, unit, _ in packs:
        spot.append(len(held))
        held += [pltpu.ACC(unit)((rows, 2 * block), jnp.float32)] * (4 if size == 4 else 1)
    pl.run_scoped(on_units, *held)
    kept[...] = acc[:half]
    sent[...] = acc[half:books].astype(sent.dtype)


def reversed_bits(count):
    order = [0]
    while len(order) < count:
        order = [2 * i for i in order] + [2 * i + 1 for i in order]
    return order


def shards(returns, vol_hist, vol_now, sensitivity, block_pairs, book_order):
    groups = lax.axis_size("blk")
    own_rows, width = returns.shape
    slots, block, _ = sensitivity.shape
    own = width // groups
    rows = groups * own_rows
    books = book_order.shape[0]
    siblings = [(i, i ^ 1) for i in range(groups)]
    rescaled = (returns.astype(jnp.float32) * vol_now[None, :] / vol_hist).astype(jnp.bfloat16)
    bits = groups.bit_length() - 1
    flip = tuple(reversed(range(bits))) + (bits, bits + 1)
    outgoing = rescaled.reshape(own_rows, groups, own).swapaxes(0, 1).reshape((2,) * bits + (own_rows, own))
    outgoing = outgoing.transpose(flip).reshape(groups, own_rows, own)
    incoming = lax.all_to_all(outgoing, "blk", 0, 0, axis_index_groups=[reversed_bits(groups)])
    incoming = incoming.reshape((2,) * bits + (own_rows, own)).transpose(flip)
    shocks = incoming.reshape(rows, own // block, block).transpose(1, 0, 2)
    chunks = slots // UNROLL
    kept, sent = pl.pallas_call(
        functools.partial(accumulate, groups),
        in_specs=[VMEM, HBM, HBM, HBM],
        out_specs=[VMEM, VMEM],
        out_shape=[
            jax.ShapeDtypeStruct((books // 2, rows, block), jnp.float32),
            jax.ShapeDtypeStruct((books // 2, rows, block), jnp.bfloat16),
        ],
        scratch_shapes=[
            pltpu.VMEM((books + 1, rows, block), jnp.float32),
            pltpu.VMEM(sensitivity.shape, sensitivity.dtype),
            pltpu.SMEM((3, slots + UNROLL), jnp.int32),
            pltpu.SMEM((books,), jnp.int32),
            pltpu.SMEM((books + 1,), jnp.int32),
            pltpu.SemaphoreType.DMA((2,)),
            pltpu.SemaphoreType.DMA((chunks,)),
        ],
        compiler_params=pltpu.CompilerParams(vmem_limit_bytes=VMEM_LIMIT),
        cost_estimate=pl.CostEstimate(
            flops=2 * slots * rows * block * block,
            bytes_accessed=2 * slots * block * block,
            transcendentals=0,
        ),
    )(shocks, *(pltpu.with_memory_space_constraint(x, pltpu.HBM) for x in (block_pairs.T, book_order, sensitivity)))
    across = lax.ppermute(sent, "blk", siblings)
    per_owner = books // groups
    chips = groups // 2
    chip_sum = (kept + across.astype(jnp.float32)).astype(jnp.bfloat16).reshape(chips, per_owner, rows, block)
    same_core = [[2 * chip + c for chip in reversed_bits(chips)] for c in range(2)]
    arrived = lax.all_to_all(chip_sum, "blk", 0, 0, axis_index_groups=same_core)
    owned = jnp.sum(arrived.astype(jnp.float32), axis=0)
    profit_loss = owned.transpose(1, 0, 2).reshape(rows, per_owner * block)
    spans = lax.axis_size("scen")
    squares = jnp.sum(owned * owned, axis=1).reshape(-1)
    if spans == 2:
        squares = squares + lax.ppermute(squares, "scen", [(0, 1), (1, 0)])
    else:
        squares = lax.psum(squares, "scen")
    book_rms = jnp.sqrt(squares / (rows * spans) + 1e-06)
    return (profit_loss, book_rms)


def solution(mesh):
    def on_mesh(*args):
        with jax.sharding.use_abstract_mesh(mesh.abstract_mesh):
            return whole(*args)

    whole = jax.shard_map(
        shards,
        mesh=mesh,
        in_specs=(
            P(("scen", "blk"), None),
            P(("scen", "blk"), None),
            P(),
            P("blk", None, None),
            P("blk", None),
            P(),
        ),
        out_specs=(P("scen", "blk"), P("blk")),
        check_vma=False,
    )
    return on_mesh
```

```python
import functools

import jax
import jax.numpy as jnp
from jax import lax
from jax.experimental import pallas as pl
from jax.experimental.pallas import tpu as pltpu
from jax.sharding import PartitionSpec as P

UNROLL = 32
SIZES = (4, 2, 2, 4, 2, 2)
LAG = 6
AHEAD = 2
PIECES = 4
VMEM_LIMIT = 32 * 1024 * 1024
VMEM = pl.BlockSpec(memory_space=pltpu.VMEM)
HBM = pl.BlockSpec(memory_space=pltpu.HBM)


def accumulate(
    groups, shocks, pairs_hbm, order_hbm, sens_hbm, kept, sent, acc, sens, pairs, order, position, small, arrived
):
    slots = sens.shape[0]
    factors = shocks.shape[0]
    chunks = arrived.shape[0]
    chunk = slots // chunks
    half = kept.shape[0]
    books = 2 * half
    per_owner = books // groups
    index = lax.axis_index("blk")
    core = index & 1

    def fetch(c):
        span = pl.ds(c * chunk, chunk)
        return pltpu.make_async_copy(sens_hbm.at[span], sens.at[span], arrived.at[c])

    def begin(c, carry):
        part = chunk // PIECES
        for j in range(PIECES):
            span = pl.ds(c * chunk + j * part, part)
            pltpu.make_async_copy(sens_hbm.at[span], sens.at[span], arrived.at[c]).start()
        return carry

    get_order = pltpu.make_async_copy(order_hbm, order, small.at[0])
    get_pairs = pltpu.make_async_copy(pairs_hbm, pairs.at[:, pl.ds(0, slots)], small.at[1])
    get_order.start()
    get_pairs.start()
    for c in range(AHEAD):
        begin(c, 0)
    acc[...] = jnp.zeros_like(acc)
    position[books] = books
    first_factor = index * factors
    for u in range(chunk):
        pairs[0, slots + u] = first_factor
        pairs[1, slots + u] = 0
        pairs[2, slots + u] = 0
    padding = chunks
    rows, block = shocks.shape[1:]
    none = jnp.zeros((rows, block), shocks.dtype)
    blank = jnp.zeros((block, block), sens.dtype)

    packs = []
    for j, size in enumerate(SIZES):
        for unit in range(2):
            first = unit * (chunk // 2) + sum(SIZES[:j])
            packs.append((first, size, unit, j % 2))
    many = len(packs)

    def on_units(*units):
        def push(i, rhs):
            _, _, unit, staged = packs[i]
            pltpu.matmul_push_rhs(rhs, staged, unit)

        def stage(c, i):
            k = c * chunk + packs[i][0]
            if packs[i][1] == 4:
                tiles = [[sens[k], sens[k + 1]], [sens[k + 2], sens[k + 3]]]
            else:
                tiles = [[sens[k], blank], [blank, sens[k + 1]]]
            push(i, jnp.concatenate([jnp.concatenate(row, axis=1) for row in tiles], axis=0))

        def multiply(c, i):
            first, size, _, staged = packs[i]
            scenarios = [shocks[pairs[0, c * chunk + first + t] - first_factor] for t in range(size)]
            if size == 4:
                passes = [[x, none] if t < 2 else [none, x] for t, x in enumerate(scenarios)]
            else:
                passes = [scenarios]
            for t, halves in enumerate(passes):
                target = units[spot[i] + t]
                pltpu.matmul_acc_lhs(target, jnp.concatenate(halves, axis=1), load_staged_rhs=None if t else staged)

        def collect(c, i):
            first, size, _, _ = packs[i]
            popped = [pltpu.matmul_pop(units[spot[i] + t]) for t in range(4 if size == 4 else 1)]
            for t in range(size):
                k = c * chunk + first + t
                book = jnp.where(pairs[2, k] != 0, pairs[1, k], books)
                side = (t % 2) * block
                acc[position[book]] += popped[t if size == 4 else 0][:, side : side + block]

        zeros = jnp.zeros((2 * block, 2 * block), sens.dtype)
        for i in range(many - LAG, many):
            push(i, zeros)
            if i < many - 2:
                multiply(padding, i)

        def work(c, carry):
            fetch(c).wait()
            before = jnp.where(c == 0, padding, c - 1)
            for i in range(many):
                stage(c, i)
                multiply(*((before, i - 2 + many) if i < 2 else (c, i - 2)))
                collect(*((before, i - LAG + many) if i < LAG else (c, i - LAG)))
            return carry

        get_pairs.wait()

        def count(c, busy):
            return busy + jnp.where(pairs[2, c * chunk] != 0, 1, 0)

        busy = lax.fori_loop(0, chunks, count, 0)

        lax.fori_loop(AHEAD, busy, begin, 0)
        get_order.wait()
        for p in range(books):
            owner = p // per_owner
            place = (owner // 2) * per_owner + p % per_owner
            position[order[p]] = place + half * ((owner & 1) ^ core)
        lax.fori_loop(0, busy, work, 0)
        last = jnp.where(busy == 0, padding, busy - 1)
        for i in range(many - 2, many):
            multiply(last, i)
        for i in range(many - LAG, many):
            collect(last, i)

        def drop(c, carry):
            fetch(c).wait()
            return carry

        lax.fori_loop(busy, AHEAD, drop, 0)

    spot = []
    held = []
    for _, size, unit, _ in packs:
        spot.append(len(held))
        held += [pltpu.ACC(unit)((rows, 2 * block), jnp.float32)] * (4 if size == 4 else 1)
    pl.run_scoped(on_units, *held)
    kept[...] = acc[:half]
    sent[...] = acc[half:books].astype(sent.dtype)


def shards(returns, vol_hist, vol_now, sensitivity, block_pairs, book_order):
    groups = lax.axis_size("blk")
    own_rows, width = returns.shape
    slots, block, _ = sensitivity.shape
    own = width // groups
    rows = groups * own_rows
    books = book_order.shape[0]
    siblings = [(i, i ^ 1) for i in range(groups)]
    rescaled = (returns.astype(jnp.float32) * vol_now[None, :] / vol_hist).astype(jnp.bfloat16)
    outgoing = rescaled.reshape(own_rows, groups, own).swapaxes(0, 1)
    incoming = lax.all_to_all(outgoing, "blk", 0, 0)
    shocks = incoming.reshape(rows, own // block, block).transpose(1, 0, 2)
    chunks = slots // UNROLL
    kept, sent = pl.pallas_call(
        functools.partial(accumulate, groups),
        in_specs=[VMEM, HBM, HBM, HBM],
        out_specs=[VMEM, VMEM],
        out_shape=[
            jax.ShapeDtypeStruct((books // 2, rows, block), jnp.float32),
            jax.ShapeDtypeStruct((books // 2, rows, block), jnp.bfloat16),
        ],
        scratch_shapes=[
            pltpu.VMEM((books + 1, rows, block), jnp.float32),
            pltpu.VMEM(sensitivity.shape, sensitivity.dtype),
            pltpu.SMEM((3, slots + UNROLL), jnp.int32),
            pltpu.SMEM((books,), jnp.int32),
            pltpu.SMEM((books + 1,), jnp.int32),
            pltpu.SemaphoreType.DMA((2,)),
            pltpu.SemaphoreType.DMA((chunks,)),
        ],
        compiler_params=pltpu.CompilerParams(vmem_limit_bytes=VMEM_LIMIT),
        cost_estimate=pl.CostEstimate(
            flops=2 * slots * rows * block * block,
            bytes_accessed=2 * slots * block * block,
            transcendentals=0,
        ),
    )(shocks, *(pltpu.with_memory_space_constraint(x, pltpu.HBM) for x in (block_pairs.T, book_order, sensitivity)))
    across = lax.ppermute(sent, "blk", siblings)
    per_owner = books // groups
    chips = groups // 2
    chip_sum = (kept + across.astype(jnp.float32)).astype(jnp.bfloat16).reshape(chips, per_owner, rows, block)
    same_core = [list(range(c, groups, 2)) for c in range(2)]
    arrived = lax.all_to_all(chip_sum, "blk", 0, 0, axis_index_groups=same_core)
    owned = jnp.sum(arrived.astype(jnp.float32), axis=0)
    profit_loss = owned.transpose(1, 0, 2).reshape(rows, per_owner * block)
    spans = lax.axis_size("scen")
    squares = jnp.sum(owned * owned, axis=1).reshape(-1)
    if spans == 2:
        squares = squares + lax.ppermute(squares, "scen", [(0, 1), (1, 0)])
    else:
        squares = lax.psum(squares, "scen")
    book_rms = jnp.sqrt(squares / (rows * spans) + 1e-06)
    return (profit_loss, book_rms)


def solution(mesh):
    def on_mesh(*args):
        with jax.sharding.use_abstract_mesh(mesh.abstract_mesh):
            return whole(*args)

    whole = jax.shard_map(
        shards,
        mesh=mesh,
        in_specs=(
            P(("scen", "blk"), None),
            P(("scen", "blk"), None),
            P(),
            P("blk", None, None),
            P("blk", None),
            P(),
        ),
        out_specs=(P("scen", "blk"), P("blk")),
        check_vma=False,
    )
    return on_mesh
```

```python
import functools

import jax
import jax.numpy as jnp
from jax import lax
from jax.experimental import pallas as pl
from jax.experimental.pallas import tpu as pltpu
from jax.sharding import PartitionSpec as P

UNROLL = 32
SIZES = (4, 2, 2, 4, 2, 2)
LAG = 4
AHEAD = 2
PIECES = 4
VMEM_LIMIT = 32 * 1024 * 1024
VMEM = pl.BlockSpec(memory_space=pltpu.VMEM)
HBM = pl.BlockSpec(memory_space=pltpu.HBM)


def accumulate(
    groups, shocks, pairs_hbm, order_hbm, sens_hbm, kept, sent, acc, sens, pairs, order, position, small, arrived
):
    slots = sens.shape[0]
    factors = shocks.shape[0]
    chunks = arrived.shape[0]
    chunk = slots // chunks
    half = kept.shape[0]
    books = 2 * half
    per_owner = books // groups
    index = lax.axis_index("blk")
    core = index & 1

    def fetch(c):
        span = pl.ds(c * chunk, chunk)
        return pltpu.make_async_copy(sens_hbm.at[span], sens.at[span], arrived.at[c])

    def begin(c, carry):
        part = chunk // PIECES
        for j in range(PIECES):
            span = pl.ds(c * chunk + j * part, part)
            pltpu.make_async_copy(sens_hbm.at[span], sens.at[span], arrived.at[c]).start()
        return carry

    get_order = pltpu.make_async_copy(order_hbm, order, small.at[0])
    get_pairs = pltpu.make_async_copy(pairs_hbm, pairs.at[:, pl.ds(0, slots)], small.at[1])
    begin(0, 0)
    get_pairs.start()
    get_order.start()
    for c in range(1, AHEAD):
        begin(c, 0)
    acc[...] = jnp.zeros_like(acc)
    position[books] = books
    first_factor = index * factors
    for u in range(chunk):
        pairs[0, slots + u] = first_factor
        pairs[1, slots + u] = 0
        pairs[2, slots + u] = 0
    padding = chunks
    rows, block = shocks.shape[1:]
    none = jnp.zeros((rows, block), shocks.dtype)
    blank = jnp.zeros((block, block), sens.dtype)

    packs = []
    for j, size in enumerate(SIZES):
        for unit in range(2):
            first = unit * (chunk // 2) + sum(SIZES[:j])
            packs.append((first, size, unit, j % 2))
    many = len(packs)

    def on_units(*units):
        def push(i, rhs):
            _, _, unit, staged = packs[i]
            pltpu.matmul_push_rhs(rhs, staged, unit)

        def stage(c, i):
            k = c * chunk + packs[i][0]
            if packs[i][1] == 4:
                tiles = [[sens[k], sens[k + 1]], [sens[k + 2], sens[k + 3]]]
            else:
                tiles = [[sens[k], blank], [blank, sens[k + 1]]]
            push(i, jnp.concatenate([jnp.concatenate(row, axis=1) for row in tiles], axis=0))

        def multiply(c, i):
            first, size, _, staged = packs[i]
            scenarios = [shocks[pairs[0, c * chunk + first + t] - first_factor] for t in range(size)]
            if size == 4:
                passes = [[x, none] if t < 2 else [none, x] for t, x in enumerate(scenarios)]
            else:
                passes = [scenarios]
            for t, halves in enumerate(passes):
                target = units[spot[i] + t]
                pltpu.matmul_acc_lhs(target, jnp.concatenate(halves, axis=1), load_staged_rhs=None if t else staged)

        def collect(c, i):
            first, size, _, _ = packs[i]
            popped = [pltpu.matmul_pop(units[spot[i] + t]) for t in range(4 if size == 4 else 1)]
            for t in range(size):
                k = c * chunk + first + t
                book = jnp.where(pairs[2, k] != 0, pairs[1, k], books)
                side = (t % 2) * block
                acc[position[book]] += popped[t if size == 4 else 0][:, side : side + block]

        zeros = jnp.zeros((2 * block, 2 * block), sens.dtype)
        for i in range(many - LAG, many):
            push(i, zeros)
            if i < many - 2:
                multiply(padding, i)

        def work(c, carry):
            fetch(c).wait()
            before = jnp.where(c == 0, padding, c - 1)
            for i in range(many):
                stage(c, i)
                multiply(*((before, i - 2 + many) if i < 2 else (c, i - 2)))
                collect(*((before, i - LAG + many) if i < LAG else (c, i - LAG)))
            return carry

        get_pairs.wait()

        def count(c, busy):
            return busy + jnp.where(pairs[2, c * chunk] != 0, 1, 0)

        busy = lax.fori_loop(0, chunks, count, 0)

        lax.fori_loop(AHEAD, busy, begin, 0)
        get_order.wait()
        for p in range(books):
            owner = p // per_owner
            place = (owner // 2) * per_owner + p % per_owner
            position[order[p]] = place + half * ((owner & 1) ^ core)
        lax.fori_loop(0, busy, work, 0)
        last = jnp.where(busy == 0, padding, busy - 1)
        for i in range(many - 2, many):
            multiply(last, i)
        for i in range(many - LAG, many):
            collect(last, i)

        def drop(c, carry):
            fetch(c).wait()
            return carry

        lax.fori_loop(busy, AHEAD, drop, 0)

    spot = []
    held = []
    for _, size, unit, _ in packs:
        spot.append(len(held))
        held += [pltpu.ACC(unit)((rows, 2 * block), jnp.float32)] * (4 if size == 4 else 1)
    pl.run_scoped(on_units, *held)
    kept[...] = acc[:half]
    sent[...] = acc[half:books].astype(sent.dtype)


def shards(returns, vol_hist, vol_now, sensitivity, block_pairs, book_order):
    groups = lax.axis_size("blk")
    own_rows, width = returns.shape
    slots, block, _ = sensitivity.shape
    own = width // groups
    rows = groups * own_rows
    books = book_order.shape[0]
    siblings = [(i, i ^ 1) for i in range(groups)]
    rescaled = (returns.astype(jnp.float32) * vol_now[None, :] / vol_hist).astype(jnp.bfloat16)
    outgoing = rescaled.reshape(own_rows, groups, own).swapaxes(0, 1)
    incoming = lax.all_to_all(outgoing, "blk", 0, 0)
    shocks = incoming.reshape(rows, own // block, block).transpose(1, 0, 2)
    chunks = slots // UNROLL
    kept, sent = pl.pallas_call(
        functools.partial(accumulate, groups),
        in_specs=[VMEM, HBM, HBM, HBM],
        out_specs=[VMEM, VMEM],
        out_shape=[
            jax.ShapeDtypeStruct((books // 2, rows, block), jnp.float32),
            jax.ShapeDtypeStruct((books // 2, rows, block), jnp.bfloat16),
        ],
        scratch_shapes=[
            pltpu.VMEM((books + 1, rows, block), jnp.float32),
            pltpu.VMEM(sensitivity.shape, sensitivity.dtype),
            pltpu.SMEM((3, slots + UNROLL), jnp.int32),
            pltpu.SMEM((books,), jnp.int32),
            pltpu.SMEM((books + 1,), jnp.int32),
            pltpu.SemaphoreType.DMA((2,)),
            pltpu.SemaphoreType.DMA((chunks,)),
        ],
        compiler_params=pltpu.CompilerParams(vmem_limit_bytes=VMEM_LIMIT),
        cost_estimate=pl.CostEstimate(
            flops=2 * slots * rows * block * block,
            bytes_accessed=2 * slots * block * block,
            transcendentals=0,
        ),
    )(shocks, *(pltpu.with_memory_space_constraint(x, pltpu.HBM) for x in (block_pairs.T, book_order, sensitivity)))
    across = lax.ppermute(sent, "blk", siblings)
    per_owner = books // groups
    chips = groups // 2
    chip_sum = (kept + across.astype(jnp.float32)).astype(jnp.bfloat16).reshape(chips, per_owner, rows, block)
    same_core = [list(range(c, groups, 2)) for c in range(2)]
    arrived = lax.all_to_all(chip_sum, "blk", 0, 0, axis_index_groups=same_core)
    owned = jnp.sum(arrived.astype(jnp.float32), axis=0)
    profit_loss = owned.transpose(1, 0, 2).reshape(rows, per_owner * block)
    spans = lax.axis_size("scen")
    squares = jnp.sum(owned * owned, axis=1).reshape(-1)
    if spans == 2:
        squares = squares + lax.ppermute(squares, "scen", [(0, 1), (1, 0)])
    else:
        squares = lax.psum(squares, "scen")
    book_rms = jnp.sqrt(squares / (rows * spans) + 1e-06)
    return (profit_loss, book_rms)


def solution(mesh):
    def on_mesh(*args):
        with jax.sharding.use_abstract_mesh(mesh.abstract_mesh):
            return whole(*args)

    whole = jax.shard_map(
        shards,
        mesh=mesh,
        in_specs=(
            P(("scen", "blk"), None),
            P(("scen", "blk"), None),
            P(),
            P("blk", None, None),
            P("blk", None),
            P(),
        ),
        out_specs=(P("scen", "blk"), P("blk")),
        check_vma=False,
    )
    return on_mesh
```

```python
import functools

import jax
import jax.numpy as jnp
from jax import lax
from jax.experimental import pallas as pl
from jax.experimental.pallas import tpu as pltpu
from jax.sharding import PartitionSpec as P

UNROLL = 32
SIZES = (4, 2, 2, 4, 2, 2)
LAG = 8
AHEAD = 2
PIECES = 4
VMEM_LIMIT = 32 * 1024 * 1024
VMEM = pl.BlockSpec(memory_space=pltpu.VMEM)
HBM = pl.BlockSpec(memory_space=pltpu.HBM)


def accumulate(
    groups, shocks, pairs_hbm, order_hbm, sens_hbm, kept, sent, acc, sens, pairs, order, position, small, arrived
):
    slots = sens.shape[0]
    factors = shocks.shape[0]
    chunks = arrived.shape[0]
    chunk = slots // chunks
    half = kept.shape[0]
    books = 2 * half
    per_owner = books // groups
    index = lax.axis_index("blk")
    core = index & 1

    def fetch(c):
        span = pl.ds(c * chunk, chunk)
        return pltpu.make_async_copy(sens_hbm.at[span], sens.at[span], arrived.at[c])

    def begin(c, carry):
        part = chunk // PIECES
        for j in range(PIECES):
            span = pl.ds(c * chunk + j * part, part)
            pltpu.make_async_copy(sens_hbm.at[span], sens.at[span], arrived.at[c]).start()
        return carry

    get_order = pltpu.make_async_copy(order_hbm, order, small.at[0])
    get_pairs = pltpu.make_async_copy(pairs_hbm, pairs.at[:, pl.ds(0, slots)], small.at[1])
    get_order.start()
    get_pairs.start()
    for c in range(AHEAD):
        begin(c, 0)
    acc[...] = jnp.zeros_like(acc)
    position[books] = books
    first_factor = index * factors
    for u in range(chunk):
        pairs[0, slots + u] = first_factor
        pairs[1, slots + u] = 0
        pairs[2, slots + u] = 0
    padding = chunks
    rows, block = shocks.shape[1:]
    none = jnp.zeros((rows, block), shocks.dtype)
    blank = jnp.zeros((block, block), sens.dtype)

    packs = []
    for j, size in enumerate(SIZES):
        for unit in range(2):
            first = unit * (chunk // 2) + sum(SIZES[:j])
            packs.append((first, size, unit, j % 2))
    many = len(packs)

    def on_units(*units):
        def push(i, rhs):
            _, _, unit, staged = packs[i]
            pltpu.matmul_push_rhs(rhs, staged, unit)

        def stage(c, i):
            k = c * chunk + packs[i][0]
            if packs[i][1] == 4:
                tiles = [[sens[k], sens[k + 1]], [sens[k + 2], sens[k + 3]]]
            else:
                tiles = [[sens[k], blank], [blank, sens[k + 1]]]
            push(i, jnp.concatenate([jnp.concatenate(row, axis=1) for row in tiles], axis=0))

        def multiply(c, i):
            first, size, _, staged = packs[i]
            scenarios = [shocks[pairs[0, c * chunk + first + t] - first_factor] for t in range(size)]
            if size == 4:
                passes = [[x, none] if t < 2 else [none, x] for t, x in enumerate(scenarios)]
            else:
                passes = [scenarios]
            for t, halves in enumerate(passes):
                target = units[spot[i] + t]
                pltpu.matmul_acc_lhs(target, jnp.concatenate(halves, axis=1), load_staged_rhs=None if t else staged)

        def collect(c, i):
            first, size, _, _ = packs[i]
            popped = [pltpu.matmul_pop(units[spot[i] + t]) for t in range(4 if size == 4 else 1)]
            for t in range(size):
                k = c * chunk + first + t
                book = jnp.where(pairs[2, k] != 0, pairs[1, k], books)
                side = (t % 2) * block
                acc[position[book]] += popped[t if size == 4 else 0][:, side : side + block]

        zeros = jnp.zeros((2 * block, 2 * block), sens.dtype)
        for i in range(many - LAG, many):
            push(i, zeros)
            if i < many - 2:
                multiply(padding, i)

        def work(c, carry):
            fetch(c).wait()
            before = jnp.where(c == 0, padding, c - 1)
            for i in range(many):
                stage(c, i)
                multiply(*((before, i - 2 + many) if i < 2 else (c, i - 2)))
                collect(*((before, i - LAG + many) if i < LAG else (c, i - LAG)))
            return carry

        get_pairs.wait()

        def count(c, busy):
            return busy + jnp.where(pairs[2, c * chunk] != 0, 1, 0)

        busy = lax.fori_loop(0, chunks, count, 0)

        lax.fori_loop(AHEAD, busy, begin, 0)
        get_order.wait()
        for p in range(books):
            owner = p // per_owner
            place = (owner // 2) * per_owner + p % per_owner
            position[order[p]] = place + half * ((owner & 1) ^ core)
        lax.fori_loop(0, busy, work, 0)
        last = jnp.where(busy == 0, padding, busy - 1)
        for i in range(many - 2, many):
            multiply(last, i)
        for i in range(many - LAG, many):
            collect(last, i)

        def drop(c, carry):
            fetch(c).wait()
            return carry

        lax.fori_loop(busy, AHEAD, drop, 0)

    spot = []
    held = []
    for _, size, unit, _ in packs:
        spot.append(len(held))
        held += [pltpu.ACC(unit)((rows, 2 * block), jnp.float32)] * (4 if size == 4 else 1)
    pl.run_scoped(on_units, *held)
    kept[...] = acc[:half]
    sent[...] = acc[half:books].astype(sent.dtype)


def shards(returns, vol_hist, vol_now, sensitivity, block_pairs, book_order):
    groups = lax.axis_size("blk")
    own_rows, width = returns.shape
    slots, block, _ = sensitivity.shape
    own = width // groups
    rows = groups * own_rows
    books = book_order.shape[0]
    siblings = [(i, i ^ 1) for i in range(groups)]
    rescaled = (returns.astype(jnp.float32) * vol_now[None, :] / vol_hist).astype(jnp.bfloat16)
    outgoing = rescaled.reshape(own_rows, groups, own).swapaxes(0, 1)
    incoming = lax.all_to_all(outgoing, "blk", 0, 0)
    shocks = incoming.reshape(rows, own // block, block).transpose(1, 0, 2)
    chunks = slots // UNROLL
    kept, sent = pl.pallas_call(
        functools.partial(accumulate, groups),
        in_specs=[VMEM, HBM, HBM, HBM],
        out_specs=[VMEM, VMEM],
        out_shape=[
            jax.ShapeDtypeStruct((books // 2, rows, block), jnp.float32),
            jax.ShapeDtypeStruct((books // 2, rows, block), jnp.bfloat16),
        ],
        scratch_shapes=[
            pltpu.VMEM((books + 1, rows, block), jnp.float32),
            pltpu.VMEM(sensitivity.shape, sensitivity.dtype),
            pltpu.SMEM((3, slots + UNROLL), jnp.int32),
            pltpu.SMEM((books,), jnp.int32),
            pltpu.SMEM((books + 1,), jnp.int32),
            pltpu.SemaphoreType.DMA((2,)),
            pltpu.SemaphoreType.DMA((chunks,)),
        ],
        compiler_params=pltpu.CompilerParams(vmem_limit_bytes=VMEM_LIMIT),
        cost_estimate=pl.CostEstimate(
            flops=2 * slots * rows * block * block,
            bytes_accessed=2 * slots * block * block,
            transcendentals=0,
        ),
    )(shocks, *(pltpu.with_memory_space_constraint(x, pltpu.HBM) for x in (block_pairs.T, book_order, sensitivity)))
    across = lax.ppermute(sent, "blk", siblings)
    per_owner = books // groups
    chips = groups // 2
    chip_sum = (kept + across.astype(jnp.float32)).astype(jnp.bfloat16).reshape(chips, per_owner, rows, block)
    same_core = [list(range(c, groups, 2)) for c in range(2)]
    arrived = lax.all_to_all(chip_sum, "blk", 0, 0, axis_index_groups=same_core)
    owned = jnp.sum(arrived.astype(jnp.float32), axis=0)
    profit_loss = owned.transpose(1, 0, 2).reshape(rows, per_owner * block)
    spans = lax.axis_size("scen")
    squares = jnp.sum(owned * owned, axis=1).reshape(-1)
    if spans == 2:
        squares = squares + lax.ppermute(squares, "scen", [(0, 1), (1, 0)])
    else:
        squares = lax.psum(squares, "scen")
    book_rms = jnp.sqrt(squares / (rows * spans) + 1e-06)
    return (profit_loss, book_rms)


def solution(mesh):
    def on_mesh(*args):
        with jax.sharding.use_abstract_mesh(mesh.abstract_mesh):
            return whole(*args)

    whole = jax.shard_map(
        shards,
        mesh=mesh,
        in_specs=(
            P(("scen", "blk"), None),
            P(("scen", "blk"), None),
            P(),
            P("blk", None, None),
            P("blk", None),
            P(),
        ),
        out_specs=(P("scen", "blk"), P("blk")),
        check_vma=False,
    )
    return on_mesh
```

```python
import functools

import jax
import jax.numpy as jnp
from jax import lax
from jax.experimental import pallas as pl
from jax.experimental.pallas import tpu as pltpu
from jax.sharding import PartitionSpec as P

UNROLL = 32
SIZES = (4, 2, 2, 4, 2, 2)
LAG = 6
AHEAD = 2
PIECES = 2
VMEM_LIMIT = 32 * 1024 * 1024
VMEM = pl.BlockSpec(memory_space=pltpu.VMEM)
HBM = pl.BlockSpec(memory_space=pltpu.HBM)


def accumulate(
    groups, shocks, pairs_hbm, order_hbm, sens_hbm, kept, sent, acc, sens, pairs, order, position, small, arrived
):
    slots = sens.shape[0]
    factors = shocks.shape[0]
    chunks = arrived.shape[0]
    chunk = slots // chunks
    half = kept.shape[0]
    books = 2 * half
    per_owner = books // groups
    index = lax.axis_index("blk")
    core = index & 1

    def fetch(c):
        span = pl.ds(c * chunk, chunk)
        return pltpu.make_async_copy(sens_hbm.at[span], sens.at[span], arrived.at[c])

    def begin(c, carry):
        part = chunk // PIECES
        for j in range(PIECES):
            span = pl.ds(c * chunk + j * part, part)
            pltpu.make_async_copy(sens_hbm.at[span], sens.at[span], arrived.at[c]).start()
        return carry

    get_order = pltpu.make_async_copy(order_hbm, order, small.at[0])
    get_pairs = pltpu.make_async_copy(pairs_hbm, pairs.at[:, pl.ds(0, slots)], small.at[1])
    get_order.start()
    get_pairs.start()
    for c in range(AHEAD):
        begin(c, 0)
    acc[...] = jnp.zeros_like(acc)
    position[books] = books
    first_factor = index * factors
    for u in range(chunk):
        pairs[0, slots + u] = first_factor
        pairs[1, slots + u] = 0
        pairs[2, slots + u] = 0
    padding = chunks
    rows, block = shocks.shape[1:]
    none = jnp.zeros((rows, block), shocks.dtype)
    blank = jnp.zeros((block, block), sens.dtype)

    packs = []
    for j, size in enumerate(SIZES):
        for unit in range(2):
            first = unit * (chunk // 2) + sum(SIZES[:j])
            packs.append((first, size, unit, j % 2))
    many = len(packs)

    def on_units(*units):
        def push(i, rhs):
            _, _, unit, staged = packs[i]
            pltpu.matmul_push_rhs(rhs, staged, unit)

        def stage(c, i):
            k = c * chunk + packs[i][0]
            if packs[i][1] == 4:
                tiles = [[sens[k], sens[k + 1]], [sens[k + 2], sens[k + 3]]]
            else:
                tiles = [[sens[k], blank], [blank, sens[k + 1]]]
            push(i, jnp.concatenate([jnp.concatenate(row, axis=1) for row in tiles], axis=0))

        def multiply(c, i):
            first, size, _, staged = packs[i]
            scenarios = [shocks[pairs[0, c * chunk + first + t] - first_factor] for t in range(size)]
            if size == 4:
                passes = [[x, none] if t < 2 else [none, x] for t, x in enumerate(scenarios)]
            else:
                passes = [scenarios]
            for t, halves in enumerate(passes):
                target = units[spot[i] + t]
                pltpu.matmul_acc_lhs(target, jnp.concatenate(halves, axis=1), load_staged_rhs=None if t else staged)

        def collect(c, i):
            first, size, _, _ = packs[i]
            popped = [pltpu.matmul_pop(units[spot[i] + t]) for t in range(4 if size == 4 else 1)]
            for t in range(size):
                k = c * chunk + first + t
                book = jnp.where(pairs[2, k] != 0, pairs[1, k], books)
                side = (t % 2) * block
                acc[position[book]] += popped[t if size == 4 else 0][:, side : side + block]

        zeros = jnp.zeros((2 * block, 2 * block), sens.dtype)
        for i in range(many - LAG, many):
            push(i, zeros)
            if i < many - 2:
                multiply(padding, i)

        def work(c, carry):
            fetch(c).wait()
            before = jnp.where(c == 0, padding, c - 1)
            for i in range(many):
                stage(c, i)
                multiply(*((before, i - 2 + many) if i < 2 else (c, i - 2)))
                collect(*((before, i - LAG + many) if i < LAG else (c, i - LAG)))
            return carry

        get_pairs.wait()

        def count(c, busy):
            return busy + jnp.where(pairs[2, c * chunk] != 0, 1, 0)

        busy = lax.fori_loop(0, chunks, count, 0)

        lax.fori_loop(AHEAD, busy, begin, 0)
        get_order.wait()
        for p in range(books):
            owner = p // per_owner
            place = (owner // 2) * per_owner + p % per_owner
            position[order[p]] = place + half * ((owner & 1) ^ core)
        lax.fori_loop(0, busy, work, 0)
        last = jnp.where(busy == 0, padding, busy - 1)
        for i in range(many - 2, many):
            multiply(last, i)
        for i in range(many - LAG, many):
            collect(last, i)

        def drop(c, carry):
            fetch(c).wait()
            return carry

        lax.fori_loop(busy, AHEAD, drop, 0)

    spot = []
    held = []
    for _, size, unit, _ in packs:
        spot.append(len(held))
        held += [pltpu.ACC(unit)((rows, 2 * block), jnp.float32)] * (4 if size == 4 else 1)
    pl.run_scoped(on_units, *held)
    kept[...] = acc[:half]
    sent[...] = acc[half:books].astype(sent.dtype)


def shards(returns, vol_hist, vol_now, sensitivity, block_pairs, book_order):
    groups = lax.axis_size("blk")
    own_rows, width = returns.shape
    slots, block, _ = sensitivity.shape
    own = width // groups
    rows = groups * own_rows
    books = book_order.shape[0]
    siblings = [(i, i ^ 1) for i in range(groups)]
    rescaled = (returns.astype(jnp.float32) * vol_now[None, :] / vol_hist).astype(jnp.bfloat16)
    outgoing = rescaled.reshape(own_rows, groups, own).swapaxes(0, 1)
    incoming = lax.all_to_all(outgoing, "blk", 0, 0)
    shocks = incoming.reshape(rows, own // block, block).transpose(1, 0, 2)
    chunks = slots // UNROLL
    kept, sent = pl.pallas_call(
        functools.partial(accumulate, groups),
        in_specs=[VMEM, HBM, HBM, HBM],
        out_specs=[VMEM, VMEM],
        out_shape=[
            jax.ShapeDtypeStruct((books // 2, rows, block), jnp.float32),
            jax.ShapeDtypeStruct((books // 2, rows, block), jnp.bfloat16),
        ],
        scratch_shapes=[
            pltpu.VMEM((books + 1, rows, block), jnp.float32),
            pltpu.VMEM(sensitivity.shape, sensitivity.dtype),
            pltpu.SMEM((3, slots + UNROLL), jnp.int32),
            pltpu.SMEM((books,), jnp.int32),
            pltpu.SMEM((books + 1,), jnp.int32),
            pltpu.SemaphoreType.DMA((2,)),
            pltpu.SemaphoreType.DMA((chunks,)),
        ],
        compiler_params=pltpu.CompilerParams(vmem_limit_bytes=VMEM_LIMIT),
        cost_estimate=pl.CostEstimate(
            flops=2 * slots * rows * block * block,
            bytes_accessed=2 * slots * block * block,
            transcendentals=0,
        ),
    )(shocks, *(pltpu.with_memory_space_constraint(x, pltpu.HBM) for x in (block_pairs.T, book_order, sensitivity)))
    across = lax.ppermute(sent, "blk", siblings)
    per_owner = books // groups
    chips = groups // 2
    chip_sum = (kept + across.astype(jnp.float32)).astype(jnp.bfloat16).reshape(chips, per_owner, rows, block)
    same_core = [list(range(c, groups, 2)) for c in range(2)]
    arrived = lax.all_to_all(chip_sum, "blk", 0, 0, axis_index_groups=same_core)
    owned = jnp.sum(arrived.astype(jnp.float32), axis=0)
    profit_loss = owned.transpose(1, 0, 2).reshape(rows, per_owner * block)
    spans = lax.axis_size("scen")
    squares = jnp.sum(owned * owned, axis=1).reshape(-1)
    if spans == 2:
        squares = squares + lax.ppermute(squares, "scen", [(0, 1), (1, 0)])
    else:
        squares = lax.psum(squares, "scen")
    book_rms = jnp.sqrt(squares / (rows * spans) + 1e-06)
    return (profit_loss, book_rms)


def solution(mesh):
    def on_mesh(*args):
        with jax.sharding.use_abstract_mesh(mesh.abstract_mesh):
            return whole(*args)

    whole = jax.shard_map(
        shards,
        mesh=mesh,
        in_specs=(
            P(("scen", "blk"), None),
            P(("scen", "blk"), None),
            P(),
            P("blk", None, None),
            P("blk", None),
            P(),
        ),
        out_specs=(P("scen", "blk"), P("blk")),
        check_vma=False,
    )
    return on_mesh
```
